32 devices in a mesh: samp: 8 (over z, x), blk: 4 (over y, core).
Axes of the slice: x: 2, y: 2, z: 4, core: 2. Of those that a mesh axis runs over, the one named last changes fastest.
Arguments:
- dosages: bfloat16 [5120, 2048], P('samp', 'blk'), may hold values from 0 to 2
- traits: bfloat16 [16, 5120], P(None, 'samp'), may hold values from -6 to 6
- folds: int32 [5120], P('samp'), may hold values from 0 to 4
Outputs:
- level0: float32 [4, 5, 16, 5120], P(None, None, 'blk', 'samp')
- blend: float32 [16, 5120], P('blk', 'samp')
The draws below stay inside these ranges and needn't reach their ends.
All inputs are finite; a program needn't handle non-finite values.
Results may differ from the reference program's by a relative error of at most 0.0097.
Values may be sent and summed in bfloat16 or wider, within the bound.
A program may use at most 64 MiB of HBM per device.

```python
import math
import jax
import jax.numpy as jnp
from jax import lax

VB = 512
TRAITS = 16
FOLDS = 5
SHRINK = 5
BLOCKS = 4
VARIANTS = 2048
SAMPLES = 5120


def draw_dosages(key, part):
    key_freq, key_rows, key_own, key_shared, key_weight = jax.random.split(key, 5)
    frequency = jnp.exp(jax.random.uniform(key_freq, (1, VARIANTS), jnp.float32, math.log(0.05), math.log(0.5)))
    position = jnp.arange(SAMPLES, dtype=jnp.float32)[:, None] / SAMPLES
    run_count = (VARIANTS + 31) // 32
    run_weight = jax.random.uniform(key_weight, (1, run_count), jnp.float32, 0.5, 0.85)
    run_weight = jnp.repeat(run_weight, 32, axis=1)[:, :VARIANTS]
    row_scale = jnp.exp(math.log(3.0) * position) * jnp.exp(jax.random.uniform(key_rows, (SAMPLES, 1), jnp.float32, 0.0, math.log(3.5)))
    own_noise = jax.random.exponential(key_own, (SAMPLES, VARIANTS), jnp.float32)
    shared_noise = jax.random.exponential(key_shared, (SAMPLES, run_count), jnp.float32)
    shared_noise = jnp.repeat(shared_noise, 32, axis=1)[:, :VARIANTS]
    mixture = (1.0 - run_weight) * own_noise + run_weight * shared_noise
    dosage_value = 2.0 * (1.0 - jnp.exp(-frequency * row_scale * mixture))
    return dosage_value.astype(jnp.bfloat16)


def place_ends(entries, stream_key, smallest, high):
    spot = [jax.random.randint(jax.random.fold_in(stream_key, axis), (), 0, length) for axis, length in enumerate(entries.shape)]
    main_axis = entries.shape.index(max(entries.shape))
    neighbour = spot[:main_axis] + [(spot[main_axis] + 1) % entries.shape[main_axis]] + spot[main_axis + 1:]
    return entries.at[tuple(spot)].set(smallest).at[tuple(neighbour)].set(high)


def levels(stream_key, shape, cuts, low, top_value):
    def one(axis_at, shards_of):
        heights = jax.random.uniform(jax.random.fold_in(jax.random.fold_in(stream_key, 6), axis_at), (shards_of,), jnp.float32, low / len(cuts), top_value / len(cuts))
        return jnp.repeat(jnp.exp(heights), shape[axis_at] // shards_of).reshape((-1,) + (1,) * (len(shape) - axis_at - 1))

    level = one(*cuts[0])
    for cut in cuts[1:]:
        level = level * one(*cut)
    return level


def gaussian(own_key, shape, scale, bound, cuts=(), kind=jnp.bfloat16):
    values = scale * jax.random.normal(own_key, shape, jnp.float32)
    if cuts:
        values = values * levels(own_key, shape, cuts, -0.22, 0.18)
    return jnp.clip(values, -bound, bound).astype(kind)


def setup_inputs(seed: int = 0) -> dict:
    key_list = jax.random.split(jax.random.key(seed), 4)
    return {
        "dosages": draw_dosages(jax.random.fold_in(key_list[3], 71), 0),
        "traits": gaussian(key_list[1], (TRAITS, SAMPLES), 1.0, 6.0, ((1, 8),)),
        "folds": place_ends(jax.random.randint(key_list[2], (SAMPLES,), 0, FOLDS), jax.random.fold_in(key_list[2], 1), 0, FOLDS - 1).astype(jnp.int32),
    }


RATIOS = (99.0, 3.0, 1.0, 1.0 / 3.0, 1.0 / 99.0)
EPS = 1e-05
HIGH = lax.Precision.HIGHEST

def solve_batch(systems, right_sides):
    factors = jnp.linalg.cholesky(systems)

    def solve_single(factor, right_side):
        return jax.scipy.linalg.cho_solve((factor, True), right_side)
    return jax.vmap(solve_single)(factors, right_sides)

def reference(dosages, traits, folds):
    fold_ids = jnp.arange(FOLDS, dtype=jnp.int32)
    masks = (folds[None, :] == fold_ids[:, None]).astype(jnp.float32)
    mask_half = masks.astype(jnp.bfloat16)
    traits_wide = traits.astype(jnp.float32)
    trait_sums = jnp.einsum('ks,ts->kt', masks, traits_wide, precision=HIGH)
    counts = lax.optimization_barrier(jnp.sum(masks, axis=1))
    ratios = jnp.array(RATIOS, dtype=jnp.float32)
    identity = jnp.eye(VB, dtype=jnp.float32)
    total = jnp.sum(counts)
    block_preds = []
    for block in range(BLOCKS):
        columns = dosages[:, block * VB:(block + 1) * VB]
        grams = []
        crosses = []
        for fold in range(FOLDS):
            weighted = columns * mask_half[fold][:, None]
            grams.append(jnp.dot(columns.T.astype(jnp.float32), weighted.astype(jnp.float32), preferred_element_type=jnp.float32))
            crosses.append(jnp.dot((traits * mask_half[fold][None, :]).astype(jnp.float32), columns.astype(jnp.float32), preferred_element_type=jnp.float32))
        gram = jnp.stack(grams)
        cross = jnp.stack(crosses)
        sums = jnp.dot(mask_half.astype(jnp.float32), columns.astype(jnp.float32), preferred_element_type=jnp.float32)
        mean = lax.optimization_barrier(jnp.sum(sums, axis=0)) / SAMPLES
        gram_total = lax.optimization_barrier(jnp.sum(gram, axis=0))
        variance = jnp.diagonal(gram_total) / SAMPLES - mean * mean
        scale = lax.rsqrt(variance + EPS)
        sums_total = lax.optimization_barrier(jnp.sum(sums, axis=0))
        cross_total = lax.optimization_barrier(jnp.sum(cross, axis=0))
        trait_total = lax.optimization_barrier(jnp.sum(trait_sums, axis=0))
        accum = jnp.zeros((SHRINK, TRAITS, SAMPLES), jnp.float32)
        for fold in range(FOLDS):
            train_gram = gram_total - gram[fold]
            train_sums = sums_total - sums[fold]
            train_count = total - counts[fold]
            train_cross = cross_total - cross[fold]
            train_traits = trait_total - trait_sums[fold]
            centered = train_gram - mean[:, None] * train_sums[None, :] - train_sums[:, None] * mean[None, :] + train_count * mean[:, None] * mean[None, :]
            system = scale[:, None] * centered * scale[None, :]
            target = scale[:, None] * (train_cross.T - mean[:, None] * train_traits[None, :])
            shrunk = system[None] + (ratios * VB)[:, None, None] * identity[None]
            beta = solve_batch(shrunk, jnp.broadcast_to(target, (SHRINK,) + target.shape))
            coef = (scale[None, :, None] * beta).astype(jnp.bfloat16)
            shift = jnp.einsum('v,lvt->lt', mean, coef.astype(jnp.float32), precision=HIGH)
            for shrink in range(SHRINK):
                pred = jnp.dot(columns.astype(jnp.float32), coef[shrink].astype(jnp.float32), preferred_element_type=jnp.float32) - shift[shrink][None, :]
                accum = accum.at[shrink].add(pred.T * masks[fold][None, :])
        block_preds.append(accum)
    preds = jnp.stack(block_preds)
    pmean = lax.optimization_barrier(jnp.sum(preds, axis=-1)) / SAMPLES
    pvar = lax.optimization_barrier(jnp.sum(preds * preds, axis=-1)) / SAMPLES - pmean * pmean
    level0 = (preds - pmean[..., None]) * lax.rsqrt(pvar + EPS)[..., None]
    flat = level0.reshape(BLOCKS * SHRINK, TRAITS, SAMPLES)
    fold_grams = []
    fold_cross = []
    for fold in range(FOLDS):
        weighted = flat * masks[fold][None, None, :]
        fold_grams.append(jnp.einsum('ats,bts->tab', weighted, flat, precision=HIGH))
        fold_cross.append(jnp.einsum('ats,ts->ta', weighted, traits_wide, precision=HIGH))
    fold_grams = jnp.stack(fold_grams)
    fold_cross = jnp.stack(fold_cross)
    train_grams = lax.optimization_barrier(jnp.sum(fold_grams, axis=0))[None] - fold_grams
    train_cross = lax.optimization_barrier(jnp.sum(fold_cross, axis=0))[None] - fold_cross
    count_pred = BLOCKS * SHRINK
    shrunk = train_grams + SAMPLES / 4.0 * jnp.eye(count_pred, dtype=jnp.float32)
    weights = solve_batch(shrunk.reshape(-1, count_pred, count_pred), train_cross.reshape(-1, count_pred))
    weights = weights.reshape(FOLDS, TRAITS, count_pred)
    every_fold = jnp.einsum('ats,kta->kts', flat, weights, precision=HIGH)
    blended = jnp.einsum('kts,ks->ts', every_fold, masks, precision=HIGH)
    bmean = lax.optimization_barrier(jnp.sum(blended, axis=-1)) / SAMPLES
    bvar = lax.optimization_barrier(jnp.sum(blended * blended, axis=-1)) / SAMPLES - bmean * bmean
    blend = (blended - bmean[:, None]) * lax.rsqrt(bvar + EPS)[:, None]
    return (level0, blend)
```

```python
import functools

import jax
import jax.numpy as jnp
from jax import lax
from jax.experimental import pallas as pl
from jax.experimental.pallas import tpu as pltpu
from jax.sharding import PartitionSpec as P

FOLDS = 5
SHRINK = 5


RATIOS = (99.0, 3.0, 1.0, 1.0 / 3.0, 1.0 / 99.0)
EPS = 1e-05
HIGH = lax.Precision.HIGHEST


def solve_batch(systems, right_sides):
    factors = jnp.linalg.cholesky(systems)

    def solve_single(factor, right_side):
        return jax.scipy.linalg.cho_solve((factor, True), right_side)

    return jax.vmap(solve_single)(factors, right_sides)


def shards(dosages, traits, folds):
    rows, width = dosages.shape
    traits_count = traits.shape[0]
    fold_ids = jnp.arange(FOLDS, dtype=jnp.int32)
    masks = (folds[None, :] == fold_ids[:, None]).astype(jnp.float32)
    mask_half = masks.astype(jnp.bfloat16)
    traits_wide = traits.astype(jnp.float32)
    grams = []
    crosses = []
    for fold in range(FOLDS):
        weighted = dosages * mask_half[fold][:, None]
        grams.append(jnp.einsum("ri,rj->ij", dosages, weighted, preferred_element_type=jnp.float32))
        crosses.append(
            jnp.dot(traits * mask_half[fold][None, :], dosages, preferred_element_type=jnp.float32)
        )
    gram = jnp.stack(grams)
    cross = jnp.stack(crosses)
    sums = jnp.dot(mask_half, dosages, preferred_element_type=jnp.float32)
    counts = jnp.sum(masks, axis=1)
    trait_sums = jnp.einsum("ks,ts->kt", masks, traits_wide, precision=HIGH)
    gram, sums, cross, counts, trait_sums = lax.psum(
        (gram, sums, cross, counts, trait_sums), "samp"
    )
    total = jnp.sum(counts)
    mean = jnp.sum(sums, axis=0) / total
    gram_total = jnp.sum(gram, axis=0)
    variance = jnp.diagonal(gram_total) / total - mean * mean
    scale = lax.rsqrt(variance + EPS)
    sums_total = jnp.sum(sums, axis=0)
    cross_total = jnp.sum(cross, axis=0)
    trait_total = jnp.sum(trait_sums, axis=0)
    ratios = jnp.array(RATIOS, dtype=jnp.float32)
    identity = jnp.eye(width, dtype=jnp.float32)

    def train_system(fold):
        train_gram = gram_total - lax.dynamic_index_in_dim(gram, fold, 0, keepdims=False)
        train_sums = sums_total - lax.dynamic_index_in_dim(sums, fold, 0, keepdims=False)
        train_count = total - lax.dynamic_index_in_dim(counts, fold, 0, keepdims=False)
        train_cross = cross_total - lax.dynamic_index_in_dim(cross, fold, 0, keepdims=False)
        train_traits = trait_total - lax.dynamic_index_in_dim(trait_sums, fold, 0, keepdims=False)
        centered = (
            train_gram
            - mean[:, None] * train_sums[None, :]
            - train_sums[:, None] * mean[None, :]
            + train_count * mean[:, None] * mean[None, :]
        )
        system = scale[:, None] * centered * scale[None, :]
        target = scale[:, None] * (train_cross.T - mean[:, None] * train_traits[None, :])
        return (system, target)

    systems_count = FOLDS * SHRINK
    per_device = -(-systems_count // lax.axis_size("samp"))
    first = lax.axis_index("samp") * per_device

    def solve_own(offset):
        which = jnp.minimum(first + offset, systems_count - 1)
        fold = which // SHRINK
        shrink = which - fold * SHRINK
        system, target = train_system(fold)
        penalty = jnp.sum(
            jnp.where(jnp.arange(SHRINK, dtype=jnp.int32) == shrink, ratios * width, 0.0)
        )
        beta = solve_batch((system + penalty * identity)[None], target[None])[0]
        return (scale[:, None] * beta).astype(jnp.bfloat16)

    owned = lax.map(solve_own, jnp.arange(per_device, dtype=jnp.int32))
    collected = lax.all_gather(owned, "samp", axis=0, tiled=True)
    coef = collected[:systems_count].reshape(FOLDS, SHRINK, width, traits_count)
    coef_flat = coef.transpose(2, 0, 1, 3).reshape(width, FOLDS * SHRINK * traits_count)
    shift = jnp.einsum("v,klvt->klt", mean, coef.astype(jnp.float32), precision=HIGH)
    raw = jnp.einsum("vc,rv->cr", coef_flat, dosages, preferred_element_type=jnp.float32)
    outcome = raw.reshape(FOLDS, SHRINK, traits_count, rows) - shift[..., None]
    level_pred = jnp.einsum("kltr,kr->ltr", outcome, masks, precision=HIGH)
    group = traits_count // lax.axis_size("blk")
    start = lax.axis_index("blk") * group
    own_traits = lax.dynamic_slice_in_dim(traits_wide, start, group, 0)
    own_sums = lax.dynamic_slice_in_dim(trait_sums, start, group, 1)
    arrived = lax.all_to_all(level_pred[None], "blk", split_axis=2, concat_axis=0, tiled=True)
    count_pred = arrived.shape[0] * arrived.shape[1]
    flat = arrived.reshape(count_pred, group, rows)
    raw_grams = jnp.einsum("ks,ats,bts->ktab", masks, flat, flat, precision=HIGH)
    raw_cross = jnp.einsum("ks,ats,ts->kta", masks, flat, own_traits, precision=HIGH)
    raw_sums = jnp.einsum("ks,ats->kta", masks, flat, precision=HIGH)
    raw_grams, raw_cross, raw_sums = lax.psum((raw_grams, raw_cross, raw_sums), "samp")
    pred_mean = jnp.sum(raw_sums, axis=0) / total
    pred_sq = jnp.diagonal(jnp.sum(raw_grams, axis=0), axis1=1, axis2=2)
    pred_scale = lax.rsqrt(pred_sq / total - pred_mean * pred_mean + EPS)
    standard = (flat - pred_mean.T[:, :, None]) * pred_scale.T[:, :, None]
    outer_scale = pred_scale[None, :, :, None] * pred_scale[None, :, None, :]
    fold_grams = outer_scale * (
        raw_grams
        - pred_mean[None, :, :, None] * raw_sums[:, :, None, :]
        - raw_sums[:, :, :, None] * pred_mean[None, :, None, :]
        + counts[:, None, None, None] * pred_mean[None, :, :, None] * pred_mean[None, :, None, :]
    )
    fold_cross = pred_scale[None] * (raw_cross - pred_mean[None] * own_sums[:, :, None])
    level0 = standard.reshape(arrived.shape)
    train_grams = jnp.sum(fold_grams, axis=0)[None] - fold_grams
    train_cross = jnp.sum(fold_cross, axis=0)[None] - fold_cross
    shrunk = train_grams + total / 4.0 * jnp.eye(count_pred, dtype=jnp.float32)
    weights = solve_batch(
        shrunk.reshape(-1, count_pred, count_pred), train_cross.reshape(-1, count_pred)
    )
    weights = weights.reshape(FOLDS, group, count_pred)
    every_fold = jnp.einsum("ats,kta->kts", standard, weights, precision=HIGH)
    blended = jnp.einsum("kts,ks->ts", every_fold, masks, precision=HIGH)
    blend_sum, blend_sq = lax.psum(
        (jnp.sum(blended, axis=-1), jnp.sum(blended * blended, axis=-1)), "samp"
    )
    blend_mean = blend_sum / total
    blend_var = blend_sq / total - blend_mean * blend_mean
    blend = (blended - blend_mean[:, None]) * lax.rsqrt(blend_var + EPS)[:, None]
    return (level0, blend)


MESH = pl.DeviceIdType.MESH
AUX = 32
ROWS1 = 24
PANEL = 128
LIMIT = 48 * 1024 * 1024
VMEM = pl.BlockSpec(memory_space=pltpu.VMEM)
ANY = pl.BlockSpec(memory_space=pl.ANY)


def high_dot(a, b, dims):
    return lax.dot_general(
        a, b, (dims, ((), ())), precision=HIGH, preferred_element_type=jnp.float32
    )


def greet(axis, count):
    barrier = pltpu.get_barrier_semaphore()
    me = lax.axis_index(axis)
    for step in range(1, count):
        pl.semaphore_signal(
            barrier, inc=1, device_id={axis: lax.rem(me + step, count)}, device_id_type=MESH
        )
    pl.semaphore_wait(barrier, count - 1)


def gather_kernel(depth, x_ref, aux_ref, xo_ref, auxo_ref, send, recv, asend, arecv, own):
    me = lax.axis_index("samp")
    z, x = me // 2, lax.rem(me, 2)
    greet("samp", 2 * depth)
    keep = pltpu.make_async_copy(x_ref, xo_ref.at[me], own.at[0])
    keep.start()
    keep_aux = pltpu.make_async_copy(aux_ref, auxo_ref.at[me], own.at[1])
    keep_aux.start()

    def x_copy(src, slot, lane, target):
        return pltpu.make_async_remote_copy(
            src_ref=src,
            dst_ref=xo_ref.at[slot],
            send_sem=send.at[lane],
            recv_sem=recv.at[slot],
            device_id={"samp": target},
            device_id_type=MESH,
        )

    def aux_copy(step):
        return pltpu.make_async_remote_copy(
            src_ref=aux_ref,
            dst_ref=auxo_ref.at[me],
            send_sem=asend.at[step],
            recv_sem=arecv.at[me],
            device_id={"samp": lax.rem(me + step, 2 * depth)},
            device_id_type=MESH,
        )

    partner = z * 2 + 1 - x
    for step in range(1, 2 * depth):
        aux_copy(step).start()

    @pl.when(z + 1 < depth)
    def _():
        x_copy(x_ref, me, 0, me + 2).start()

    @pl.when(z >= 1)
    def _():
        x_copy(x_ref, me, depth, me - 2).start()

    x_copy(x_ref, me, 2 * depth, partner).start()
    for far in range(1, depth):
        below, above = me - 2 * far, me + 2 * far

        @pl.when(z >= far)
        def _():
            x_copy(xo_ref.at[below], below, 0, partner).wait_recv()

            @pl.when(z + 1 < depth)
            def _():
                x_copy(xo_ref.at[below], below, far, me + 2).start()

            x_copy(xo_ref.at[below], below, 2 * depth + far, partner).start()

        @pl.when(z + far < depth)
        def _():
            x_copy(xo_ref.at[above], above, 0, partner).wait_recv()

            @pl.when(z >= 1)
            def _():
                x_copy(xo_ref.at[above], above, depth + far, me - 2).start()

            x_copy(xo_ref.at[above], above, 3 * depth + far, partner).start()

    for layer in range(depth):
        slot = layer * 2 + 1 - x
        x_copy(xo_ref.at[slot], slot, 0, partner).wait_recv()
    for step in range(1, 2 * depth):
        slot = lax.rem(me + step, 2 * depth)
        pltpu.make_async_remote_copy(
            src_ref=aux_ref,
            dst_ref=auxo_ref.at[slot],
            send_sem=asend.at[step],
            recv_sem=arecv.at[slot],
            device_id={"samp": slot},
            device_id_type=MESH,
        ).wait()
    x_copy(x_ref, me, 2 * depth, partner).wait_send()
    for far in range(depth):

        @pl.when((z >= far) & (z + 1 < depth))
        def _():
            x_copy(x_ref, me, far, partner).wait_send()

        @pl.when((z + far < depth) & (z >= 1))
        def _():
            x_copy(x_ref, me, depth + far, partner).wait_send()

        if far:

            @pl.when(z >= far)
            def _():
                x_copy(x_ref, me, 2 * depth + far, partner).wait_send()

            @pl.when(z + far < depth)
            def _():
                x_copy(x_ref, me, 3 * depth + far, partner).wait_send()

    keep.wait()
    keep_aux.wait()


def gather_samples(x, aux, count):
    return pl.pallas_call(
        functools.partial(gather_kernel, count // 2),
        out_shape=(
            jax.ShapeDtypeStruct((count,) + x.shape, x.dtype),
            jax.ShapeDtypeStruct((count,) + aux.shape, aux.dtype),
        ),
        in_specs=[ANY, ANY],
        out_specs=(ANY, ANY),
        scratch_shapes=[
            pltpu.SemaphoreType.DMA((2 * count,)),
            pltpu.SemaphoreType.DMA((count,)),
            pltpu.SemaphoreType.DMA((count,)),
            pltpu.SemaphoreType.DMA((count,)),
            pltpu.SemaphoreType.DMA((2,)),
        ],
        compiler_params=pltpu.CompilerParams(collective_id=0, has_side_effects=True),
        name="gather_samples",
    )(x, aux)


def spread_kernel(axis, count, split, a_ref, o_ref, send, recv, own):
    me = lax.axis_index(axis)
    greet(axis, count)
    keep = pltpu.make_async_copy(a_ref.at[me] if split else a_ref, o_ref.at[me], own)
    keep.start()
    for step in range(1, count):
        other = lax.rem(me + step, count)
        pltpu.make_async_remote_copy(
            src_ref=a_ref.at[other] if split else a_ref,
            dst_ref=o_ref.at[me],
            send_sem=send.at[step],
            recv_sem=recv.at[me],
            device_id={axis: other},
            device_id_type=MESH,
        ).start()
    for step in range(1, count):
        other = lax.rem(me + step, count)
        pltpu.make_async_remote_copy(
            src_ref=a_ref.at[other] if split else a_ref,
            dst_ref=o_ref.at[other],
            send_sem=send.at[step],
            recv_sem=recv.at[other],
            device_id={axis: other},
            device_id_type=MESH,
        ).wait()
    keep.wait()


def spread(a, axis, count, split, number):
    return pl.pallas_call(
        functools.partial(spread_kernel, axis, count, split),
        out_shape=jax.ShapeDtypeStruct(a.shape if split else (count,) + a.shape, a.dtype),
        in_specs=[VMEM],
        out_specs=VMEM,
        scratch_shapes=[
            pltpu.SemaphoreType.DMA((count,)),
            pltpu.SemaphoreType.DMA((count,)),
            pltpu.SemaphoreType.DMA,
        ],
        compiler_params=pltpu.CompilerParams(collective_id=number, has_side_effects=True),
        name="spread_" + axis + str(number),
    )(a)


def sweep(m_ref, batch, pivot):
    size, lanes = m_ref.shape[1:]
    row_at = lax.broadcasted_iota(jnp.int32, (size, lanes), 0) == pivot
    lane_at = lax.broadcasted_iota(jnp.int32, (size, lanes), 1) == pivot
    row_col = lax.broadcasted_iota(jnp.int32, (size, 1), 0) == pivot
    lane_row = lax.broadcasted_iota(jnp.int32, (1, lanes), 1) == pivot
    cross = row_at | lane_at
    for b in range(batch):
        whole = m_ref[b]
        row = m_ref[b, pl.ds(pivot, 1), :]
        column = jnp.sum(jnp.where(lane_at, whole, 0.0), axis=1, keepdims=True)
        head = jnp.sum(jnp.where(lane_row, row, 0.0), axis=1, keepdims=True)
        inverse = 1.0 / head
        row = jnp.where(lane_row, -inverse, row * inverse)
        column = jnp.where(row_col, -1.0, column)
        m_ref[b] = jnp.where(cross, 0.0, whole) - column * row


def solve_kernel(systems, own, x_ref, aux_ref, coef_ref, mean_ref, gram, cross, pairs, all_aux, sq, mats, rhs, diag):
    count, rows, width = x_ref.shape
    traits = coef_ref.shape[0] // own
    total = count * rows
    first = lax.axis_index("samp") * own
    fold_of = [jnp.minimum(first + i, systems - 1) // SHRINK for i in range(own)]
    folds = [fold_of[0], fold_of[own - 1]]
    for ref in (gram, cross, pairs, all_aux, sq):
        ref[...] = jnp.zeros_like(ref)
    aux_row = lax.broadcasted_iota(jnp.int32, (AUX, width), 0)
    fold_rows = (aux_row >= traits) & (aux_row < traits + FOLDS)
    picks = jnp.concatenate(
        [
            jnp.where(fold_rows & (aux_row != traits + fold), 1.0, 0.0).astype(jnp.bfloat16)
            for fold in folds
        ],
        axis=1,
    )
    row_id = lax.broadcasted_iota(jnp.int32, (AUX, rows), 0)

    def add_block(i, _):
        x = x_ref[i]
        aux = aux_ref[i]
        aux_wide = aux.astype(jnp.float32)
        keep = lax.dot_general(
            aux, picks, (((0,), (0,)), ((), ())), preferred_element_type=jnp.float32
        ).astype(jnp.bfloat16)
        weighted = jnp.concatenate([x, x], axis=1) * keep
        gram[...] += lax.dot_general(
            x, weighted, (((0,), (0,)), ((), ())), preferred_element_type=jnp.float32
        )
        all_aux[...] += jnp.dot(aux, x, preferred_element_type=jnp.float32)
        wide = x.astype(jnp.float32)
        sq[...] += jnp.sum(wide * wide, axis=0, keepdims=True)
        for j, fold in enumerate(folds):
            held = jnp.sum(jnp.where(row_id == traits + fold, aux_wide, 0.0), axis=0, keepdims=True)
            aux_train = (aux_wide * (1.0 - held)).astype(jnp.bfloat16)
            cross[j] += jnp.dot(aux_train, x, preferred_element_type=jnp.float32)
            pairs[j] += lax.dot_general(
                aux_train, aux, (((1,), (1,)), ((), ())), preferred_element_type=jnp.float32
            )
        return 0

    lax.fori_loop(0, count, add_block, 0)
    fold_lines = lambda a: jnp.sum(jnp.where(fold_rows, a, 0.0), axis=0, keepdims=True)
    mean = fold_lines(all_aux[...]) / total
    scale = lax.rsqrt(sq[...] / total - mean * mean + EPS)
    mean_ref[...] = jnp.broadcast_to(mean, mean_ref.shape)
    pair_row = lax.broadcasted_iota(jnp.int32, (AUX, AUX), 0)
    pair_col = lax.broadcasted_iota(jnp.int32, (AUX, AUX), 1)
    pair_fold = (pair_col >= traits) & (pair_col < traits + FOLDS)
    eye = lax.broadcasted_iota(jnp.int32, (width, width), 0) == lax.broadcasted_iota(
        jnp.int32, (width, width), 1
    )
    column_of = lambda line: jnp.sum(jnp.where(eye, line, 0.0), axis=1, keepdims=True)
    mean_col, scale_col = column_of(mean), column_of(scale)
    for j in range(2):
        sums = fold_lines(cross[j])
        pair = pairs[j]
        kept = jnp.sum(jnp.where(pair_fold & (pair_row == pair_col), pair, 0.0))
        trait_sums = jnp.sum(jnp.where(pair_fold, pair, 0.0), axis=1, keepdims=True)[:traits]
        half = slice(j * width, (j + 1) * width)
        gram[:, half] = scale_col * scale * (
            gram[:, half] - mean_col * sums - column_of(sums) * mean + kept * (mean_col * mean)
        )
        cross[j, :traits] = scale * (cross[j, :traits] - trait_sums * mean)
    for i in range(own):
        shrink = jnp.minimum(first + i, systems - 1) - fold_of[i] * SHRINK
        penalty = jnp.float32(RATIOS[0] * width)
        for l in range(1, SHRINK):
            penalty = jnp.where(shrink == l, jnp.float32(RATIOS[l] * width), penalty)
        late = fold_of[i] != folds[0]
        mats[i] = jnp.where(late, gram[:, width:], gram[:, :width]) + jnp.where(eye, penalty, 0.0)
        rhs[i] = jnp.where(late, cross[1, :traits], cross[0, :traits])
    steps = width // PANEL
    for j in range(steps):
        here = slice(j * PANEL, (j + 1) * PANEL)
        rest = slice((j + 1) * PANEL, width)
        at = diag.at[j]
        for i in range(own):
            at[i] = mats[i, here, here]

        def one(pivot, _):
            sweep(at, own, pivot)
            return 0

        lax.fori_loop(0, PANEL, one, 0)
        for i in range(own):
            right = -high_dot(rhs[i, :, here], at[i], ((1,), (0,)))
            rhs[i, :, here] = right
            if j + 1 < steps:
                tail = mats[i, here, rest]
                solved = high_dot(at[i], tail, ((1,), (0,)))
                mats[i, rest, rest] += high_dot(tail, solved, ((0,), (0,)))
                rhs[i, :, rest] -= high_dot(right, tail, ((1,), (0,)))
    for j in range(steps - 2, -1, -1):
        here = slice(j * PANEL, (j + 1) * PANEL)
        rest = slice((j + 1) * PANEL, width)
        for i in range(own):
            back = high_dot(rhs[i, :, rest], mats[i, here, rest], ((1,), (1,)))
            rhs[i, :, here] += high_dot(back, diag[j, i], ((1,), (0,)))
    for i in range(own):
        coef_ref[i * traits : (i + 1) * traits] = (rhs[i] * scale).astype(jnp.bfloat16)


def solve_level0(x_all, aux_all, traits):
    count, rows, width = x_all.shape
    systems = FOLDS * SHRINK
    own = -(-systems // count)
    f32 = jnp.float32
    return pl.pallas_call(
        functools.partial(solve_kernel, systems, own),
        out_shape=(
            jax.ShapeDtypeStruct((own * traits, width), jnp.bfloat16),
            jax.ShapeDtypeStruct((8, width), f32),
        ),
        in_specs=[VMEM, VMEM],
        out_specs=(VMEM, VMEM),
        scratch_shapes=[
            pltpu.VMEM((width, 2 * width), f32),
            pltpu.VMEM((2, AUX, width), f32),
            pltpu.VMEM((2, AUX, AUX), f32),
            pltpu.VMEM((AUX, width), f32),
            pltpu.VMEM((1, width), f32),
            pltpu.VMEM((own, width, width), f32),
            pltpu.VMEM((own, traits, width), f32),
            pltpu.VMEM((width // PANEL, own, PANEL, PANEL), f32),
        ],
        compiler_params=pltpu.CompilerParams(vmem_limit_bytes=LIMIT),
        name="solve_level0",
    )(x_all, aux_all)


def predict_kernel(coef_ref, mean_ref, x_ref, folds_ref, o_ref):
    parts, _, group, _ = o_ref.shape
    traits = parts * group
    per_fold = SHRINK * traits
    coef = coef_ref[: FOLDS * per_fold]
    raw = lax.dot_general(
        coef, x_ref[...], (((1,), (1,)), ((), ())), preferred_element_type=jnp.float32
    )
    shift = jnp.sum(coef.astype(jnp.float32) * mean_ref[:1], axis=1, keepdims=True)
    raw = raw - shift
    folds = folds_ref[...]
    out = jnp.zeros((per_fold, raw.shape[1]), jnp.float32)
    for k in range(FOLDS):
        out = jnp.where(folds == k, raw[k * per_fold : (k + 1) * per_fold], out)
    for g in range(parts):
        for l in range(SHRINK):
            o_ref[g, l] = out[l * traits + g * group : l * traits + (g + 1) * group]


def moments_kernel(p_ref, traits_ref, folds_ref, f_ref, e_ref):
    blocks, shrinks, group, rows = p_ref.shape
    preds = blocks * shrinks
    f_ref[...] = jnp.zeros_like(f_ref)
    for t in range(group):
        base = t * ROWS1
        for b in range(blocks):
            for l in range(shrinks):
                at = base + b * shrinks + l
                f_ref[at : at + 1] = p_ref[b, l, t : t + 1]
        f_ref[base + preds : base + preds + 1] = traits_ref[t : t + 1]
        f_ref[base + preds + 1 : base + preds + 2] = jnp.ones((1, rows), jnp.float32)
    f = f_ref[...]
    size = group * ROWS1
    folds = folds_ref[...]
    lane = lax.broadcasted_iota(jnp.int32, (ROWS1, size), 1)
    for k in range(FOLDS):
        full = high_dot(jnp.where(folds == k, f, 0.0), f, ((1,), (1,)))
        packed = jnp.zeros((ROWS1, size), jnp.float32)
        for t in range(group):
            inside = (lane >= t * ROWS1) & (lane < (t + 1) * ROWS1)
            packed = jnp.where(inside, full[t * ROWS1 : (t + 1) * ROWS1], packed)
        e_ref[k * ROWS1 : (k + 1) * ROWS1] = packed


def blend_kernel(total, e_ref, f_ref, p_ref, folds_ref, level_ref, blend_ref, mats):
    blocks, shrinks, group, rows = p_ref.shape
    preds = blocks * shrinks
    summed = jnp.sum(e_ref[...], axis=0)
    shape = (ROWS1, ROWS1)
    row = lax.broadcasted_iota(jnp.int32, shape, 0)
    col = lax.broadcasted_iota(jnp.int32, shape, 1)
    col_in = lax.broadcasted_iota(jnp.int32, (ROWS1, 1), 0) < preds
    row_in = lax.broadcasted_iota(jnp.int32, (1, ROWS1), 1) < preds
    one_lane = lax.broadcasted_iota(jnp.int32, (1, ROWS1), 1) == preds + 1
    ridge = jnp.where((row == col) & (row < preds), total / 4.0, 0.0)
    own = [
        [
            summed[k * ROWS1 : (k + 1) * ROWS1, t * ROWS1 : (t + 1) * ROWS1]
            for k in range(FOLDS)
        ]
        for t in range(group)
    ]
    means, scales = [], []
    for t in range(group):
        full = own[t][0]
        for k in range(1, FOLDS):
            full = full + own[t][k]
        mean_row = jnp.where(row_in, full[preds + 1 : preds + 2] / total, 0.0)
        mean_col = jnp.where(col_in, full[:, preds + 1 : preds + 2] / total, 0.0)
        square = jnp.where(row == col, full, 0.0) / total
        sq_row = jnp.sum(square, axis=0, keepdims=True)
        sq_col = jnp.sum(square, axis=1, keepdims=True)
        scale_row = jnp.where(row_in, lax.rsqrt(sq_row - mean_row * mean_row + EPS), 1.0)
        scale_col = jnp.where(col_in, lax.rsqrt(sq_col - mean_col * mean_col + EPS), 1.0)
        means.append((mean_row, mean_col))
        scales.append((scale_row, scale_col))
        for k in range(FOLDS):
            train = full - own[t][k]
            sums_row = train[preds + 1 : preds + 2]
            sums_col = train[:, preds + 1 : preds + 2]
            kept = train[preds + 1 : preds + 2, preds + 1 : preds + 2]
            centered = (
                train - mean_col * sums_row - sums_col * mean_row + kept * (mean_col * mean_row)
            )
            mats[t * FOLDS + k] = scale_col * scale_row * centered + ridge
    for b in range(blocks):
        for l in range(shrinks):
            at = b * shrinks + l
            means_at = jnp.concatenate([means[t][1][at : at + 1] for t in range(group)], axis=0)
            scales_at = jnp.concatenate([scales[t][1][at : at + 1] for t in range(group)], axis=0)
            level_ref[b, l] = (p_ref[b, l] - means_at) * scales_at

    def one(pivot, _):
        sweep(mats, group * FOLDS, pivot)
        return 0

    lax.fori_loop(0, preds, one, 0)
    folds = folds_ref[...]
    for t in range(group):
        mean_row, scale_row = means[t][0], scales[t][0]
        lines = []
        first = jnp.zeros((1, 1), jnp.float32)
        second = jnp.zeros((1, 1), jnp.float32)
        for k in range(FOLDS):
            line = jnp.where(row_in, mats[t * FOLDS + k, preds : preds + 1, :] * scale_row, 0.0)
            offset = jnp.sum(line * mean_row, axis=1, keepdims=True)
            line = jnp.where(one_lane, -offset, line)
            lines.append(line)
            product = jnp.sum(own[t][k] * line, axis=1, keepdims=True)
            line_col = jnp.sum(jnp.where(row == col, line, 0.0), axis=1, keepdims=True)
            first = first + product[preds + 1 : preds + 2]
            second = second + jnp.sum(product * line_col, axis=0, keepdims=True)
        lines.append(jnp.zeros((8 - FOLDS, ROWS1), jnp.float32))
        every = high_dot(
            jnp.concatenate(lines, axis=0),
            f_ref[t * ROWS1 : (t + 1) * ROWS1],
            ((1,), (0,)),
        )
        p = jnp.zeros((1, rows), jnp.float32)
        for k in range(FOLDS):
            p = jnp.where(folds == k, every[k : k + 1], p)
        mean = first / total
        spread_of = second / total - mean * mean
        blend_ref[t : t + 1] = (p - mean) * lax.rsqrt(spread_of + EPS)


def plain(kernel, out_shape, name, *args, scratch=()):
    return pl.pallas_call(
        kernel,
        out_shape=out_shape,
        in_specs=[VMEM] * len(args),
        out_specs=jax.tree.map(lambda _: VMEM, out_shape),
        scratch_shapes=list(scratch),
        compiler_params=pltpu.CompilerParams(vmem_limit_bytes=LIMIT),
        name=name,
    )(*args)


def fast(samp, blk, dosages, traits, folds):
    rows, width = dosages.shape
    count_traits = traits.shape[0]
    group = count_traits // blk
    f32 = jnp.float32
    fold_ids = jnp.arange(AUX - count_traits, dtype=jnp.int32)
    one_hot = (folds[None, :] == fold_ids[:, None]).astype(jnp.bfloat16)
    aux = jnp.concatenate([traits, one_hot], axis=0)
    folds_row = folds[None, :]
    own_traits = lax.dynamic_slice_in_dim(
        traits, lax.axis_index("blk") * group, group, 0
    ).astype(f32)
    x_all, aux_all = gather_samples(dosages, aux, samp)
    coef, mean = solve_level0(x_all, aux_all, count_traits)
    coef_all = spread(coef, "samp", samp, False, 1).reshape(-1, width)
    shape = jax.ShapeDtypeStruct((blk, SHRINK, group, rows), f32)
    pred = plain(predict_kernel, shape, "predict", coef_all, mean, dosages, folds_row)
    pred = spread(pred, "blk", blk, True, 2)
    size = group * ROWS1
    stacked, moments = plain(
        moments_kernel,
        (jax.ShapeDtypeStruct((size, rows), f32), jax.ShapeDtypeStruct((FOLDS * ROWS1, size), f32)),
        "moments",
        pred,
        own_traits,
        folds_row,
    )
    moments = spread(moments, "samp", samp, False, 3)
    level0, blend = plain(
        functools.partial(blend_kernel, float(samp * rows)),
        (shape, jax.ShapeDtypeStruct((group, rows), f32)),
        "blend",
        moments,
        stacked,
        pred,
        folds_row,
        scratch=[pltpu.VMEM((group * FOLDS, ROWS1, ROWS1), f32)],
    )
    return level0, blend


def solution(mesh):
    in_specs = (P("samp", "blk"), P(None, "samp"), P("samp"))
    out_specs = (P(None, None, "blk", "samp"), P("blk", "samp"))
    samp, blk = mesh.shape["samp"], mesh.shape["blk"]
    body = functools.partial(fast, samp, blk) if samp == 8 else shards
    return jax.shard_map(body, mesh=mesh, in_specs=in_specs, out_specs=out_specs, check_vma=False)
```

```python
import functools

import jax
import jax.numpy as jnp
from jax import lax
from jax.experimental import pallas as pl
from jax.experimental.pallas import tpu as pltpu
from jax.sharding import PartitionSpec as P

FOLDS = 5
SHRINK = 5


RATIOS = (99.0, 3.0, 1.0, 1.0 / 3.0, 1.0 / 99.0)
EPS = 1e-05
HIGH = lax.Precision.HIGHEST


def solve_batch(systems, right_sides):
    factors = jnp.linalg.cholesky(systems)

    def solve_single(factor, right_side):
        return jax.scipy.linalg.cho_solve((factor, True), right_side)

    return jax.vmap(solve_single)(factors, right_sides)


def shards(dosages, traits, folds):
    rows, width = dosages.shape
    traits_count = traits.shape[0]
    fold_ids = jnp.arange(FOLDS, dtype=jnp.int32)
    masks = (folds[None, :] == fold_ids[:, None]).astype(jnp.float32)
    mask_half = masks.astype(jnp.bfloat16)
    traits_wide = traits.astype(jnp.float32)
    grams = []
    crosses = []
    for fold in range(FOLDS):
        weighted = dosages * mask_half[fold][:, None]
        grams.append(jnp.einsum("ri,rj->ij", dosages, weighted, preferred_element_type=jnp.float32))
        crosses.append(
            jnp.dot(traits * mask_half[fold][None, :], dosages, preferred_element_type=jnp.float32)
        )
    gram = jnp.stack(grams)
    cross = jnp.stack(crosses)
    sums = jnp.dot(mask_half, dosages, preferred_element_type=jnp.float32)
    counts = jnp.sum(masks, axis=1)
    trait_sums = jnp.einsum("ks,ts->kt", masks, traits_wide, precision=HIGH)
    gram, sums, cross, counts, trait_sums = lax.psum(
        (gram, sums, cross, counts, trait_sums), "samp"
    )
    total = jnp.sum(counts)
    mean = jnp.sum(sums, axis=0) / total
    gram_total = jnp.sum(gram, axis=0)
    variance = jnp.diagonal(gram_total) / total - mean * mean
    scale = lax.rsqrt(variance + EPS)
    sums_total = jnp.sum(sums, axis=0)
    cross_total = jnp.sum(cross, axis=0)
    trait_total = jnp.sum(trait_sums, axis=0)
    ratios = jnp.array(RATIOS, dtype=jnp.float32)
    identity = jnp.eye(width, dtype=jnp.float32)

    def train_system(fold):
        train_gram = gram_total - lax.dynamic_index_in_dim(gram, fold, 0, keepdims=False)
        train_sums = sums_total - lax.dynamic_index_in_dim(sums, fold, 0, keepdims=False)
        train_count = total - lax.dynamic_index_in_dim(counts, fold, 0, keepdims=False)
        train_cross = cross_total - lax.dynamic_index_in_dim(cross, fold, 0, keepdims=False)
        train_traits = trait_total - lax.dynamic_index_in_dim(trait_sums, fold, 0, keepdims=False)
        centered = (
            train_gram
            - mean[:, None] * train_sums[None, :]
            - train_sums[:, None] * mean[None, :]
            + train_count * mean[:, None] * mean[None, :]
        )
        system = scale[:, None] * centered * scale[None, :]
        target = scale[:, None] * (train_cross.T - mean[:, None] * train_traits[None, :])
        return (system, target)

    systems_count = FOLDS * SHRINK
    per_device = -(-systems_count // lax.axis_size("samp"))
    first = lax.axis_index("samp") * per_device

    def solve_own(offset):
        which = jnp.minimum(first + offset, systems_count - 1)
        fold = which // SHRINK
        shrink = which - fold * SHRINK
        system, target = train_system(fold)
        penalty = jnp.sum(
            jnp.where(jnp.arange(SHRINK, dtype=jnp.int32) == shrink, ratios * width, 0.0)
        )
        beta = solve_batch((system + penalty * identity)[None], target[None])[0]
        return (scale[:, None] * beta).astype(jnp.bfloat16)

    owned = lax.map(solve_own, jnp.arange(per_device, dtype=jnp.int32))
    collected = lax.all_gather(owned, "samp", axis=0, tiled=True)
    coef = collected[:systems_count].reshape(FOLDS, SHRINK, width, traits_count)
    coef_flat = coef.transpose(2, 0, 1, 3).reshape(width, FOLDS * SHRINK * traits_count)
    shift = jnp.einsum("v,klvt->klt", mean, coef.astype(jnp.float32), precision=HIGH)
    raw = jnp.einsum("vc,rv->cr", coef_flat, dosages, preferred_element_type=jnp.float32)
    outcome = raw.reshape(FOLDS, SHRINK, traits_count, rows) - shift[..., None]
    level_pred = jnp.einsum("kltr,kr->ltr", outcome, masks, precision=HIGH)
    group = traits_count // lax.axis_size("blk")
    start = lax.axis_index("blk") * group
    own_traits = lax.dynamic_slice_in_dim(traits_wide, start, group, 0)
    own_sums = lax.dynamic_slice_in_dim(trait_sums, start, group, 1)
    arrived = lax.all_to_all(level_pred[None], "blk", split_axis=2, concat_axis=0, tiled=True)
    count_pred = arrived.shape[0] * arrived.shape[1]
    flat = arrived.reshape(count_pred, group, rows)
    raw_grams = jnp.einsum("ks,ats,bts->ktab", masks, flat, flat, precision=HIGH)
    raw_cross = jnp.einsum("ks,ats,ts->kta", masks, flat, own_traits, precision=HIGH)
    raw_sums = jnp.einsum("ks,ats->kta", masks, flat, precision=HIGH)
    raw_grams, raw_cross, raw_sums = lax.psum((raw_grams, raw_cross, raw_sums), "samp")
    pred_mean = jnp.sum(raw_sums, axis=0) / total
    pred_sq = jnp.diagonal(jnp.sum(raw_grams, axis=0), axis1=1, axis2=2)
    pred_scale = lax.rsqrt(pred_sq / total - pred_mean * pred_mean + EPS)
    standard = (flat - pred_mean.T[:, :, None]) * pred_scale.T[:, :, None]
    outer_scale = pred_scale[None, :, :, None] * pred_scale[None, :, None, :]
    fold_grams = outer_scale * (
        raw_grams
        - pred_mean[None, :, :, None] * raw_sums[:, :, None, :]
        - raw_sums[:, :, :, None] * pred_mean[None, :, None, :]
        + counts[:, None, None, None] * pred_mean[None, :, :, None] * pred_mean[None, :, None, :]
    )
    fold_cross = pred_scale[None] * (raw_cross - pred_mean[None] * own_sums[:, :, None])
    level0 = standard.reshape(arrived.shape)
    train_grams = jnp.sum(fold_grams, axis=0)[None] - fold_grams
    train_cross = jnp.sum(fold_cross, axis=0)[None] - fold_cross
    shrunk = train_grams + total / 4.0 * jnp.eye(count_pred, dtype=jnp.float32)
    weights = solve_batch(
        shrunk.reshape(-1, count_pred, count_pred), train_cross.reshape(-1, count_pred)
    )
    weights = weights.reshape(FOLDS, group, count_pred)
    every_fold = jnp.einsum("ats,kta->kts", standard, weights, precision=HIGH)
    blended = jnp.einsum("kts,ks->ts", every_fold, masks, precision=HIGH)
    blend_sum, blend_sq = lax.psum(
        (jnp.sum(blended, axis=-1), jnp.sum(blended * blended, axis=-1)), "samp"
    )
    blend_mean = blend_sum / total
    blend_var = blend_sq / total - blend_mean * blend_mean
    blend = (blended - blend_mean[:, None]) * lax.rsqrt(blend_var + EPS)[:, None]
    return (level0, blend)


MESH = pl.DeviceIdType.MESH
AUX = 32
ROWS1 = 24
PANEL = 128
LIMIT = 48 * 1024 * 1024
VMEM = pl.BlockSpec(memory_space=pltpu.VMEM)
ANY = pl.BlockSpec(memory_space=pl.ANY)


def high_dot(a, b, dims):
    return lax.dot_general(
        a, b, (dims, ((), ())), precision=HIGH, preferred_element_type=jnp.float32
    )


def greet(axis, count):
    barrier = pltpu.get_barrier_semaphore()
    me = lax.axis_index(axis)
    for step in range(1, count):
        pl.semaphore_signal(
            barrier, inc=1, device_id={axis: lax.rem(me + step, count)}, device_id_type=MESH
        )
    pl.semaphore_wait(barrier, count - 1)


def gather_kernel(depth, x_ref, aux_ref, xo_ref, auxo_ref, send, recv, asend, arecv, own):
    me = lax.axis_index("samp")
    z, x = me // 2, lax.rem(me, 2)
    greet("samp", 2 * depth)
    keep = pltpu.make_async_copy(x_ref, xo_ref.at[me], own.at[0])
    keep.start()
    keep_aux = pltpu.make_async_copy(aux_ref, auxo_ref.at[me], own.at[1])
    keep_aux.start()

    def x_copy(src, slot, lane, target):
        return pltpu.make_async_remote_copy(
            src_ref=src,
            dst_ref=xo_ref.at[slot],
            send_sem=send.at[lane],
            recv_sem=recv.at[slot],
            device_id={"samp": target},
            device_id_type=MESH,
        )

    def aux_copy(step):
        return pltpu.make_async_remote_copy(
            src_ref=aux_ref,
            dst_ref=auxo_ref.at[me],
            send_sem=asend.at[step],
            recv_sem=arecv.at[me],
            device_id={"samp": lax.rem(me + step, 2 * depth)},
            device_id_type=MESH,
        )

    partner = z * 2 + 1 - x
    for step in range(1, 2 * depth):
        aux_copy(step).start()

    @pl.when(z + 1 < depth)
    def _():
        x_copy(x_ref, me, 0, me + 2).start()

    @pl.when(z >= 1)
    def _():
        x_copy(x_ref, me, depth, me - 2).start()

    x_copy(x_ref, me, 2 * depth, partner).start()
    for far in range(1, depth):
        below, above = me - 2 * far, me + 2 * far

        @pl.when(z >= far)
        def _():
            x_copy(xo_ref.at[below], below, 0, partner).wait_recv()

            @pl.when(z + 1 < depth)
            def _():
                x_copy(xo_ref.at[below], below, far, me + 2).start()

            x_copy(xo_ref.at[below], below, 2 * depth + far, partner).start()

        @pl.when(z + far < depth)
        def _():
            x_copy(xo_ref.at[above], above, 0, partner).wait_recv()

            @pl.when(z >= 1)
            def _():
                x_copy(xo_ref.at[above], above, depth + far, me - 2).start()

            x_copy(xo_ref.at[above], above, 3 * depth + far, partner).start()

    for layer in range(depth):
        slot = layer * 2 + 1 - x
        x_copy(xo_ref.at[slot], slot, 0, partner).wait_recv()
    for step in range(1, 2 * depth):
        slot = lax.rem(me + step, 2 * depth)
        pltpu.make_async_remote_copy(
            src_ref=aux_ref,
            dst_ref=auxo_ref.at[slot],
            send_sem=asend.at[step],
            recv_sem=arecv.at[slot],
            device_id={"samp": slot},
            device_id_type=MESH,
        ).wait()
    x_copy(x_ref, me, 2 * depth, partner).wait_send()
    for far in range(depth):

        @pl.when((z >= far) & (z + 1 < depth))
        def _():
            x_copy(x_ref, me, far, partner).wait_send()

        @pl.when((z + far < depth) & (z >= 1))
        def _():
            x_copy(x_ref, me, depth + far, partner).wait_send()

        if far:

            @pl.when(z >= far)
            def _():
                x_copy(x_ref, me, 2 * depth + far, partner).wait_send()

            @pl.when(z + far < depth)
            def _():
                x_copy(x_ref, me, 3 * depth + far, partner).wait_send()

    keep.wait()
    keep_aux.wait()


def gather_samples(x, aux, count):
    return pl.pallas_call(
        functools.partial(gather_kernel, count // 2),
        out_shape=(
            jax.ShapeDtypeStruct((count,) + x.shape, x.dtype),
            jax.ShapeDtypeStruct((count,) + aux.shape, aux.dtype),
        ),
        in_specs=[ANY, ANY],
        out_specs=(ANY, ANY),
        scratch_shapes=[
            pltpu.SemaphoreType.DMA((2 * count,)),
            pltpu.SemaphoreType.DMA((count,)),
            pltpu.SemaphoreType.DMA((count,)),
            pltpu.SemaphoreType.DMA((count,)),
            pltpu.SemaphoreType.DMA((2,)),
        ],
        compiler_params=pltpu.CompilerParams(collective_id=0, has_side_effects=True),
        name="gather_samples",
    )(x, aux)


def spread_kernel(axis, count, split, a_ref, o_ref, send, recv, own):
    me = lax.axis_index(axis)
    greet(axis, count)
    keep = pltpu.make_async_copy(a_ref.at[me] if split else a_ref, o_ref.at[me], own)
    keep.start()
    for step in range(1, count):
        other = lax.rem(me + step, count)
        pltpu.make_async_remote_copy(
            src_ref=a_ref.at[other] if split else a_ref,
            dst_ref=o_ref.at[me],
            send_sem=send.at[step],
            recv_sem=recv.at[me],
            device_id={axis: other},
            device_id_type=MESH,
        ).start()
    for step in range(1, count):
        other = lax.rem(me + step, count)
        pltpu.make_async_remote_copy(
            src_ref=a_ref.at[other] if split else a_ref,
            dst_ref=o_ref.at[other],
            send_sem=send.at[step],
            recv_sem=recv.at[other],
            device_id={axis: other},
            device_id_type=MESH,
        ).wait()
    keep.wait()


def spread(a, axis, count, split, number):
    return pl.pallas_call(
        functools.partial(spread_kernel, axis, count, split),
        out_shape=jax.ShapeDtypeStruct(a.shape if split else (count,) + a.shape, a.dtype),
        in_specs=[VMEM],
        out_specs=VMEM,
        scratch_shapes=[
            pltpu.SemaphoreType.DMA((count,)),
            pltpu.SemaphoreType.DMA((count,)),
            pltpu.SemaphoreType.DMA,
        ],
        compiler_params=pltpu.CompilerParams(collective_id=number, has_side_effects=True),
        name="spread_" + axis + str(number),
    )(a)


def sweep(m_ref, batch, pivot):
    size, lanes = m_ref.shape[1:]
    row_at = lax.broadcasted_iota(jnp.int32, (size, lanes), 0) == pivot
    lane_at = lax.broadcasted_iota(jnp.int32, (size, lanes), 1) == pivot
    row_col = lax.broadcasted_iota(jnp.int32, (size, 1), 0) == pivot
    lane_row = lax.broadcasted_iota(jnp.int32, (1, lanes), 1) == pivot
    cross = row_at | lane_at
    rows = [m_ref[b, pl.ds(pivot, 1), :] for b in range(batch)]
    wholes = [m_ref[b] for b in range(batch)]
    heads = [jnp.sum(jnp.where(lane_row, row, 0.0), axis=1, keepdims=True) for row in rows]
    columns = [jnp.sum(jnp.where(lane_at, m, 0.0), axis=1, keepdims=True) for m in wholes]
    for b in range(batch):
        inverse = 1.0 / heads[b]
        row = jnp.where(lane_row, -inverse, rows[b] * inverse)
        column = jnp.where(row_col, -1.0, columns[b])
        m_ref[b] = jnp.where(cross, 0.0, wholes[b]) - column * row


def sweep_panel(m_ref, batch, step):
    size, lanes = m_ref.shape[1:]
    start = pl.multiple_of(step * 8, 8)
    sub = lax.broadcasted_iota(jnp.int32, (8, lanes), 0)
    lane = lax.broadcasted_iota(jnp.int32, (8, lanes), 1) - start
    inside = (lane >= 0) & (lane < 8)
    unit = jnp.where(lane == sub, 1.0, 0.0)
    panels = [m_ref[b, pl.ds(start, 8), :] for b in range(batch)]
    turned = [pltpu.roll(p, lanes - start, 1) for p in panels]
    columns = [
        [jnp.broadcast_to(p[:, j : j + 1], (8, lanes)) for j in range(8)] for p in turned
    ]
    solved = [jnp.where(inside, unit, p) for p in panels]
    for p in range(8):
        here = sub == p
        for b in range(batch):
            inverse = 1.0 / columns[b][p][p : p + 1]
            own = columns[b][p]
            line = solved[b][p : p + 1] * inverse
            solved[b] = jnp.where(here, line, solved[b] - own * line)
            for j in range(p + 1, 8):
                line = columns[b][j][p : p + 1] * inverse
                columns[b][j] = jnp.where(here, line, columns[b][j] - own * line)
    row = lax.broadcasted_iota(jnp.int32, (size, lanes), 0) - start
    col = lax.broadcasted_iota(jnp.int32, (size, lanes), 1) - start
    cross = ((row >= 0) & (row < 8)) | ((col >= 0) & (col < 8))
    for b in range(batch):
        left = jnp.where(inside, -unit, panels[b])
        right = jnp.where(inside, -solved[b], solved[b])
        m_ref[b] = jnp.where(cross, 0.0, m_ref[b]) - high_dot(left, right, ((0,), (0,)))


def solve_kernel(systems, own, x_ref, aux_ref, coef_ref, mean_ref, gram, cross, pairs, all_aux, sq, mats, rhs, diag):
    count, rows, width = x_ref.shape
    traits = coef_ref.shape[0] // own
    total = count * rows
    first = lax.axis_index("samp") * own
    fold_of = [jnp.minimum(first + i, systems - 1) // SHRINK for i in range(own)]
    folds = [fold_of[0], fold_of[own - 1]]
    for ref in (gram, cross, pairs, all_aux, sq):
        ref[...] = jnp.zeros_like(ref)
    aux_row = lax.broadcasted_iota(jnp.int32, (AUX, width), 0)
    fold_rows = (aux_row >= traits) & (aux_row < traits + FOLDS)
    picks = jnp.concatenate(
        [
            jnp.where(fold_rows & (aux_row != traits + fold), 1.0, 0.0).astype(jnp.bfloat16)
            for fold in folds
        ],
        axis=1,
    )
    row_id = lax.broadcasted_iota(jnp.int32, (AUX, rows), 0)

    def add_block(i, _):
        x = x_ref[i]
        aux = aux_ref[i]
        aux_wide = aux.astype(jnp.float32)
        keep = lax.dot_general(
            aux, picks, (((0,), (0,)), ((), ())), preferred_element_type=jnp.float32
        ).astype(jnp.bfloat16)
        weighted = jnp.concatenate([x, x], axis=1) * keep
        gram[...] += lax.dot_general(
            x, weighted, (((0,), (0,)), ((), ())), preferred_element_type=jnp.float32
        )
        all_aux[...] += jnp.dot(aux, x, preferred_element_type=jnp.float32)
        wide = x.astype(jnp.float32)
        sq[...] += jnp.sum(wide * wide, axis=0, keepdims=True)
        for j, fold in enumerate(folds):
            held = jnp.sum(jnp.where(row_id == traits + fold, aux_wide, 0.0), axis=0, keepdims=True)
            aux_train = (aux_wide * (1.0 - held)).astype(jnp.bfloat16)
            cross[j] += jnp.dot(aux_train, x, preferred_element_type=jnp.float32)
            pairs[j] += lax.dot_general(
                aux_train, aux, (((1,), (1,)), ((), ())), preferred_element_type=jnp.float32
            )
        return 0

    lax.fori_loop(0, count, add_block, 0)
    fold_lines = lambda a: jnp.sum(jnp.where(fold_rows, a, 0.0), axis=0, keepdims=True)
    mean = fold_lines(all_aux[...]) / total
    scale = lax.rsqrt(sq[...] / total - mean * mean + EPS)
    mean_ref[...] = jnp.broadcast_to(mean, mean_ref.shape)
    pair_row = lax.broadcasted_iota(jnp.int32, (AUX, AUX), 0)
    pair_col = lax.broadcasted_iota(jnp.int32, (AUX, AUX), 1)
    pair_fold = (pair_col >= traits) & (pair_col < traits + FOLDS)
    eye = lax.broadcasted_iota(jnp.int32, (width, width), 0) == lax.broadcasted_iota(
        jnp.int32, (width, width), 1
    )
    column_of = lambda line: jnp.sum(jnp.where(eye, line, 0.0), axis=1, keepdims=True)
    mean_col, scale_col = column_of(mean), column_of(scale)
    for j in range(2):
        sums = fold_lines(cross[j])
        pair = pairs[j]
        kept = jnp.sum(jnp.where(pair_fold & (pair_row == pair_col), pair, 0.0))
        trait_sums = jnp.sum(jnp.where(pair_fold, pair, 0.0), axis=1, keepdims=True)[:traits]
        half = slice(j * width, (j + 1) * width)
        gram[:, half] = scale_col * scale * (
            gram[:, half] - mean_col * sums - column_of(sums) * mean + kept * (mean_col * mean)
        )
        cross[j, :traits] = scale * (cross[j, :traits] - trait_sums * mean)
    for i in range(own):
        shrink = jnp.minimum(first + i, systems - 1) - fold_of[i] * SHRINK
        penalty = jnp.float32(RATIOS[0] * width)
        for l in range(1, SHRINK):
            penalty = jnp.where(shrink == l, jnp.float32(RATIOS[l] * width), penalty)
        late = fold_of[i] != folds[0]
        mats[i] = jnp.where(late, gram[:, width:], gram[:, :width]) + jnp.where(eye, penalty, 0.0)
        rhs[i] = jnp.where(late, cross[1, :traits], cross[0, :traits])
    steps = width // PANEL
    for j in range(steps):
        here = slice(j * PANEL, (j + 1) * PANEL)
        rest = slice((j + 1) * PANEL, width)
        at = diag.at[j]
        for i in range(own):
            at[i] = mats[i, here, here]

        def one(pivot, _):
            sweep_panel(at, own, pivot)
            return 0

        lax.fori_loop(0, PANEL // 8, one, 0)
        for i in range(own):
            right = -high_dot(rhs[i, :, here], at[i], ((1,), (0,)))
            rhs[i, :, here] = right
            if j + 1 < steps:
                tail = mats[i, here, rest]
                solved = high_dot(at[i], tail, ((1,), (0,)))
                mats[i, rest, rest] += high_dot(tail, solved, ((0,), (0,)))
                rhs[i, :, rest] -= high_dot(right, tail, ((1,), (0,)))
    for j in range(steps - 2, -1, -1):
        here = slice(j * PANEL, (j + 1) * PANEL)
        rest = slice((j + 1) * PANEL, width)
        for i in range(own):
            back = high_dot(rhs[i, :, rest], mats[i, here, rest], ((1,), (1,)))
            rhs[i, :, here] += high_dot(back, diag[j, i], ((1,), (0,)))
    for i in range(own):
        coef_ref[i * traits : (i + 1) * traits] = (rhs[i] * scale).astype(jnp.bfloat16)


def solve_level0(x_all, aux_all, traits):
    count, rows, width = x_all.shape
    systems = FOLDS * SHRINK
    own = -(-systems // count)
    f32 = jnp.float32
    return pl.pallas_call(
        functools.partial(solve_kernel, systems, own),
        out_shape=(
            jax.ShapeDtypeStruct((own * traits, width), jnp.bfloat16),
            jax.ShapeDtypeStruct((8, width), f32),
        ),
        in_specs=[VMEM, VMEM],
        out_specs=(VMEM, VMEM),
        scratch_shapes=[
            pltpu.VMEM((width, 2 * width), f32),
            pltpu.VMEM((2, AUX, width), f32),
            pltpu.VMEM((2, AUX, AUX), f32),
            pltpu.VMEM((AUX, width), f32),
            pltpu.VMEM((1, width), f32),
            pltpu.VMEM((own, width, width), f32),
            pltpu.VMEM((own, traits, width), f32),
            pltpu.VMEM((width // PANEL, own, PANEL, PANEL), f32),
        ],
        compiler_params=pltpu.CompilerParams(vmem_limit_bytes=LIMIT),
        name="solve_level0",
    )(x_all, aux_all)


def predict_kernel(coef_ref, mean_ref, x_ref, folds_ref, o_ref):
    parts, _, group, _ = o_ref.shape
    traits = parts * group
    per_fold = SHRINK * traits
    coef = coef_ref[: FOLDS * per_fold]
    raw = lax.dot_general(
        coef, x_ref[...], (((1,), (1,)), ((), ())), preferred_element_type=jnp.float32
    )
    shift = jnp.sum(coef.astype(jnp.float32) * mean_ref[:1], axis=1, keepdims=True)
    raw = raw - shift
    folds = folds_ref[...]
    out = jnp.zeros((per_fold, raw.shape[1]), jnp.float32)
    for k in range(FOLDS):
        out = jnp.where(folds == k, raw[k * per_fold : (k + 1) * per_fold], out)
    for g in range(parts):
        for l in range(SHRINK):
            o_ref[g, l] = out[l * traits + g * group : l * traits + (g + 1) * group]


def moments_kernel(p_ref, traits_ref, folds_ref, f_ref, e_ref):
    blocks, shrinks, group, rows = p_ref.shape
    preds = blocks * shrinks
    f_ref[...] = jnp.zeros_like(f_ref)
    for t in range(group):
        base = t * ROWS1
        for b in range(blocks):
            for l in range(shrinks):
                at = base + b * shrinks + l
                f_ref[at : at + 1] = p_ref[b, l, t : t + 1]
        f_ref[base + preds : base + preds + 1] = traits_ref[t : t + 1]
        f_ref[base + preds + 1 : base + preds + 2] = jnp.ones((1, rows), jnp.float32)
    f = f_ref[...]
    size = group * ROWS1
    folds = folds_ref[...]
    lane = lax.broadcasted_iota(jnp.int32, (ROWS1, size), 1)
    for k in range(FOLDS):
        full = high_dot(jnp.where(folds == k, f, 0.0), f, ((1,), (1,)))
        packed = jnp.zeros((ROWS1, size), jnp.float32)
        for t in range(group):
            inside = (lane >= t * ROWS1) & (lane < (t + 1) * ROWS1)
            packed = jnp.where(inside, full[t * ROWS1 : (t + 1) * ROWS1], packed)
        e_ref[k * ROWS1 : (k + 1) * ROWS1] = packed


def blend_kernel(total, e_ref, f_ref, p_ref, folds_ref, level_ref, blend_ref, mats):
    blocks, shrinks, group, rows = p_ref.shape
    preds = blocks * shrinks
    summed = jnp.sum(e_ref[...], axis=0)
    shape = (ROWS1, ROWS1)
    row = lax.broadcasted_iota(jnp.int32, shape, 0)
    col = lax.broadcasted_iota(jnp.int32, shape, 1)
    col_in = lax.broadcasted_iota(jnp.int32, (ROWS1, 1), 0) < preds
    row_in = lax.broadcasted_iota(jnp.int32, (1, ROWS1), 1) < preds
    one_lane = lax.broadcasted_iota(jnp.int32, (1, ROWS1), 1) == preds + 1
    ridge = jnp.where((row == col) & (row < preds), total / 4.0, 0.0)
    own = [
        [
            summed[k * ROWS1 : (k + 1) * ROWS1, t * ROWS1 : (t + 1) * ROWS1]
            for k in range(FOLDS)
        ]
        for t in range(group)
    ]
    means, scales = [], []
    for t in range(group):
        full = own[t][0]
        for k in range(1, FOLDS):
            full = full + own[t][k]
        mean_row = jnp.where(row_in, full[preds + 1 : preds + 2] / total, 0.0)
        mean_col = jnp.where(col_in, full[:, preds + 1 : preds + 2] / total, 0.0)
        square = jnp.where(row == col, full, 0.0) / total
        sq_row = jnp.sum(square, axis=0, keepdims=True)
        sq_col = jnp.sum(square, axis=1, keepdims=True)
        scale_row = jnp.where(row_in, lax.rsqrt(sq_row - mean_row * mean_row + EPS), 1.0)
        scale_col = jnp.where(col_in, lax.rsqrt(sq_col - mean_col * mean_col + EPS), 1.0)
        means.append((mean_row, mean_col))
        scales.append((scale_row, scale_col))
        for k in range(FOLDS):
            train = full - own[t][k]
            sums_row = train[preds + 1 : preds + 2]
            sums_col = train[:, preds + 1 : preds + 2]
            kept = train[preds + 1 : preds + 2, preds + 1 : preds + 2]
            centered = (
                train - mean_col * sums_row - sums_col * mean_row + kept * (mean_col * mean_row)
            )
            mats[t * FOLDS + k] = scale_col * scale_row * centered + ridge
    for b in range(blocks):
        for l in range(shrinks):
            at = b * shrinks + l
            means_at = jnp.concatenate([means[t][1][at : at + 1] for t in range(group)], axis=0)
            scales_at = jnp.concatenate([scales[t][1][at : at + 1] for t in range(group)], axis=0)
            level_ref[b, l] = (p_ref[b, l] - means_at) * scales_at

    def one(pivot, _):
        sweep(mats, group * FOLDS, pivot)
        return 0

    lax.fori_loop(0, preds, one, 0)
    folds = folds_ref[...]
    for t in range(group):
        mean_row, scale_row = means[t][0], scales[t][0]
        lines = []
        first = jnp.zeros((1, 1), jnp.float32)
        second = jnp.zeros((1, 1), jnp.float32)
        for k in range(FOLDS):
            line = jnp.where(row_in, mats[t * FOLDS + k, preds : preds + 1, :] * scale_row, 0.0)
            offset = jnp.sum(line * mean_row, axis=1, keepdims=True)
            line = jnp.where(one_lane, -offset, line)
            lines.append(line)
            product = jnp.sum(own[t][k] * line, axis=1, keepdims=True)
            line_col = jnp.sum(jnp.where(row == col, line, 0.0), axis=1, keepdims=True)
            first = first + product[preds + 1 : preds + 2]
            second = second + jnp.sum(product * line_col, axis=0, keepdims=True)
        lines.append(jnp.zeros((8 - FOLDS, ROWS1), jnp.float32))
        every = high_dot(
            jnp.concatenate(lines, axis=0),
            f_ref[t * ROWS1 : (t + 1) * ROWS1],
            ((1,), (0,)),
        )
        p = jnp.zeros((1, rows), jnp.float32)
        for k in range(FOLDS):
            p = jnp.where(folds == k, every[k : k + 1], p)
        mean = first / total
        spread_of = second / total - mean * mean
        blend_ref[t : t + 1] = (p - mean) * lax.rsqrt(spread_of + EPS)


def plain(kernel, out_shape, name, *args, scratch=()):
    return pl.pallas_call(
        kernel,
        out_shape=out_shape,
        in_specs=[VMEM] * len(args),
        out_specs=jax.tree.map(lambda _: VMEM, out_shape),
        scratch_shapes=list(scratch),
        compiler_params=pltpu.CompilerParams(vmem_limit_bytes=LIMIT),
        name=name,
    )(*args)


def fast(samp, blk, dosages, traits, folds):
    rows, width = dosages.shape
    count_traits = traits.shape[0]
    group = count_traits // blk
    f32 = jnp.float32
    fold_ids = jnp.arange(AUX - count_traits, dtype=jnp.int32)
    one_hot = (folds[None, :] == fold_ids[:, None]).astype(jnp.bfloat16)
    aux = jnp.concatenate([traits, one_hot], axis=0)
    folds_row = folds[None, :]
    own_traits = lax.dynamic_slice_in_dim(
        traits, lax.axis_index("blk") * group, group, 0
    ).astype(f32)
    x_all, aux_all = gather_samples(dosages, aux, samp)
    coef, mean = solve_level0(x_all, aux_all, count_traits)
    coef_all = spread(coef, "samp", samp, False, 1).reshape(-1, width)
    shape = jax.ShapeDtypeStruct((blk, SHRINK, group, rows), f32)
    pred = plain(predict_kernel, shape, "predict", coef_all, mean, dosages, folds_row)
    pred = spread(pred, "blk", blk, True, 2)
    size = group * ROWS1
    stacked, moments = plain(
        moments_kernel,
        (jax.ShapeDtypeStruct((size, rows), f32), jax.ShapeDtypeStruct((FOLDS * ROWS1, size), f32)),
        "moments",
        pred,
        own_traits,
        folds_row,
    )
    moments = spread(moments, "samp", samp, False, 3)
    level0, blend = plain(
        functools.partial(blend_kernel, float(samp * rows)),
        (shape, jax.ShapeDtypeStruct((group, rows), f32)),
        "blend",
        moments,
        stacked,
        pred,
        folds_row,
        scratch=[pltpu.VMEM((group * FOLDS, ROWS1, ROWS1), f32)],
    )
    return level0, blend


def solution(mesh):
    in_specs = (P("samp", "blk"), P(None, "samp"), P("samp"))
    out_specs = (P(None, None, "blk", "samp"), P("blk", "samp"))
    samp, blk = mesh.shape["samp"], mesh.shape["blk"]
    body = functools.partial(fast, samp, blk) if samp == 8 else shards
    return jax.shard_map(body, mesh=mesh, in_specs=in_specs, out_specs=out_specs, check_vma=False)
```

```python
import functools

import jax
import jax.numpy as jnp
from jax import lax
from jax.experimental import pallas as pl
from jax.experimental.pallas import tpu as pltpu
from jax.sharding import PartitionSpec as P

FOLDS = 5
SHRINK = 5


RATIOS = (99.0, 3.0, 1.0, 1.0 / 3.0, 1.0 / 99.0)
EPS = 1e-05
HIGH = lax.Precision.HIGHEST


def solve_batch(systems, right_sides):
    factors = jnp.linalg.cholesky(systems)

    def solve_single(factor, right_side):
        return jax.scipy.linalg.cho_solve((factor, True), right_side)

    return jax.vmap(solve_single)(factors, right_sides)


def shards(dosages, traits, folds):
    rows, width = dosages.shape
    traits_count = traits.shape[0]
    fold_ids = jnp.arange(FOLDS, dtype=jnp.int32)
    masks = (folds[None, :] == fold_ids[:, None]).astype(jnp.float32)
    mask_half = masks.astype(jnp.bfloat16)
    traits_wide = traits.astype(jnp.float32)
    grams = []
    crosses = []
    for fold in range(FOLDS):
        weighted = dosages * mask_half[fold][:, None]
        grams.append(jnp.einsum("ri,rj->ij", dosages, weighted, preferred_element_type=jnp.float32))
        crosses.append(
            jnp.dot(traits * mask_half[fold][None, :], dosages, preferred_element_type=jnp.float32)
        )
    gram = jnp.stack(grams)
    cross = jnp.stack(crosses)
    sums = jnp.dot(mask_half, dosages, preferred_element_type=jnp.float32)
    counts = jnp.sum(masks, axis=1)
    trait_sums = jnp.einsum("ks,ts->kt", masks, traits_wide, precision=HIGH)
    gram, sums, cross, counts, trait_sums = lax.psum(
        (gram, sums, cross, counts, trait_sums), "samp"
    )
    total = jnp.sum(counts)
    mean = jnp.sum(sums, axis=0) / total
    gram_total = jnp.sum(gram, axis=0)
    variance = jnp.diagonal(gram_total) / total - mean * mean
    scale = lax.rsqrt(variance + EPS)
    sums_total = jnp.sum(sums, axis=0)
    cross_total = jnp.sum(cross, axis=0)
    trait_total = jnp.sum(trait_sums, axis=0)
    ratios = jnp.array(RATIOS, dtype=jnp.float32)
    identity = jnp.eye(width, dtype=jnp.float32)

    def train_system(fold):
        train_gram = gram_total - lax.dynamic_index_in_dim(gram, fold, 0, keepdims=False)
        train_sums = sums_total - lax.dynamic_index_in_dim(sums, fold, 0, keepdims=False)
        train_count = total - lax.dynamic_index_in_dim(counts, fold, 0, keepdims=False)
        train_cross = cross_total - lax.dynamic_index_in_dim(cross, fold, 0, keepdims=False)
        train_traits = trait_total - lax.dynamic_index_in_dim(trait_sums, fold, 0, keepdims=False)
        centered = (
            train_gram
            - mean[:, None] * train_sums[None, :]
            - train_sums[:, None] * mean[None, :]
            + train_count * mean[:, None] * mean[None, :]
        )
        system = scale[:, None] * centered * scale[None, :]
        target = scale[:, None] * (train_cross.T - mean[:, None] * train_traits[None, :])
        return (system, target)

    systems_count = FOLDS * SHRINK
    per_device = -(-systems_count // lax.axis_size("samp"))
    first = lax.axis_index("samp") * per_device

    def solve_own(offset):
        which = jnp.minimum(first + offset, systems_count - 1)
        fold = which // SHRINK
        shrink = which - fold * SHRINK
        system, target = train_system(fold)
        penalty = jnp.sum(
            jnp.where(jnp.arange(SHRINK, dtype=jnp.int32) == shrink, ratios * width, 0.0)
        )
        beta = solve_batch((system + penalty * identity)[None], target[None])[0]
        return (scale[:, None] * beta).astype(jnp.bfloat16)

    owned = lax.map(solve_own, jnp.arange(per_device, dtype=jnp.int32))
    collected = lax.all_gather(owned, "samp", axis=0, tiled=True)
    coef = collected[:systems_count].reshape(FOLDS, SHRINK, width, traits_count)
    coef_flat = coef.transpose(2, 0, 1, 3).reshape(width, FOLDS * SHRINK * traits_count)
    shift = jnp.einsum("v,klvt->klt", mean, coef.astype(jnp.float32), precision=HIGH)
    raw = jnp.einsum("vc,rv->cr", coef_flat, dosages, preferred_element_type=jnp.float32)
    outcome = raw.reshape(FOLDS, SHRINK, traits_count, rows) - shift[..., None]
    level_pred = jnp.einsum("kltr,kr->ltr", outcome, masks, precision=HIGH)
    group = traits_count // lax.axis_size("blk")
    start = lax.axis_index("blk") * group
    own_traits = lax.dynamic_slice_in_dim(traits_wide, start, group, 0)
    own_sums = lax.dynamic_slice_in_dim(trait_sums, start, group, 1)
    arrived = lax.all_to_all(level_pred[None], "blk", split_axis=2, concat_axis=0, tiled=True)
    count_pred = arrived.shape[0] * arrived.shape[1]
    flat = arrived.reshape(count_pred, group, rows)
    raw_grams = jnp.einsum("ks,ats,bts->ktab", masks, flat, flat, precision=HIGH)
    raw_cross = jnp.einsum("ks,ats,ts->kta", masks, flat, own_traits, precision=HIGH)
    raw_sums = jnp.einsum("ks,ats->kta", masks, flat, precision=HIGH)
    raw_grams, raw_cross, raw_sums = lax.psum((raw_grams, raw_cross, raw_sums), "samp")
    pred_mean = jnp.sum(raw_sums, axis=0) / total
    pred_sq = jnp.diagonal(jnp.sum(raw_grams, axis=0), axis1=1, axis2=2)
    pred_scale = lax.rsqrt(pred_sq / total - pred_mean * pred_mean + EPS)
    standard = (flat - pred_mean.T[:, :, None]) * pred_scale.T[:, :, None]
    outer_scale = pred_scale[None, :, :, None] * pred_scale[None, :, None, :]
    fold_grams = outer_scale * (
        raw_grams
        - pred_mean[None, :, :, None] * raw_sums[:, :, None, :]
        - raw_sums[:, :, :, None] * pred_mean[None, :, None, :]
        + counts[:, None, None, None] * pred_mean[None, :, :, None] * pred_mean[None, :, None, :]
    )
    fold_cross = pred_scale[None] * (raw_cross - pred_mean[None] * own_sums[:, :, None])
    level0 = standard.reshape(arrived.shape)
    train_grams = jnp.sum(fold_grams, axis=0)[None] - fold_grams
    train_cross = jnp.sum(fold_cross, axis=0)[None] - fold_cross
    shrunk = train_grams + total / 4.0 * jnp.eye(count_pred, dtype=jnp.float32)
    weights = solve_batch(
        shrunk.reshape(-1, count_pred, count_pred), train_cross.reshape(-1, count_pred)
    )
    weights = weights.reshape(FOLDS, group, count_pred)
    every_fold = jnp.einsum("ats,kta->kts", standard, weights, precision=HIGH)
    blended = jnp.einsum("kts,ks->ts", every_fold, masks, precision=HIGH)
    blend_sum, blend_sq = lax.psum(
        (jnp.sum(blended, axis=-1), jnp.sum(blended * blended, axis=-1)), "samp"
    )
    blend_mean = blend_sum / total
    blend_var = blend_sq / total - blend_mean * blend_mean
    blend = (blended - blend_mean[:, None]) * lax.rsqrt(blend_var + EPS)[:, None]
    return (level0, blend)


MESH = pl.DeviceIdType.MESH
AUX = 32
ROWS1 = 24
PANEL = 128
LIMIT = 48 * 1024 * 1024
VMEM = pl.BlockSpec(memory_space=pltpu.VMEM)
ANY = pl.BlockSpec(memory_space=pl.ANY)


def high_dot(a, b, dims):
    return lax.dot_general(
        a, b, (dims, ((), ())), precision=HIGH, preferred_element_type=jnp.float32
    )


def greet(axis, count):
    barrier = pltpu.get_barrier_semaphore()
    me = lax.axis_index(axis)
    for step in range(1, count):
        pl.semaphore_signal(
            barrier, inc=1, device_id={axis: lax.rem(me + step, count)}, device_id_type=MESH
        )
    pl.semaphore_wait(barrier, count - 1)


def ranked(z, depth, rank):
    near = jnp.minimum(z, depth - 1 - z)
    both = jnp.where(lax.rem(rank, 2) == 1, z - (rank + 1) // 2, z + rank // 2)
    one = jnp.where(z < depth - 1 - z, z + rank - near, z - rank + near)
    return jnp.where(rank <= 2 * near, both, one)


def gram_kernel(
    depth, own_systems, traits, x_ref, aux_ref,
    gram, cross, pairs, all_aux, sq,
    xs, auxs, send_up, send_down, send_pair, recv, asend, arecv, own,
):
    me = lax.axis_index("samp")
    z, x = me // 2, lax.rem(me, 2)
    partner = z * 2 + 1 - x
    count = 2 * depth
    keep = pltpu.make_async_copy(x_ref, xs.at[me], own.at[0])
    keep.start()
    keep_aux = pltpu.make_async_copy(aux_ref, auxs.at[me], own.at[1])
    keep_aux.start()
    greet("samp", count)

    def x_copy(slot, sem, target):
        return pltpu.make_async_remote_copy(
            src_ref=xs.at[slot],
            dst_ref=xs.at[slot],
            send_sem=sem,
            recv_sem=recv.at[slot],
            device_id={"samp": target},
            device_id_type=MESH,
        )

    def aux_copy(step, slot):
        other = lax.rem(me + step, count)
        return pltpu.make_async_remote_copy(
            src_ref=auxs.at[slot],
            dst_ref=auxs.at[slot],
            send_sem=asend.at[step],
            recv_sem=arecv.at[slot],
            device_id={"samp": other},
            device_id_type=MESH,
        )

    keep.wait()
    keep_aux.wait()
    _, width = gram.shape
    width = width // 2
    rows = xs.shape[1]
    folds = owned_folds(own_systems, FOLDS * SHRINK)
    aux_row = lax.broadcasted_iota(jnp.int32, (AUX, width), 0)
    fold_rows = (aux_row >= traits) & (aux_row < traits + FOLDS)
    picks = jnp.concatenate(
        [
            jnp.where(fold_rows & (aux_row != traits + fold), 1.0, 0.0).astype(jnp.bfloat16)
            for fold in folds
        ],
        axis=1,
    )
    row_id = lax.broadcasted_iota(jnp.int32, (AUX, rows), 0)

    def forward(rank, layer, slot):
        @pl.when((layer <= z) & (z + 1 < depth))
        def _():
            x_copy(slot, send_up.at[rank], me + 2).start()

        @pl.when((layer >= z) & (z >= 1))
        def _():
            x_copy(slot, send_down.at[rank], me - 2).start()

        x_copy(slot, send_pair.at[rank], partner).start()

    forward(0, z, me)
    for step in range(1, count):
        aux_copy(step, me).start()
    for ref in (gram, cross, pairs, all_aux, sq):
        ref[...] = jnp.zeros_like(ref)

    def add_block(i, _):
        body = i < 2 * depth - 2
        is_column = (i < 2) | (body & (lax.rem(i, 2) == 0))
        column_rank = jnp.where(i < 2, i, i // 2 + 1)
        pair_rank = jnp.where(body, (i - 3) // 2, i - depth)
        rank = jnp.where(is_column, column_rank, pair_rank)
        layer = ranked(z, depth, rank)
        slot = layer * 2 + jnp.where(is_column, x, 1 - x)

        @pl.when(i > 0)
        def _():
            x_copy(slot, send_pair.at[0], partner).wait_recv()

            @pl.when(is_column)
            def _():
                forward(rank, layer, slot)

            aux_copy(1, slot).wait_recv()

        block = xs[slot]
        aux = auxs[slot]
        aux_wide = aux.astype(jnp.float32)
        keep = lax.dot_general(
            aux, picks, (((0,), (0,)), ((), ())), preferred_element_type=jnp.float32
        ).astype(jnp.bfloat16)
        weighted = jnp.concatenate([block, block], axis=1) * keep
        gram[...] += lax.dot_general(
            block, weighted, (((0,), (0,)), ((), ())), preferred_element_type=jnp.float32
        )
        all_aux[...] += jnp.dot(aux, block, preferred_element_type=jnp.float32)
        wide = block.astype(jnp.float32)
        sq[...] += jnp.sum(wide * wide, axis=0, keepdims=True)
        for j, fold in enumerate(folds):
            held = jnp.sum(jnp.where(row_id == traits + fold, aux_wide, 0.0), axis=0, keepdims=True)
            aux_train = (aux_wide * (1.0 - held)).astype(jnp.bfloat16)
            cross[j] += jnp.dot(aux_train, block, preferred_element_type=jnp.float32)
            pairs[j] += lax.dot_general(
                aux_train, aux, (((1,), (1,)), ((), ())), preferred_element_type=jnp.float32
            )
        return 0

    lax.fori_loop(0, count, add_block, 0)
    for step in range(1, count):
        aux_copy(step, me).wait_send()
    for rank in range(depth):
        layer = ranked(z, depth, jnp.int32(rank))
        slot = layer * 2 + x

        @pl.when((layer <= z) & (z + 1 < depth))
        def _():
            x_copy(slot, send_up.at[rank], partner).wait_send()

        @pl.when((layer >= z) & (z >= 1))
        def _():
            x_copy(slot, send_down.at[rank], partner).wait_send()

        x_copy(slot, send_pair.at[rank], partner).wait_send()


def owned_systems(count):
    return -(-FOLDS * SHRINK // count)


def owned_folds(own, systems):
    first = lax.axis_index("samp") * own
    return [jnp.minimum(first + i, systems - 1) // SHRINK for i in (0, own - 1)]


def gather_grams(x, aux, count, traits):
    rows, width = x.shape
    f32 = jnp.float32
    depth = count // 2
    return pl.pallas_call(
        functools.partial(gram_kernel, depth, owned_systems(count), traits),
        out_shape=(
            jax.ShapeDtypeStruct((width, 2 * width), f32),
            jax.ShapeDtypeStruct((2, AUX, width), f32),
            jax.ShapeDtypeStruct((2, AUX, AUX), f32),
            jax.ShapeDtypeStruct((AUX, width), f32),
            jax.ShapeDtypeStruct((1, width), f32),
        ),
        in_specs=[ANY, ANY],
        out_specs=(VMEM,) * 5,
        scratch_shapes=[
            pltpu.VMEM((count, rows, width), x.dtype),
            pltpu.VMEM((count, AUX, rows), aux.dtype),
            pltpu.SemaphoreType.DMA((depth,)),
            pltpu.SemaphoreType.DMA((depth,)),
            pltpu.SemaphoreType.DMA((depth,)),
            pltpu.SemaphoreType.DMA((count,)),
            pltpu.SemaphoreType.DMA((count,)),
            pltpu.SemaphoreType.DMA((count,)),
            pltpu.SemaphoreType.DMA((2,)),
        ],
        compiler_params=pltpu.CompilerParams(
            collective_id=0, has_side_effects=True, vmem_limit_bytes=LIMIT
        ),
        name="gather_grams",
    )(x, aux)


def sweep(m_ref, batch, pivot):
    size, lanes = m_ref.shape[1:]
    row_at = lax.broadcasted_iota(jnp.int32, (size, lanes), 0) == pivot
    lane_at = lax.broadcasted_iota(jnp.int32, (size, lanes), 1) == pivot
    row_col = lax.broadcasted_iota(jnp.int32, (size, 1), 0) == pivot
    lane_row = lax.broadcasted_iota(jnp.int32, (1, lanes), 1) == pivot
    cross = row_at | lane_at
    rows = [m_ref[b, pl.ds(pivot, 1), :] for b in range(batch)]
    wholes = [m_ref[b] for b in range(batch)]
    heads = [jnp.sum(jnp.where(lane_row, row, 0.0), axis=1, keepdims=True) for row in rows]
    columns = [jnp.sum(jnp.where(lane_at, m, 0.0), axis=1, keepdims=True) for m in wholes]
    for b in range(batch):
        inverse = 1.0 / heads[b]
        row = jnp.where(lane_row, -inverse, rows[b] * inverse)
        column = jnp.where(row_col, -1.0, columns[b])
        m_ref[b] = jnp.where(cross, 0.0, wholes[b]) - column * row


def sweep_panel(m_ref, batch, step):
    size, lanes = m_ref.shape[1:]
    start = pl.multiple_of(step * 8, 8)
    sub = lax.broadcasted_iota(jnp.int32, (8, lanes), 0)
    lane = lax.broadcasted_iota(jnp.int32, (8, lanes), 1) - start
    inside = (lane >= 0) & (lane < 8)
    unit = jnp.where(lane == sub, 1.0, 0.0)
    panels = [m_ref[b, pl.ds(start, 8), :] for b in range(batch)]
    turned = [pltpu.roll(p, lanes - start, 1) for p in panels]
    columns = [
        [jnp.broadcast_to(p[:, j : j + 1], (8, lanes)) for j in range(8)] for p in turned
    ]
    solved = [jnp.where(inside, unit, p) for p in panels]
    for p in range(8):
        here = sub == p
        for b in range(batch):
            inverse = 1.0 / columns[b][p][p : p + 1]
            own = columns[b][p]
            line = solved[b][p : p + 1] * inverse
            solved[b] = jnp.where(here, line, solved[b] - own * line)
            for j in range(p + 1, 8):
                line = columns[b][j][p : p + 1] * inverse
                columns[b][j] = jnp.where(here, line, columns[b][j] - own * line)
    row = lax.broadcasted_iota(jnp.int32, (size, lanes), 0) - start
    col = lax.broadcasted_iota(jnp.int32, (size, lanes), 1) - start
    cross = ((row >= 0) & (row < 8)) | ((col >= 0) & (col < 8))
    for b in range(batch):
        left = jnp.where(inside, -unit, panels[b])
        right = jnp.where(inside, -solved[b], solved[b])
        m_ref[b] = jnp.where(cross, 0.0, m_ref[b]) - high_dot(left, right, ((0,), (0,)))


def solve_kernel(
    systems, own, total, gram, cross, pairs, all_aux, sq, coef_ref, mean_ref, mats, rhs, lines, diag
):
    width = gram.shape[0]
    traits = coef_ref.shape[0] // own
    first = lax.axis_index("samp") * own
    fold_of = [jnp.minimum(first + i, systems - 1) // SHRINK for i in range(own)]
    folds = owned_folds(own, systems)
    aux_row = lax.broadcasted_iota(jnp.int32, (AUX, width), 0)
    fold_rows = (aux_row >= traits) & (aux_row < traits + FOLDS)
    fold_lines = lambda a: jnp.sum(jnp.where(fold_rows, a, 0.0), axis=0, keepdims=True)
    mean = fold_lines(all_aux[...]) / total
    scale = lax.rsqrt(sq[...] / total - mean * mean + EPS)
    mean_ref[...] = jnp.broadcast_to(mean, mean_ref.shape)
    pair_row = lax.broadcasted_iota(jnp.int32, (AUX, AUX), 0)
    pair_col = lax.broadcasted_iota(jnp.int32, (AUX, AUX), 1)
    pair_fold = (pair_col >= traits) & (pair_col < traits + FOLDS)
    eye = lax.broadcasted_iota(jnp.int32, (width, width), 0) == lax.broadcasted_iota(
        jnp.int32, (width, width), 1
    )
    column_of = lambda line: jnp.sum(jnp.where(eye, line, 0.0), axis=1, keepdims=True)
    mean_col, scale_col = column_of(mean), column_of(scale)
    for j in range(2):
        sums = fold_lines(cross[j])
        pair = pairs[j]
        kept = jnp.sum(jnp.where(pair_fold & (pair_row == pair_col), pair, 0.0))
        trait_sums = jnp.sum(jnp.where(pair_fold, pair, 0.0), axis=1, keepdims=True)[:traits]
        half = slice(j * width, (j + 1) * width)
        mats[j] = scale_col * scale * (
            gram[:, half] - mean_col * sums - column_of(sums) * mean + kept * (mean_col * mean)
        )
        lines[j] = scale * (cross[j, :traits] - trait_sums * mean)
    for i in range(own - 1, -1, -1):
        shrink = jnp.minimum(first + i, systems - 1) - fold_of[i] * SHRINK
        penalty = jnp.float32(RATIOS[0] * width)
        for l in range(1, SHRINK):
            penalty = jnp.where(shrink == l, jnp.float32(RATIOS[l] * width), penalty)
        late = jnp.where(fold_of[i] != folds[0], 1, 0)
        mats[i + 2] = mats[late] + jnp.where(eye, penalty, 0.0)
        rhs[i] = lines[late]
    steps = width // PANEL
    for j in range(steps):
        here = slice(j * PANEL, (j + 1) * PANEL)
        rest = slice((j + 1) * PANEL, width)
        at = diag.at[j]
        for i in range(own):
            at[i] = mats[i + 2, here, here]

        def one(pivot, _):
            sweep_panel(at, own, pivot)
            return 0

        lax.fori_loop(0, PANEL // 8, one, 0)
        for i in range(own):
            right = -high_dot(rhs[i, :, here], at[i], ((1,), (0,)))
            rhs[i, :, here] = right
            if j + 1 < steps:
                tail = mats[i + 2, here, rest]
                solved = high_dot(at[i], tail, ((1,), (0,)))
                mats[i + 2, rest, rest] += high_dot(tail, solved, ((0,), (0,)))
                rhs[i, :, rest] -= high_dot(right, tail, ((1,), (0,)))
    for j in range(steps - 2, -1, -1):
        here = slice(j * PANEL, (j + 1) * PANEL)
        rest = slice((j + 1) * PANEL, width)
        for i in range(own):
            back = high_dot(rhs[i, :, rest], mats[i + 2, here, rest], ((1,), (1,)))
            rhs[i, :, here] += high_dot(back, diag[j, i], ((1,), (0,)))
    for i in range(own):
        coef_ref[i * traits : (i + 1) * traits] = (rhs[i] * scale).astype(jnp.bfloat16)


def solve_level0(sums, traits, count, rows):
    width = sums[0].shape[0]
    own = owned_systems(count)
    f32 = jnp.float32
    return plain(
        functools.partial(solve_kernel, FOLDS * SHRINK, own, count * rows),
        (
            jax.ShapeDtypeStruct((own * traits, width), jnp.bfloat16),
            jax.ShapeDtypeStruct((8, width), f32),
        ),
        "solve_level0",
        *sums,
        scratch=[
            pltpu.VMEM((own + 2, width, width), f32),
            pltpu.VMEM((own, traits, width), f32),
            pltpu.VMEM((2, traits, width), f32),
            pltpu.VMEM((width // PANEL, own, PANEL, PANEL), f32),
        ],
    )


def predict(coef, mean, x, folds, o_ref):
    parts, _, group, _ = o_ref.shape
    traits = parts * group
    per_fold = SHRINK * traits
    coef = coef[: FOLDS * per_fold]
    raw = lax.dot_general(
        coef, x, (((1,), (1,)), ((), ())), preferred_element_type=jnp.float32
    )
    shift = jnp.sum(coef.astype(jnp.float32) * mean, axis=1, keepdims=True)
    raw = raw - shift
    out = jnp.zeros((per_fold, raw.shape[1]), jnp.float32)
    for k in range(FOLDS):
        out = jnp.where(folds == k, raw[k * per_fold : (k + 1) * per_fold], out)
    for g in range(parts):
        for l in range(SHRINK):
            o_ref[g, l] = out[l * traits + g * group : l * traits + (g + 1) * group]


def level_kernel(
    depth, blk, coef_ref, mean_ref, x_ref, traits_ref, folds_ref,
    p_ref, f_ref, sum_ref,
    coefs, sent, part, arrived,
    send_line, send_pair, recv, send_blk, recv_blk, send_sum, recv_sum,
):
    count = 2 * depth
    me = lax.axis_index("samp")
    here = lax.axis_index("blk")
    z, x = me // 2, lax.rem(me, 2)
    partner = z * 2 + 1 - x
    barrier = pltpu.get_barrier_semaphore()
    for axis, size, at in (("samp", count, me), ("blk", blk, here)):
        for step in range(1, size):
            pl.semaphore_signal(
                barrier,
                inc=1,
                device_id={axis: lax.rem(at + step, size)},
                device_id_type=MESH,
            )
    coefs[me] = coef_ref[...]
    pl.semaphore_wait(barrier, count + blk - 2)

    def coef_copy(slot, sem, target):
        return pltpu.make_async_remote_copy(
            src_ref=coefs.at[slot],
            dst_ref=coefs.at[slot],
            send_sem=sem,
            recv_sem=recv.at[slot],
            device_id={"samp": target},
            device_id_type=MESH,
        )

    mate = lambda step: lax.rem(z + step, depth) * 2 + x
    for step in range(1, depth):
        coef_copy(me, send_line.at[step], mate(step)).start()
    coef_copy(me, send_pair.at[0], partner).start()
    for step in range(1, depth):
        coef_copy(mate(step), send_pair.at[0], partner).wait_recv()
        coef_copy(mate(step), send_pair.at[step], partner).start()
    for step in range(depth):
        slot = lax.rem(z + step, depth) * 2 + 1 - x
        coef_copy(slot, send_pair.at[0], partner).wait_recv()
    predict(
        coefs[...].reshape(-1, coefs.shape[2]),
        mean_ref[:1],
        x_ref[...],
        folds_ref[...],
        sent,
    )

    def pred_copy(step, slot):
        other = lax.rem(here + step, blk)
        return pltpu.make_async_remote_copy(
            src_ref=sent.at[other],
            dst_ref=p_ref.at[slot],
            send_sem=send_blk.at[step],
            recv_sem=recv_blk.at[slot],
            device_id={"blk": other},
            device_id_type=MESH,
        )

    for step in range(1, blk):
        pred_copy(step, here).start()
    p_ref[here] = sent[here]
    for step in range(1, depth):
        coef_copy(me, send_line.at[step], partner).wait_send()
    for step in range(depth):
        coef_copy(me, send_pair.at[step], partner).wait_send()
    for step in range(1, blk):
        pred_copy(step, lax.rem(here + step, blk)).wait()
    moments(p_ref, traits_ref, folds_ref, f_ref, part.at[0])
    stages = part.shape[0]
    copies = []
    for stage in range(stages):
        bit = 2**stage
        other = me + bit - 2 * bit * lax.rem(me // bit, 2)
        copy = pltpu.make_async_remote_copy(
            src_ref=part.at[stage],
            dst_ref=arrived.at[stage],
            send_sem=send_sum.at[stage],
            recv_sem=recv_sum.at[stage],
            device_id={"samp": other},
            device_id_type=MESH,
        )
        copy.start()
        copies.append(copy)
        copy.wait_recv()
        summed = part[stage] + arrived[stage]
        if stage + 1 < stages:
            part[stage + 1] = summed
        else:
            sum_ref[...] = summed
    for copy in copies:
        copy.wait_send()


def moments(p_ref, traits_ref, folds_ref, f_ref, e_ref):
    blocks, shrinks, group, rows = p_ref.shape
    preds = blocks * shrinks
    f_ref[...] = jnp.zeros_like(f_ref)
    for t in range(group):
        base = t * ROWS1
        for b in range(blocks):
            for l in range(shrinks):
                at = base + b * shrinks + l
                f_ref[at : at + 1] = p_ref[b, l, t : t + 1]
        f_ref[base + preds : base + preds + 1] = traits_ref[t : t + 1]
        f_ref[base + preds + 1 : base + preds + 2] = jnp.ones((1, rows), jnp.float32)
    f = f_ref[...]
    size = group * ROWS1
    folds = folds_ref[...]
    lane = lax.broadcasted_iota(jnp.int32, (ROWS1, size), 1)
    for k in range(FOLDS):
        full = high_dot(jnp.where(folds == k, f, 0.0), f, ((1,), (1,)))
        packed = jnp.zeros((ROWS1, size), jnp.float32)
        for t in range(group):
            inside = (lane >= t * ROWS1) & (lane < (t + 1) * ROWS1)
            packed = jnp.where(inside, full[t * ROWS1 : (t + 1) * ROWS1], packed)
        e_ref[k * ROWS1 : (k + 1) * ROWS1] = packed


def blend_kernel(total, e_ref, f_ref, p_ref, folds_ref, level_ref, blend_ref, mats):
    blocks, shrinks, group, rows = p_ref.shape
    preds = blocks * shrinks
    summed = e_ref[...]
    shape = (ROWS1, ROWS1)
    row = lax.broadcasted_iota(jnp.int32, shape, 0)
    col = lax.broadcasted_iota(jnp.int32, shape, 1)
    col_in = lax.broadcasted_iota(jnp.int32, (ROWS1, 1), 0) < preds
    row_in = lax.broadcasted_iota(jnp.int32, (1, ROWS1), 1) < preds
    one_lane = lax.broadcasted_iota(jnp.int32, (1, ROWS1), 1) == preds + 1
    ridge = jnp.where((row == col) & (row < preds), total / 4.0, 0.0)
    own = [
        [
            summed[k * ROWS1 : (k + 1) * ROWS1, t * ROWS1 : (t + 1) * ROWS1]
            for k in range(FOLDS)
        ]
        for t in range(group)
    ]
    means, scales = [], []
    for t in range(group):
        full = own[t][0]
        for k in range(1, FOLDS):
            full = full + own[t][k]
        mean_row = jnp.where(row_in, full[preds + 1 : preds + 2] / total, 0.0)
        mean_col = jnp.where(col_in, full[:, preds + 1 : preds + 2] / total, 0.0)
        square = jnp.where(row == col, full, 0.0) / total
        sq_row = jnp.sum(square, axis=0, keepdims=True)
        sq_col = jnp.sum(square, axis=1, keepdims=True)
        scale_row = jnp.where(row_in, lax.rsqrt(sq_row - mean_row * mean_row + EPS), 1.0)
        scale_col = jnp.where(col_in, lax.rsqrt(sq_col - mean_col * mean_col + EPS), 1.0)
        means.append((mean_row, mean_col))
        scales.append((scale_row, scale_col))
        for k in range(FOLDS):
            train = full - own[t][k]
            sums_row = train[preds + 1 : preds + 2]
            sums_col = train[:, preds + 1 : preds + 2]
            kept = train[preds + 1 : preds + 2, preds + 1 : preds + 2]
            centered = (
                train - mean_col * sums_row - sums_col * mean_row + kept * (mean_col * mean_row)
            )
            mats[t * FOLDS + k] = scale_col * scale_row * centered + ridge
    for b in range(blocks):
        for l in range(shrinks):
            at = b * shrinks + l
            means_at = jnp.concatenate([means[t][1][at : at + 1] for t in range(group)], axis=0)
            scales_at = jnp.concatenate([scales[t][1][at : at + 1] for t in range(group)], axis=0)
            level_ref[b, l] = (p_ref[b, l] - means_at) * scales_at

    def one(pivot, _):
        sweep(mats, group * FOLDS, pivot)
        return 0

    lax.fori_loop(0, preds, one, 0)
    folds = folds_ref[...]
    for t in range(group):
        mean_row, scale_row = means[t][0], scales[t][0]
        lines = []
        first = jnp.zeros((1, 1), jnp.float32)
        second = jnp.zeros((1, 1), jnp.float32)
        for k in range(FOLDS):
            line = jnp.where(row_in, mats[t * FOLDS + k, preds : preds + 1, :] * scale_row, 0.0)
            offset = jnp.sum(line * mean_row, axis=1, keepdims=True)
            line = jnp.where(one_lane, -offset, line)
            lines.append(line)
            product = jnp.sum(own[t][k] * line, axis=1, keepdims=True)
            line_col = jnp.sum(jnp.where(row == col, line, 0.0), axis=1, keepdims=True)
            first = first + product[preds + 1 : preds + 2]
            second = second + jnp.sum(product * line_col, axis=0, keepdims=True)
        lines.append(jnp.zeros((8 - FOLDS, ROWS1), jnp.float32))
        every = high_dot(
            jnp.concatenate(lines, axis=0),
            f_ref[t * ROWS1 : (t + 1) * ROWS1],
            ((1,), (0,)),
        )
        p = jnp.zeros((1, rows), jnp.float32)
        for k in range(FOLDS):
            p = jnp.where(folds == k, every[k : k + 1], p)
        mean = first / total
        spread_of = second / total - mean * mean
        blend_ref[t : t + 1] = (p - mean) * lax.rsqrt(spread_of + EPS)


def plain(kernel, out_shape, name, *args, scratch=()):
    return pl.pallas_call(
        kernel,
        out_shape=out_shape,
        in_specs=[VMEM] * len(args),
        out_specs=jax.tree.map(lambda _: VMEM, out_shape),
        scratch_shapes=list(scratch),
        compiler_params=pltpu.CompilerParams(vmem_limit_bytes=LIMIT),
        name=name,
    )(*args)


def fast(samp, blk, dosages, traits, folds):
    rows, width = dosages.shape
    count_traits = traits.shape[0]
    group = count_traits // blk
    f32 = jnp.float32
    fold_ids = jnp.arange(AUX - count_traits, dtype=jnp.int32)
    one_hot = (folds[None, :] == fold_ids[:, None]).astype(jnp.bfloat16)
    aux = jnp.concatenate([traits, one_hot], axis=0)
    folds_row = folds[None, :]
    own_traits = lax.dynamic_slice_in_dim(
        traits, lax.axis_index("blk") * group, group, 0
    ).astype(f32)
    sums = gather_grams(dosages, aux, samp, count_traits)
    coef, mean = solve_level0(sums, count_traits, samp, rows)
    shape = jax.ShapeDtypeStruct((blk, SHRINK, group, rows), f32)
    size = group * ROWS1
    own = owned_systems(samp) * count_traits
    depth = samp // 2
    stages = samp.bit_length() - 1
    dma = pltpu.SemaphoreType.DMA
    pred, stacked, moment_sums = pl.pallas_call(
        functools.partial(level_kernel, depth, blk),
        out_shape=(
            shape,
            jax.ShapeDtypeStruct((size, rows), f32),
            jax.ShapeDtypeStruct((FOLDS * ROWS1, size), f32),
        ),
        in_specs=[VMEM] * 5,
        out_specs=(VMEM,) * 3,
        scratch_shapes=[
            pltpu.VMEM((samp, own, width), jnp.bfloat16),
            pltpu.VMEM(shape.shape, f32),
            pltpu.VMEM((stages, FOLDS * ROWS1, size), f32),
            pltpu.VMEM((stages, FOLDS * ROWS1, size), f32),
            dma((depth,)),
            dma((depth,)),
            dma((samp,)),
            dma((blk,)),
            dma((blk,)),
            dma((stages,)),
            dma((stages,)),
        ],
        compiler_params=pltpu.CompilerParams(
            collective_id=1, has_side_effects=True, vmem_limit_bytes=LIMIT
        ),
        name="predict_level0",
    )(coef, mean, dosages, own_traits, folds_row)
    level0, blend = plain(
        functools.partial(blend_kernel, float(samp * rows)),
        (shape, jax.ShapeDtypeStruct((group, rows), f32)),
        "blend",
        moment_sums,
        stacked,
        pred,
        folds_row,
        scratch=[pltpu.VMEM((group * FOLDS, ROWS1, ROWS1), f32)],
    )
    return level0, blend


def solution(mesh):
    in_specs = (P("samp", "blk"), P(None, "samp"), P("samp"))
    out_specs = (P(None, None, "blk", "samp"), P("blk", "samp"))
    samp, blk = mesh.shape["samp"], mesh.shape["blk"]
    body = functools.partial(fast, samp, blk) if samp == 8 else shards
    return jax.shard_map(body, mesh=mesh, in_specs=in_specs, out_specs=out_specs, check_vma=False)
```

```python
import functools

import jax
import jax.numpy as jnp
from jax import lax
from jax.experimental import pallas as pl
from jax.experimental.pallas import tpu as pltpu
from jax.sharding import PartitionSpec as P

FOLDS = 5
SHRINK = 5


RATIOS = (99.0, 3.0, 1.0, 1.0 / 3.0, 1.0 / 99.0)
EPS = 1e-05
HIGH = lax.Precision.HIGHEST


def solve_batch(systems, right_sides):
    factors = jnp.linalg.cholesky(systems)

    def solve_single(factor, right_side):
        return jax.scipy.linalg.cho_solve((factor, True), right_side)

    return jax.vmap(solve_single)(factors, right_sides)


def shards(dosages, traits, folds):
    rows, width = dosages.shape
    traits_count = traits.shape[0]
    fold_ids = jnp.arange(FOLDS, dtype=jnp.int32)
    masks = (folds[None, :] == fold_ids[:, None]).astype(jnp.float32)
    mask_half = masks.astype(jnp.bfloat16)
    traits_wide = traits.astype(jnp.float32)
    grams = []
    crosses = []
    for fold in range(FOLDS):
        weighted = dosages * mask_half[fold][:, None]
        grams.append(jnp.einsum("ri,rj->ij", dosages, weighted, preferred_element_type=jnp.float32))
        crosses.append(
            jnp.dot(traits * mask_half[fold][None, :], dosages, preferred_element_type=jnp.float32)
        )
    gram = jnp.stack(grams)
    cross = jnp.stack(crosses)
    sums = jnp.dot(mask_half, dosages, preferred_element_type=jnp.float32)
    counts = jnp.sum(masks, axis=1)
    trait_sums = jnp.einsum("ks,ts->kt", masks, traits_wide, precision=HIGH)
    gram, sums, cross, counts, trait_sums = lax.psum(
        (gram, sums, cross, counts, trait_sums), "samp"
    )
    total = jnp.sum(counts)
    mean = jnp.sum(sums, axis=0) / total
    gram_total = jnp.sum(gram, axis=0)
    variance = jnp.diagonal(gram_total) / total - mean * mean
    scale = lax.rsqrt(variance + EPS)
    sums_total = jnp.sum(sums, axis=0)
    cross_total = jnp.sum(cross, axis=0)
    trait_total = jnp.sum(trait_sums, axis=0)
    ratios = jnp.array(RATIOS, dtype=jnp.float32)
    identity = jnp.eye(width, dtype=jnp.float32)

    def train_system(fold):
        train_gram = gram_total - lax.dynamic_index_in_dim(gram, fold, 0, keepdims=False)
        train_sums = sums_total - lax.dynamic_index_in_dim(sums, fold, 0, keepdims=False)
        train_count = total - lax.dynamic_index_in_dim(counts, fold, 0, keepdims=False)
        train_cross = cross_total - lax.dynamic_index_in_dim(cross, fold, 0, keepdims=False)
        train_traits = trait_total - lax.dynamic_index_in_dim(trait_sums, fold, 0, keepdims=False)
        centered = (
            train_gram
            - mean[:, None] * train_sums[None, :]
            - train_sums[:, None] * mean[None, :]
            + train_count * mean[:, None] * mean[None, :]
        )
        system = scale[:, None] * centered * scale[None, :]
        target = scale[:, None] * (train_cross.T - mean[:, None] * train_traits[None, :])
        return (system, target)

    systems_count = FOLDS * SHRINK
    per_device = -(-systems_count // lax.axis_size("samp"))
    first = lax.axis_index("samp") * per_device

    def solve_own(offset):
        which = jnp.minimum(first + offset, systems_count - 1)
        fold = which // SHRINK
        shrink = which - fold * SHRINK
        system, target = train_system(fold)
        penalty = jnp.sum(
            jnp.where(jnp.arange(SHRINK, dtype=jnp.int32) == shrink, ratios * width, 0.0)
        )
        beta = solve_batch((system + penalty * identity)[None], target[None])[0]
        return (scale[:, None] * beta).astype(jnp.bfloat16)

    owned = lax.map(solve_own, jnp.arange(per_device, dtype=jnp.int32))
    collected = lax.all_gather(owned, "samp", axis=0, tiled=True)
    coef = collected[:systems_count].reshape(FOLDS, SHRINK, width, traits_count)
    coef_flat = coef.transpose(2, 0, 1, 3).reshape(width, FOLDS * SHRINK * traits_count)
    shift = jnp.einsum("v,klvt->klt", mean, coef.astype(jnp.float32), precision=HIGH)
    raw = jnp.einsum("vc,rv->cr", coef_flat, dosages, preferred_element_type=jnp.float32)
    outcome = raw.reshape(FOLDS, SHRINK, traits_count, rows) - shift[..., None]
    level_pred = jnp.einsum("kltr,kr->ltr", outcome, masks, precision=HIGH)
    group = traits_count // lax.axis_size("blk")
    start = lax.axis_index("blk") * group
    own_traits = lax.dynamic_slice_in_dim(traits_wide, start, group, 0)
    own_sums = lax.dynamic_slice_in_dim(trait_sums, start, group, 1)
    arrived = lax.all_to_all(level_pred[None], "blk", split_axis=2, concat_axis=0, tiled=True)
    count_pred = arrived.shape[0] * arrived.shape[1]
    flat = arrived.reshape(count_pred, group, rows)
    raw_grams = jnp.einsum("ks,ats,bts->ktab", masks, flat, flat, precision=HIGH)
    raw_cross = jnp.einsum("ks,ats,ts->kta", masks, flat, own_traits, precision=HIGH)
    raw_sums = jnp.einsum("ks,ats->kta", masks, flat, precision=HIGH)
    raw_grams, raw_cross, raw_sums = lax.psum((raw_grams, raw_cross, raw_sums), "samp")
    pred_mean = jnp.sum(raw_sums, axis=0) / total
    pred_sq = jnp.diagonal(jnp.sum(raw_grams, axis=0), axis1=1, axis2=2)
    pred_scale = lax.rsqrt(pred_sq / total - pred_mean * pred_mean + EPS)
    standard = (flat - pred_mean.T[:, :, None]) * pred_scale.T[:, :, None]
    outer_scale = pred_scale[None, :, :, None] * pred_scale[None, :, None, :]
    fold_grams = outer_scale * (
        raw_grams
        - pred_mean[None, :, :, None] * raw_sums[:, :, None, :]
        - raw_sums[:, :, :, None] * pred_mean[None, :, None, :]
        + counts[:, None, None, None] * pred_mean[None, :, :, None] * pred_mean[None, :, None, :]
    )
    fold_cross = pred_scale[None] * (raw_cross - pred_mean[None] * own_sums[:, :, None])
    level0 = standard.reshape(arrived.shape)
    train_grams = jnp.sum(fold_grams, axis=0)[None] - fold_grams
    train_cross = jnp.sum(fold_cross, axis=0)[None] - fold_cross
    shrunk = train_grams + total / 4.0 * jnp.eye(count_pred, dtype=jnp.float32)
    weights = solve_batch(
        shrunk.reshape(-1, count_pred, count_pred), train_cross.reshape(-1, count_pred)
    )
    weights = weights.reshape(FOLDS, group, count_pred)
    every_fold = jnp.einsum("ats,kta->kts", standard, weights, precision=HIGH)
    blended = jnp.einsum("kts,ks->ts", every_fold, masks, precision=HIGH)
    blend_sum, blend_sq = lax.psum(
        (jnp.sum(blended, axis=-1), jnp.sum(blended * blended, axis=-1)), "samp"
    )
    blend_mean = blend_sum / total
    blend_var = blend_sq / total - blend_mean * blend_mean
    blend = (blended - blend_mean[:, None]) * lax.rsqrt(blend_var + EPS)[:, None]
    return (level0, blend)


MESH = pl.DeviceIdType.MESH
AUX = 32
ROWS1 = 24
PANEL = 128
LIMIT = 48 * 1024 * 1024
VMEM = pl.BlockSpec(memory_space=pltpu.VMEM)
ANY = pl.BlockSpec(memory_space=pl.ANY)


def high_dot(a, b, dims):
    return lax.dot_general(
        a, b, (dims, ((), ())), precision=HIGH, preferred_element_type=jnp.float32
    )


def greet(axis, count):
    barrier = pltpu.get_barrier_semaphore()
    me = lax.axis_index(axis)
    for step in range(1, count):
        pl.semaphore_signal(
            barrier, inc=1, device_id={axis: lax.rem(me + step, count)}, device_id_type=MESH
        )
    pl.semaphore_wait(barrier, count - 1)


def ranked(z, depth, rank):
    near = jnp.minimum(z, depth - 1 - z)
    both = jnp.where(lax.rem(rank, 2) == 1, z - (rank + 1) // 2, z + rank // 2)
    one = jnp.where(z < depth - 1 - z, z + rank - near, z - rank + near)
    return jnp.where(rank <= 2 * near, both, one)


def gram_kernel(
    depth, own_systems, traits, x_ref, aux_ref,
    gram, cross, pairs, all_aux, sq,
    xs, auxs, send_up, send_down, send_pair, recv, asend, arecv, own,
):
    me = lax.axis_index("samp")
    z, x = me // 2, lax.rem(me, 2)
    partner = z * 2 + 1 - x
    count = 2 * depth
    keep = pltpu.make_async_copy(x_ref, xs.at[me], own.at[0])
    keep.start()
    keep_aux = pltpu.make_async_copy(aux_ref, auxs.at[me], own.at[1])
    keep_aux.start()
    greet("samp", count)

    def x_copy(slot, sem, target):
        return pltpu.make_async_remote_copy(
            src_ref=xs.at[slot],
            dst_ref=xs.at[slot],
            send_sem=sem,
            recv_sem=recv.at[slot],
            device_id={"samp": target},
            device_id_type=MESH,
        )

    def aux_copy(step, slot):
        other = lax.rem(me + step, count)
        return pltpu.make_async_remote_copy(
            src_ref=auxs.at[slot],
            dst_ref=auxs.at[slot],
            send_sem=asend.at[step],
            recv_sem=arecv.at[slot],
            device_id={"samp": other},
            device_id_type=MESH,
        )

    keep.wait()
    keep_aux.wait()
    _, width = gram.shape
    width = width // 2
    rows = xs.shape[1]
    folds = owned_folds(own_systems, FOLDS * SHRINK)
    aux_row = lax.broadcasted_iota(jnp.int32, (AUX, width), 0)
    fold_rows = (aux_row >= traits) & (aux_row < traits + FOLDS)
    picks = jnp.concatenate(
        [
            jnp.where(fold_rows & (aux_row != traits + fold), 1.0, 0.0).astype(jnp.bfloat16)
            for fold in folds
        ],
        axis=1,
    )
    row_id = lax.broadcasted_iota(jnp.int32, (AUX, rows), 0)

    def forward(rank, layer, slot):
        @pl.when((layer <= z) & (z + 1 < depth))
        def _():
            x_copy(slot, send_up.at[rank], me + 2).start()

        @pl.when((layer >= z) & (z >= 1))
        def _():
            x_copy(slot, send_down.at[rank], me - 2).start()

        x_copy(slot, send_pair.at[rank], partner).start()

    forward(0, z, me)
    for step in range(1, count):
        aux_copy(step, me).start()
    for ref in (gram, cross, pairs, all_aux, sq):
        ref[...] = jnp.zeros_like(ref)

    def add_block(i, _):
        body = i < 2 * depth - 2
        is_column = (i < 2) | (body & (lax.rem(i, 2) == 0))
        column_rank = jnp.where(i < 2, i, i // 2 + 1)
        pair_rank = jnp.where(body, (i - 3) // 2, i - depth)
        rank = jnp.where(is_column, column_rank, pair_rank)
        layer = ranked(z, depth, rank)
        slot = layer * 2 + jnp.where(is_column, x, 1 - x)

        @pl.when(i > 0)
        def _():
            x_copy(slot, send_pair.at[0], partner).wait_recv()

            @pl.when(is_column)
            def _():
                forward(rank, layer, slot)

            aux_copy(1, slot).wait_recv()

        block = xs[slot]
        aux = auxs[slot]
        aux_wide = aux.astype(jnp.float32)
        keep = lax.dot_general(
            aux, picks, (((0,), (0,)), ((), ())), preferred_element_type=jnp.float32
        ).astype(jnp.bfloat16)
        weighted = jnp.concatenate([block, block], axis=1) * keep
        gram[...] += lax.dot_general(
            block, weighted, (((0,), (0,)), ((), ())), preferred_element_type=jnp.float32
        )
        all_aux[...] += jnp.dot(aux, block, preferred_element_type=jnp.float32)
        wide = block.astype(jnp.float32)
        sq[...] += jnp.sum(wide * wide, axis=0, keepdims=True)
        for j, fold in enumerate(folds):
            held = jnp.sum(jnp.where(row_id == traits + fold, aux_wide, 0.0), axis=0, keepdims=True)
            aux_train = (aux_wide * (1.0 - held)).astype(jnp.bfloat16)
            cross[j] += jnp.dot(aux_train, block, preferred_element_type=jnp.float32)
            pairs[j] += lax.dot_general(
                aux_train, aux, (((1,), (1,)), ((), ())), preferred_element_type=jnp.float32
            )
        return 0

    lax.fori_loop(0, count, add_block, 0)
    for step in range(1, count):
        aux_copy(step, me).wait_send()
    for rank in range(depth):
        layer = ranked(z, depth, jnp.int32(rank))
        slot = layer * 2 + x

        @pl.when((layer <= z) & (z + 1 < depth))
        def _():
            x_copy(slot, send_up.at[rank], partner).wait_send()

        @pl.when((layer >= z) & (z >= 1))
        def _():
            x_copy(slot, send_down.at[rank], partner).wait_send()

        x_copy(slot, send_pair.at[rank], partner).wait_send()


def owned_systems(count):
    return -(-FOLDS * SHRINK // count)


def owned_folds(own, systems):
    first = lax.axis_index("samp") * own
    return [jnp.minimum(first + i, systems - 1) // SHRINK for i in (0, own - 1)]


def gather_grams(x, aux, count, traits):
    rows, width = x.shape
    f32 = jnp.float32
    depth = count // 2
    return pl.pallas_call(
        functools.partial(gram_kernel, depth, owned_systems(count), traits),
        out_shape=(
            jax.ShapeDtypeStruct((width, 2 * width), f32),
            jax.ShapeDtypeStruct((2, AUX, width), f32),
            jax.ShapeDtypeStruct((2, AUX, AUX), f32),
            jax.ShapeDtypeStruct((AUX, width), f32),
            jax.ShapeDtypeStruct((1, width), f32),
        ),
        in_specs=[ANY, ANY],
        out_specs=(VMEM,) * 5,
        scratch_shapes=[
            pltpu.VMEM((count, rows, width), x.dtype),
            pltpu.VMEM((count, AUX, rows), aux.dtype),
            pltpu.SemaphoreType.DMA((depth,)),
            pltpu.SemaphoreType.DMA((depth,)),
            pltpu.SemaphoreType.DMA((depth,)),
            pltpu.SemaphoreType.DMA((count,)),
            pltpu.SemaphoreType.DMA((count,)),
            pltpu.SemaphoreType.DMA((count,)),
            pltpu.SemaphoreType.DMA((2,)),
        ],
        compiler_params=pltpu.CompilerParams(
            collective_id=0, has_side_effects=True, vmem_limit_bytes=LIMIT
        ),
        name="gather_grams",
    )(x, aux)


def split_three(a):
    high = a.astype(jnp.bfloat16).astype(jnp.float32)
    rest = a - high
    middle = rest.astype(jnp.bfloat16).astype(jnp.float32)
    return high, middle, rest - middle


def thin_product(left, right):
    a, b, c = split_three(left)
    d, e, f = split_three(right)
    return lax.dot_general(
        jnp.concatenate([c, a, b, a, b, a], axis=0).astype(jnp.bfloat16),
        jnp.concatenate([d, f, e, e, d, d], axis=0).astype(jnp.bfloat16),
        (((0,), (0,)), ((), ())),
        preferred_element_type=jnp.float32,
    )


def sweep_panel(m_ref, batch, start, pivots):
    size, lanes = m_ref.shape[1:]
    sub = lax.broadcasted_iota(jnp.int32, (8, lanes), 0)
    lane = lax.broadcasted_iota(jnp.int32, (8, lanes), 1) - start
    inside = (lane >= 0) & (lane < pivots)
    unit = jnp.where(lane == sub, 1.0, 0.0)
    panels = [m_ref[b, pl.ds(start, 8), :] for b in range(batch)]
    if isinstance(start, int):
        turned, first = panels, start
    else:
        turned, first = [pltpu.roll(p, lanes - start, 1) for p in panels], 0
    columns = [
        [jnp.broadcast_to(p[:, first + j : first + j + 1], (8, lanes)) for j in range(pivots)]
        for p in turned
    ]
    solved = [jnp.where(inside, unit, p) for p in panels]
    for p in range(0, pivots, 2):
        q = p + 1
        at_p, at_q = sub == p, sub == q
        for b in range(batch):
            one, two = columns[b][p], columns[b][q]
            pp, pq = one[p : p + 1], two[p : p + 1]
            qp, qq = one[q : q + 1], two[q : q + 1]
            inverse = 1.0 / (pp * qq - pq * qp)

            def eliminate(t):
                tp, tq = t[p : p + 1], t[q : q + 1]
                up = (qq * tp - pq * tq) * inverse
                uq = (pp * tq - qp * tp) * inverse
                return jnp.where(at_p, up, jnp.where(at_q, uq, t - one * up - two * uq))

            solved[b] = eliminate(solved[b])
            for j in range(q + 1, pivots):
                columns[b][j] = eliminate(columns[b][j])
    row = lax.broadcasted_iota(jnp.int32, (size, lanes), 0) - start
    col = lax.broadcasted_iota(jnp.int32, (size, lanes), 1) - start
    cross = ((row >= 0) & (row < pivots)) | ((col >= 0) & (col < pivots))
    for b in range(batch):
        left = jnp.where(inside, -unit, panels[b])
        right = jnp.where(inside, -solved[b], solved[b])
        if pivots < 8:
            left = jnp.where(sub < pivots, left, 0.0)
            right = jnp.where(sub < pivots, right, 0.0)
        m_ref[b] = jnp.where(cross, 0.0, m_ref[b]) - thin_product(left, right)


def solve_kernel(
    systems, own, total, gram, cross, pairs, all_aux, sq, coef_ref, mean_ref, mats, rhs, lines, diag
):
    width = gram.shape[0]
    traits = coef_ref.shape[0] // own
    first = lax.axis_index("samp") * own
    fold_of = [jnp.minimum(first + i, systems - 1) // SHRINK for i in range(own)]
    folds = owned_folds(own, systems)
    aux_row = lax.broadcasted_iota(jnp.int32, (AUX, width), 0)
    fold_rows = (aux_row >= traits) & (aux_row < traits + FOLDS)
    fold_lines = lambda a: jnp.sum(jnp.where(fold_rows, a, 0.0), axis=0, keepdims=True)
    mean = fold_lines(all_aux[...]) / total
    scale = lax.rsqrt(sq[...] / total - mean * mean + EPS)
    mean_ref[...] = jnp.broadcast_to(mean, mean_ref.shape)
    pair_row = lax.broadcasted_iota(jnp.int32, (AUX, AUX), 0)
    pair_col = lax.broadcasted_iota(jnp.int32, (AUX, AUX), 1)
    pair_fold = (pair_col >= traits) & (pair_col < traits + FOLDS)
    eye = lax.broadcasted_iota(jnp.int32, (width, width), 0) == lax.broadcasted_iota(
        jnp.int32, (width, width), 1
    )
    column_of = lambda line: jnp.sum(jnp.where(eye, line, 0.0), axis=1, keepdims=True)
    mean_col, scale_col = column_of(mean), column_of(scale)
    for j in range(2):
        sums = fold_lines(cross[j])
        pair = pairs[j]
        kept = jnp.sum(jnp.where(pair_fold & (pair_row == pair_col), pair, 0.0))
        trait_sums = jnp.sum(jnp.where(pair_fold, pair, 0.0), axis=1, keepdims=True)[:traits]
        half = slice(j * width, (j + 1) * width)
        mats[j] = scale_col * scale * (
            gram[:, half] - mean_col * sums - column_of(sums) * mean + kept * (mean_col * mean)
        )
        lines[j] = scale * (cross[j, :traits] - trait_sums * mean)
    for i in range(own - 1, -1, -1):
        shrink = jnp.minimum(first + i, systems - 1) - fold_of[i] * SHRINK
        penalty = jnp.float32(RATIOS[0] * width)
        for l in range(1, SHRINK):
            penalty = jnp.where(shrink == l, jnp.float32(RATIOS[l] * width), penalty)
        late = jnp.where(fold_of[i] != folds[0], 1, 0)
        mats[i + 2] = mats[late] + jnp.where(eye, penalty, 0.0)
        rhs[i] = lines[late]
    steps = width // PANEL
    for j in range(steps):
        here = slice(j * PANEL, (j + 1) * PANEL)
        rest = slice((j + 1) * PANEL, width)
        at = diag.at[j]
        for i in range(own):
            at[i] = mats[i + 2, here, here]

        def one(step, _):
            sweep_panel(at, own, pl.multiple_of(step * 8, 8), 8)
            return 0

        lax.fori_loop(0, PANEL // 8, one, 0)
        for i in range(own):
            right = -high_dot(rhs[i, :, here], at[i], ((1,), (0,)))
            rhs[i, :, here] = right
            if j + 1 < steps:
                tail = mats[i + 2, here, rest]
                solved = high_dot(at[i], tail, ((1,), (0,)))
                mats[i + 2, rest, rest] += high_dot(tail, solved, ((0,), (0,)))
                rhs[i, :, rest] -= high_dot(right, tail, ((1,), (0,)))
    for j in range(steps - 2, -1, -1):
        here = slice(j * PANEL, (j + 1) * PANEL)
        rest = slice((j + 1) * PANEL, width)
        for i in range(own):
            back = high_dot(rhs[i, :, rest], mats[i + 2, here, rest], ((1,), (1,)))
            rhs[i, :, here] += high_dot(back, diag[j, i], ((1,), (0,)))
    for i in range(own):
        coef_ref[i * traits : (i + 1) * traits] = (rhs[i] * scale).astype(jnp.bfloat16)


def solve_level0(sums, traits, count, rows):
    width = sums[0].shape[0]
    own = owned_systems(count)
    f32 = jnp.float32
    return plain(
        functools.partial(solve_kernel, FOLDS * SHRINK, own, count * rows),
        (
            jax.ShapeDtypeStruct((own * traits, width), jnp.bfloat16),
            jax.ShapeDtypeStruct((8, width), f32),
        ),
        "solve_level0",
        *sums,
        scratch=[
            pltpu.VMEM((own + 2, width, width), f32),
            pltpu.VMEM((own, traits, width), f32),
            pltpu.VMEM((2, traits, width), f32),
            pltpu.VMEM((width // PANEL, own, PANEL, PANEL), f32),
        ],
    )


def predict(coef, mean, x, folds, o_ref):
    parts, _, group, _ = o_ref.shape
    traits = parts * group
    per_fold = SHRINK * traits
    coef = coef[: FOLDS * per_fold]
    raw = lax.dot_general(
        coef, x, (((1,), (1,)), ((), ())), preferred_element_type=jnp.float32
    )
    shift = jnp.sum(coef.astype(jnp.float32) * mean, axis=1, keepdims=True)
    raw = raw - shift
    out = jnp.zeros((per_fold, raw.shape[1]), jnp.float32)
    for k in range(FOLDS):
        out = jnp.where(folds == k, raw[k * per_fold : (k + 1) * per_fold], out)
    for g in range(parts):
        for l in range(SHRINK):
            o_ref[g, l] = out[l * traits + g * group : l * traits + (g + 1) * group]


def level_kernel(
    depth, blk, coef_ref, mean_ref, x_ref, traits_ref, folds_ref,
    p_ref, f_ref, sum_ref,
    coefs, sent, part, arrived,
    send_line, send_pair, recv, send_blk, recv_blk, send_sum, recv_sum,
):
    count = 2 * depth
    me = lax.axis_index("samp")
    here = lax.axis_index("blk")
    z, x = me // 2, lax.rem(me, 2)
    partner = z * 2 + 1 - x
    barrier = pltpu.get_barrier_semaphore()
    for axis, size, at in (("samp", count, me), ("blk", blk, here)):
        for step in range(1, size):
            pl.semaphore_signal(
                barrier,
                inc=1,
                device_id={axis: lax.rem(at + step, size)},
                device_id_type=MESH,
            )
    coefs[me] = coef_ref[...]
    pl.semaphore_wait(barrier, count + blk - 2)

    def coef_copy(slot, sem, target):
        return pltpu.make_async_remote_copy(
            src_ref=coefs.at[slot],
            dst_ref=coefs.at[slot],
            send_sem=sem,
            recv_sem=recv.at[slot],
            device_id={"samp": target},
            device_id_type=MESH,
        )

    mate = lambda step: lax.rem(z + step, depth) * 2 + x
    for step in range(1, depth):
        coef_copy(me, send_line.at[step], mate(step)).start()
    coef_copy(me, send_pair.at[0], partner).start()
    for step in range(1, depth):
        coef_copy(mate(step), send_pair.at[0], partner).wait_recv()
        coef_copy(mate(step), send_pair.at[step], partner).start()
    for step in range(depth):
        slot = lax.rem(z + step, depth) * 2 + 1 - x
        coef_copy(slot, send_pair.at[0], partner).wait_recv()
    predict(
        coefs[...].reshape(-1, coefs.shape[2]),
        mean_ref[:1],
        x_ref[...],
        folds_ref[...],
        sent,
    )

    def pred_copy(step, slot):
        other = lax.rem(here + step, blk)
        return pltpu.make_async_remote_copy(
            src_ref=sent.at[other],
            dst_ref=p_ref.at[slot],
            send_sem=send_blk.at[step],
            recv_sem=recv_blk.at[slot],
            device_id={"blk": other},
            device_id_type=MESH,
        )

    for step in range(1, blk):
        pred_copy(step, here).start()
    p_ref[here] = sent[here]
    for step in range(1, depth):
        coef_copy(me, send_line.at[step], partner).wait_send()
    for step in range(depth):
        coef_copy(me, send_pair.at[step], partner).wait_send()
    for step in range(1, blk):
        pred_copy(step, lax.rem(here + step, blk)).wait()
    moments(p_ref, traits_ref, folds_ref, f_ref, part.at[0])
    stages = part.shape[0]
    copies = []
    for stage in range(stages):
        bit = 2**stage
        other = me + bit - 2 * bit * lax.rem(me // bit, 2)
        copy = pltpu.make_async_remote_copy(
            src_ref=part.at[stage],
            dst_ref=arrived.at[stage],
            send_sem=send_sum.at[stage],
            recv_sem=recv_sum.at[stage],
            device_id={"samp": other},
            device_id_type=MESH,
        )
        copy.start()
        copies.append(copy)
        copy.wait_recv()
        summed = part[stage] + arrived[stage]
        if stage + 1 < stages:
            part[stage + 1] = summed
        else:
            sum_ref[...] = summed
    for copy in copies:
        copy.wait_send()


def moments(p_ref, traits_ref, folds_ref, f_ref, e_ref):
    blocks, shrinks, group, rows = p_ref.shape
    preds = blocks * shrinks
    f_ref[...] = jnp.zeros_like(f_ref)
    for t in range(group):
        base = t * ROWS1
        for b in range(blocks):
            for l in range(shrinks):
                at = base + b * shrinks + l
                f_ref[at : at + 1] = p_ref[b, l, t : t + 1]
        f_ref[base + preds : base + preds + 1] = traits_ref[t : t + 1]
        f_ref[base + preds + 1 : base + preds + 2] = jnp.ones((1, rows), jnp.float32)
    f = f_ref[...]
    size = group * ROWS1
    folds = folds_ref[...]
    lane = lax.broadcasted_iota(jnp.int32, (ROWS1, size), 1)
    for k in range(FOLDS):
        full = high_dot(jnp.where(folds == k, f, 0.0), f, ((1,), (1,)))
        packed = jnp.zeros((ROWS1, size), jnp.float32)
        for t in range(group):
            inside = (lane >= t * ROWS1) & (lane < (t + 1) * ROWS1)
            packed = jnp.where(inside, full[t * ROWS1 : (t + 1) * ROWS1], packed)
        e_ref[k * ROWS1 : (k + 1) * ROWS1] = packed


def blend_kernel(total, e_ref, f_ref, p_ref, folds_ref, level_ref, blend_ref, mats):
    blocks, shrinks, group, rows = p_ref.shape
    preds = blocks * shrinks
    summed = e_ref[...]
    shape = (ROWS1, ROWS1)
    row = lax.broadcasted_iota(jnp.int32, shape, 0)
    col = lax.broadcasted_iota(jnp.int32, shape, 1)
    col_in = lax.broadcasted_iota(jnp.int32, (ROWS1, 1), 0) < preds
    row_in = lax.broadcasted_iota(jnp.int32, (1, ROWS1), 1) < preds
    one_lane = lax.broadcasted_iota(jnp.int32, (1, ROWS1), 1) == preds + 1
    ridge = jnp.where((row == col) & (row < preds), total / 4.0, 0.0)
    own = [
        [
            summed[k * ROWS1 : (k + 1) * ROWS1, t * ROWS1 : (t + 1) * ROWS1]
            for k in range(FOLDS)
        ]
        for t in range(group)
    ]
    means, scales = [], []
    for t in range(group):
        full = own[t][0]
        for k in range(1, FOLDS):
            full = full + own[t][k]
        mean_row = jnp.where(row_in, full[preds + 1 : preds + 2] / total, 0.0)
        mean_col = jnp.where(col_in, full[:, preds + 1 : preds + 2] / total, 0.0)
        square = jnp.where(row == col, full, 0.0) / total
        sq_row = jnp.sum(square, axis=0, keepdims=True)
        sq_col = jnp.sum(square, axis=1, keepdims=True)
        scale_row = jnp.where(row_in, lax.rsqrt(sq_row - mean_row * mean_row + EPS), 1.0)
        scale_col = jnp.where(col_in, lax.rsqrt(sq_col - mean_col * mean_col + EPS), 1.0)
        means.append((mean_row, mean_col))
        scales.append((scale_row, scale_col))
        for k in range(FOLDS):
            train = full - own[t][k]
            sums_row = train[preds + 1 : preds + 2]
            sums_col = train[:, preds + 1 : preds + 2]
            kept = train[preds + 1 : preds + 2, preds + 1 : preds + 2]
            centered = (
                train - mean_col * sums_row - sums_col * mean_row + kept * (mean_col * mean_row)
            )
            mats[t * FOLDS + k] = scale_col * scale_row * centered + ridge
    for b in range(blocks):
        for l in range(shrinks):
            at = b * shrinks + l
            means_at = jnp.concatenate([means[t][1][at : at + 1] for t in range(group)], axis=0)
            scales_at = jnp.concatenate([scales[t][1][at : at + 1] for t in range(group)], axis=0)
            level_ref[b, l] = (p_ref[b, l] - means_at) * scales_at

    for start in range(0, preds, 8):
        sweep_panel(mats, group * FOLDS, start, min(8, preds - start))
    folds = folds_ref[...]
    for t in range(group):
        mean_row, scale_row = means[t][0], scales[t][0]
        lines = []
        first = jnp.zeros((1, 1), jnp.float32)
        second = jnp.zeros((1, 1), jnp.float32)
        for k in range(FOLDS):
            line = jnp.where(row_in, mats[t * FOLDS + k, preds : preds + 1, :] * scale_row, 0.0)
            offset = jnp.sum(line * mean_row, axis=1, keepdims=True)
            line = jnp.where(one_lane, -offset, line)
            lines.append(line)
            product = jnp.sum(own[t][k] * line, axis=1, keepdims=True)
            line_col = jnp.sum(jnp.where(row == col, line, 0.0), axis=1, keepdims=True)
            first = first + product[preds + 1 : preds + 2]
            second = second + jnp.sum(product * line_col, axis=0, keepdims=True)
        lines.append(jnp.zeros((8 - FOLDS, ROWS1), jnp.float32))
        every = high_dot(
            jnp.concatenate(lines, axis=0),
            f_ref[t * ROWS1 : (t + 1) * ROWS1],
            ((1,), (0,)),
        )
        p = jnp.zeros((1, rows), jnp.float32)
        for k in range(FOLDS):
            p = jnp.where(folds == k, every[k : k + 1], p)
        mean = first / total
        spread_of = second / total - mean * mean
        blend_ref[t : t + 1] = (p - mean) * lax.rsqrt(spread_of + EPS)


def plain(kernel, out_shape, name, *args, scratch=()):
    return pl.pallas_call(
        kernel,
        out_shape=out_shape,
        in_specs=[VMEM] * len(args),
        out_specs=jax.tree.map(lambda _: VMEM, out_shape),
        scratch_shapes=list(scratch),
        compiler_params=pltpu.CompilerParams(vmem_limit_bytes=LIMIT),
        name=name,
    )(*args)


def fast(samp, blk, dosages, traits, folds):
    rows, width = dosages.shape
    count_traits = traits.shape[0]
    group = count_traits // blk
    f32 = jnp.float32
    fold_ids = jnp.arange(AUX - count_traits, dtype=jnp.int32)
    one_hot = (folds[None, :] == fold_ids[:, None]).astype(jnp.bfloat16)
    aux = jnp.concatenate([traits, one_hot], axis=0)
    folds_row = folds[None, :]
    own_traits = lax.dynamic_slice_in_dim(
        traits, lax.axis_index("blk") * group, group, 0
    ).astype(f32)
    sums = gather_grams(dosages, aux, samp, count_traits)
    coef, mean = solve_level0(sums, count_traits, samp, rows)
    shape = jax.ShapeDtypeStruct((blk, SHRINK, group, rows), f32)
    size = group * ROWS1
    own = owned_systems(samp) * count_traits
    depth = samp // 2
    stages = samp.bit_length() - 1
    dma = pltpu.SemaphoreType.DMA
    pred, stacked, moment_sums = pl.pallas_call(
        functools.partial(level_kernel, depth, blk),
        out_shape=(
            shape,
            jax.ShapeDtypeStruct((size, rows), f32),
            jax.ShapeDtypeStruct((FOLDS * ROWS1, size), f32),
        ),
        in_specs=[VMEM] * 5,
        out_specs=(VMEM,) * 3,
        scratch_shapes=[
            pltpu.VMEM((samp, own, width), jnp.bfloat16),
            pltpu.VMEM(shape.shape, f32),
            pltpu.VMEM((stages, FOLDS * ROWS1, size), f32),
            pltpu.VMEM((stages, FOLDS * ROWS1, size), f32),
            dma((depth,)),
            dma((depth,)),
            dma((samp,)),
            dma((blk,)),
            dma((blk,)),
            dma((stages,)),
            dma((stages,)),
        ],
        compiler_params=pltpu.CompilerParams(
            collective_id=1, has_side_effects=True, vmem_limit_bytes=LIMIT
        ),
        name="predict_level0",
    )(coef, mean, dosages, own_traits, folds_row)
    level0, blend = plain(
        functools.partial(blend_kernel, float(samp * rows)),
        (shape, jax.ShapeDtypeStruct((group, rows), f32)),
        "blend",
        moment_sums,
        stacked,
        pred,
        folds_row,
        scratch=[pltpu.VMEM((group * FOLDS, ROWS1, ROWS1), f32)],
    )
    return level0, blend


def solution(mesh):
    in_specs = (P("samp", "blk"), P(None, "samp"), P("samp"))
    out_specs = (P(None, None, "blk", "samp"), P("blk", "samp"))
    samp, blk = mesh.shape["samp"], mesh.shape["blk"]
    body = functools.partial(fast, samp, blk) if samp == 8 else shards
    return jax.shard_map(body, mesh=mesh, in_specs=in_specs, out_specs=out_specs, check_vma=False)
```

```python
import functools

import jax
import jax.numpy as jnp
from jax import lax
from jax.experimental import pallas as pl
from jax.experimental.pallas import tpu as pltpu
from jax.sharding import PartitionSpec as P

FOLDS = 5
SHRINK = 5


RATIOS = (99.0, 3.0, 1.0, 1.0 / 3.0, 1.0 / 99.0)
EPS = 1e-05
HIGH = lax.Precision.HIGHEST


def solve_batch(systems, right_sides):
    factors = jnp.linalg.cholesky(systems)

    def solve_single(factor, right_side):
        return jax.scipy.linalg.cho_solve((factor, True), right_side)

    return jax.vmap(solve_single)(factors, right_sides)


def shards(dosages, traits, folds):
    rows, width = dosages.shape
    traits_count = traits.shape[0]
    fold_ids = jnp.arange(FOLDS, dtype=jnp.int32)
    masks = (folds[None, :] == fold_ids[:, None]).astype(jnp.float32)
    mask_half = masks.astype(jnp.bfloat16)
    traits_wide = traits.astype(jnp.float32)
    grams = []
    crosses = []
    for fold in range(FOLDS):
        weighted = dosages * mask_half[fold][:, None]
        grams.append(jnp.einsum("ri,rj->ij", dosages, weighted, preferred_element_type=jnp.float32))
        crosses.append(
            jnp.dot(traits * mask_half[fold][None, :], dosages, preferred_element_type=jnp.float32)
        )
    gram = jnp.stack(grams)
    cross = jnp.stack(crosses)
    sums = jnp.dot(mask_half, dosages, preferred_element_type=jnp.float32)
    counts = jnp.sum(masks, axis=1)
    trait_sums = jnp.einsum("ks,ts->kt", masks, traits_wide, precision=HIGH)
    gram, sums, cross, counts, trait_sums = lax.psum(
        (gram, sums, cross, counts, trait_sums), "samp"
    )
    total = jnp.sum(counts)
    mean = jnp.sum(sums, axis=0) / total
    gram_total = jnp.sum(gram, axis=0)
    variance = jnp.diagonal(gram_total) / total - mean * mean
    scale = lax.rsqrt(variance + EPS)
    sums_total = jnp.sum(sums, axis=0)
    cross_total = jnp.sum(cross, axis=0)
    trait_total = jnp.sum(trait_sums, axis=0)
    ratios = jnp.array(RATIOS, dtype=jnp.float32)
    identity = jnp.eye(width, dtype=jnp.float32)

    def train_system(fold):
        train_gram = gram_total - lax.dynamic_index_in_dim(gram, fold, 0, keepdims=False)
        train_sums = sums_total - lax.dynamic_index_in_dim(sums, fold, 0, keepdims=False)
        train_count = total - lax.dynamic_index_in_dim(counts, fold, 0, keepdims=False)
        train_cross = cross_total - lax.dynamic_index_in_dim(cross, fold, 0, keepdims=False)
        train_traits = trait_total - lax.dynamic_index_in_dim(trait_sums, fold, 0, keepdims=False)
        centered = (
            train_gram
            - mean[:, None] * train_sums[None, :]
            - train_sums[:, None] * mean[None, :]
            + train_count * mean[:, None] * mean[None, :]
        )
        system = scale[:, None] * centered * scale[None, :]
        target = scale[:, None] * (train_cross.T - mean[:, None] * train_traits[None, :])
        return (system, target)

    systems_count = FOLDS * SHRINK
    per_device = -(-systems_count // lax.axis_size("samp"))
    first = lax.axis_index("samp") * per_device

    def solve_own(offset):
        which = jnp.minimum(first + offset, systems_count - 1)
        fold = which // SHRINK
        shrink = which - fold * SHRINK
        system, target = train_system(fold)
        penalty = jnp.sum(
            jnp.where(jnp.arange(SHRINK, dtype=jnp.int32) == shrink, ratios * width, 0.0)
        )
        beta = solve_batch((system + penalty * identity)[None], target[None])[0]
        return (scale[:, None] * beta).astype(jnp.bfloat16)

    owned = lax.map(solve_own, jnp.arange(per_device, dtype=jnp.int32))
    collected = lax.all_gather(owned, "samp", axis=0, tiled=True)
    coef = collected[:systems_count].reshape(FOLDS, SHRINK, width, traits_count)
    coef_flat = coef.transpose(2, 0, 1, 3).reshape(width, FOLDS * SHRINK * traits_count)
    shift = jnp.einsum("v,klvt->klt", mean, coef.astype(jnp.float32), precision=HIGH)
    raw = jnp.einsum("vc,rv->cr", coef_flat, dosages, preferred_element_type=jnp.float32)
    outcome = raw.reshape(FOLDS, SHRINK, traits_count, rows) - shift[..., None]
    level_pred = jnp.einsum("kltr,kr->ltr", outcome, masks, precision=HIGH)
    group = traits_count // lax.axis_size("blk")
    start = lax.axis_index("blk") * group
    own_traits = lax.dynamic_slice_in_dim(traits_wide, start, group, 0)
    own_sums = lax.dynamic_slice_in_dim(trait_sums, start, group, 1)
    arrived = lax.all_to_all(level_pred[None], "blk", split_axis=2, concat_axis=0, tiled=True)
    count_pred = arrived.shape[0] * arrived.shape[1]
    flat = arrived.reshape(count_pred, group, rows)
    raw_grams = jnp.einsum("ks,ats,bts->ktab", masks, flat, flat, precision=HIGH)
    raw_cross = jnp.einsum("ks,ats,ts->kta", masks, flat, own_traits, precision=HIGH)
    raw_sums = jnp.einsum("ks,ats->kta", masks, flat, precision=HIGH)
    raw_grams, raw_cross, raw_sums = lax.psum((raw_grams, raw_cross, raw_sums), "samp")
    pred_mean = jnp.sum(raw_sums, axis=0) / total
    pred_sq = jnp.diagonal(jnp.sum(raw_grams, axis=0), axis1=1, axis2=2)
    pred_scale = lax.rsqrt(pred_sq / total - pred_mean * pred_mean + EPS)
    standard = (flat - pred_mean.T[:, :, None]) * pred_scale.T[:, :, None]
    outer_scale = pred_scale[None, :, :, None] * pred_scale[None, :, None, :]
    fold_grams = outer_scale * (
        raw_grams
        - pred_mean[None, :, :, None] * raw_sums[:, :, None, :]
        - raw_sums[:, :, :, None] * pred_mean[None, :, None, :]
        + counts[:, None, None, None] * pred_mean[None, :, :, None] * pred_mean[None, :, None, :]
    )
    fold_cross = pred_scale[None] * (raw_cross - pred_mean[None] * own_sums[:, :, None])
    level0 = standard.reshape(arrived.shape)
    train_grams = jnp.sum(fold_grams, axis=0)[None] - fold_grams
    train_cross = jnp.sum(fold_cross, axis=0)[None] - fold_cross
    shrunk = train_grams + total / 4.0 * jnp.eye(count_pred, dtype=jnp.float32)
    weights = solve_batch(
        shrunk.reshape(-1, count_pred, count_pred), train_cross.reshape(-1, count_pred)
    )
    weights = weights.reshape(FOLDS, group, count_pred)
    every_fold = jnp.einsum("ats,kta->kts", standard, weights, precision=HIGH)
    blended = jnp.einsum("kts,ks->ts", every_fold, masks, precision=HIGH)
    blend_sum, blend_sq = lax.psum(
        (jnp.sum(blended, axis=-1), jnp.sum(blended * blended, axis=-1)), "samp"
    )
    blend_mean = blend_sum / total
    blend_var = blend_sq / total - blend_mean * blend_mean
    blend = (blended - blend_mean[:, None]) * lax.rsqrt(blend_var + EPS)[:, None]
    return (level0, blend)


MESH = pl.DeviceIdType.MESH
AUX = 32
ROWS1 = 24
PANEL = 128
LIMIT = 48 * 1024 * 1024
VMEM = pl.BlockSpec(memory_space=pltpu.VMEM)
ANY = pl.BlockSpec(memory_space=pl.ANY)


def high_dot(a, b, dims):
    return lax.dot_general(
        a, b, (dims, ((), ())), precision=HIGH, preferred_element_type=jnp.float32
    )


def greet(axis, count):
    barrier = pltpu.get_barrier_semaphore()
    me = lax.axis_index(axis)
    for step in range(1, count):
        pl.semaphore_signal(
            barrier, inc=1, device_id={axis: lax.rem(me + step, count)}, device_id_type=MESH
        )
    pl.semaphore_wait(barrier, count - 1)


def ranked(z, depth, rank):
    near = jnp.minimum(z, depth - 1 - z)
    both = jnp.where(lax.rem(rank, 2) == 1, z - (rank + 1) // 2, z + rank // 2)
    one = jnp.where(z < depth - 1 - z, z + rank - near, z - rank + near)
    return jnp.where(rank <= 2 * near, both, one)


def gram_kernel(
    depth, own_systems, traits, x_ref, aux_ref,
    gram, cross, pairs, all_aux, sq,
    xs, auxs, send_up, send_down, send_pair, recv, asend, arecv, own, send_extra, recv_half,
):
    me = lax.axis_index("samp")
    z, x = me // 2, lax.rem(me, 2)
    partner = z * 2 + 1 - x
    count = 2 * depth
    is_end = (z == 0) | (z == depth - 1)
    is_middle = (z > 0) & (z < depth - 1)
    far = jnp.where(z < depth // 2, depth - 1, 0)
    near = depth - 1 - far
    half = xs.shape[1] // 2
    keep = pltpu.make_async_copy(x_ref, xs.at[me], own.at[0])
    keep.start()
    keep_aux = pltpu.make_async_copy(aux_ref, auxs.at[me], own.at[1])
    keep_aux.start()
    greet("samp", count)

    def x_copy(slot, sem, target):
        return pltpu.make_async_remote_copy(
            src_ref=xs.at[slot],
            dst_ref=xs.at[slot],
            send_sem=sem,
            recv_sem=recv.at[slot],
            device_id={"samp": target},
            device_id_type=MESH,
        )

    def half_copy(slot, part, send_sem, recv_sem, target):
        piece = xs.at[slot, pl.ds(part * half, half)]
        return pltpu.make_async_remote_copy(
            src_ref=piece,
            dst_ref=piece,
            send_sem=send_sem,
            recv_sem=recv_sem,
            device_id={"samp": target},
            device_id_type=MESH,
        )

    def to_pair(rank, layer, slot, act):
        @pl.when((is_end & (layer != far)) | (is_middle & (layer != near)))
        def _():
            act(x_copy(slot, send_pair.at[rank], partner))

        @pl.when(is_end & (layer == far))
        def _():
            act(half_copy(slot, 1, send_pair.at[rank], recv.at[slot], partner))

    def extra(act):
        target = jnp.where((z == 0) | ((z != depth - 1) & (z >= depth // 2)), me + 2, me - 2)

        @pl.when(is_end)
        def _():
            act(x_copy(partner, send_extra.at[0], target))

        @pl.when(is_middle)
        def _():
            slot = far * 2 + 1 - x
            act(half_copy(slot, 0, send_extra.at[0], recv_half.at[0], target))

    def aux_copy(step, slot):
        other = lax.rem(me + step, count)
        return pltpu.make_async_remote_copy(
            src_ref=auxs.at[slot],
            dst_ref=auxs.at[slot],
            send_sem=asend.at[step],
            recv_sem=arecv.at[slot],
            device_id={"samp": other},
            device_id_type=MESH,
        )

    keep.wait()
    keep_aux.wait()
    _, width = gram.shape
    width = width // 2
    rows = xs.shape[1]
    folds = owned_folds(own_systems, FOLDS * SHRINK)
    aux_row = lax.broadcasted_iota(jnp.int32, (AUX, width), 0)
    fold_rows = (aux_row >= traits) & (aux_row < traits + FOLDS)
    picks = jnp.concatenate(
        [
            jnp.where(fold_rows & (aux_row != traits + fold), 1.0, 0.0).astype(jnp.bfloat16)
            for fold in folds
        ],
        axis=1,
    )
    row_id = lax.broadcasted_iota(jnp.int32, (AUX, rows), 0)

    def forward(rank, layer, slot):
        @pl.when((layer <= z) & (z + 1 < depth))
        def _():
            x_copy(slot, send_up.at[rank], me + 2).start()

        @pl.when((layer >= z) & (z >= 1))
        def _():
            x_copy(slot, send_down.at[rank], me - 2).start()

        to_pair(rank, layer, slot, lambda copy: copy.start())

    forward(0, z, me)
    for step in range(1, count):
        aux_copy(step, me).start()
    for ref in (gram, cross, pairs, all_aux, sq):
        ref[...] = jnp.zeros_like(ref)

    def add_block(i, _):
        body = i < 2 * depth - 2
        swap = is_end & (i >= 2) & body
        i_first = i
        i = jnp.where(swap, i + 1 - 2 * lax.rem(i, 2), i)
        is_column = (i < 2) | (body & (lax.rem(i, 2) == 0))
        column_rank = jnp.where(i < 2, i, i // 2 + 1)
        pair_rank = jnp.where(body, (i - 3) // 2, i - depth)
        rank = jnp.where(is_column, column_rank, pair_rank)
        layer = ranked(z, depth, rank)
        slot = layer * 2 + jnp.where(is_column, x, 1 - x)

        @pl.when(i_first > 0)
        def _():
            cut = is_end & jnp.logical_not(is_column) & (layer == far)

            @pl.when(jnp.logical_not(cut))
            def _():
                x_copy(slot, send_pair.at[0], partner).wait_recv()

            @pl.when(cut)
            def _():
                half_copy(slot, 1, send_pair.at[0], recv.at[slot], partner).wait_recv()
                half_copy(slot, 0, send_pair.at[0], recv_half.at[0], partner).wait_recv()

            @pl.when(is_column)
            def _():
                forward(rank, layer, slot)

            @pl.when(jnp.logical_not(is_column) & (layer == jnp.where(is_end, z, far)))
            def _():
                extra(lambda copy: copy.start())

            aux_copy(1, slot).wait_recv()

        block = xs[slot]
        aux = auxs[slot]
        aux_wide = aux.astype(jnp.float32)
        keep = lax.dot_general(
            aux, picks, (((0,), (0,)), ((), ())), preferred_element_type=jnp.float32
        ).astype(jnp.bfloat16)
        weighted = jnp.concatenate([block, block], axis=1) * keep
        gram[...] += lax.dot_general(
            block, weighted, (((0,), (0,)), ((), ())), preferred_element_type=jnp.float32
        )
        all_aux[...] += jnp.dot(aux, block, preferred_element_type=jnp.float32)
        wide = block.astype(jnp.float32)
        sq[...] += jnp.sum(wide * wide, axis=0, keepdims=True)
        for j, fold in enumerate(folds):
            held = jnp.sum(jnp.where(row_id == traits + fold, aux_wide, 0.0), axis=0, keepdims=True)
            aux_train = (aux_wide * (1.0 - held)).astype(jnp.bfloat16)
            cross[j] += jnp.dot(aux_train, block, preferred_element_type=jnp.float32)
            pairs[j] += lax.dot_general(
                aux_train, aux, (((1,), (1,)), ((), ())), preferred_element_type=jnp.float32
            )
        return 0

    lax.fori_loop(0, count, add_block, 0)
    for step in range(1, count):
        aux_copy(step, me).wait_send()
    for rank in range(depth):
        layer = ranked(z, depth, jnp.int32(rank))
        slot = layer * 2 + x

        @pl.when((layer <= z) & (z + 1 < depth))
        def _():
            x_copy(slot, send_up.at[rank], partner).wait_send()

        @pl.when((layer >= z) & (z >= 1))
        def _():
            x_copy(slot, send_down.at[rank], partner).wait_send()

        to_pair(rank, layer, slot, lambda copy: copy.wait_send())
    extra(lambda copy: copy.wait_send())


def owned_systems(count):
    return -(-FOLDS * SHRINK // count)


def owned_folds(own, systems):
    first = lax.axis_index("samp") * own
    return [jnp.minimum(first + i, systems - 1) // SHRINK for i in (0, own - 1)]


def gather_grams(x, aux, count, traits):
    rows, width = x.shape
    f32 = jnp.float32
    depth = count // 2
    return pl.pallas_call(
        functools.partial(gram_kernel, depth, owned_systems(count), traits),
        out_shape=(
            jax.ShapeDtypeStruct((width, 2 * width), f32),
            jax.ShapeDtypeStruct((2, AUX, width), f32),
            jax.ShapeDtypeStruct((2, AUX, AUX), f32),
            jax.ShapeDtypeStruct((AUX, width), f32),
            jax.ShapeDtypeStruct((1, width), f32),
        ),
        in_specs=[ANY, ANY],
        out_specs=(VMEM,) * 5,
        scratch_shapes=[
            pltpu.VMEM((count, rows, width), x.dtype),
            pltpu.VMEM((count, AUX, rows), aux.dtype),
            pltpu.SemaphoreType.DMA((depth,)),
            pltpu.SemaphoreType.DMA((depth,)),
            pltpu.SemaphoreType.DMA((depth,)),
            pltpu.SemaphoreType.DMA((count,)),
            pltpu.SemaphoreType.DMA((count,)),
            pltpu.SemaphoreType.DMA((count,)),
            pltpu.SemaphoreType.DMA((2,)),
            pltpu.SemaphoreType.DMA((1,)),
            pltpu.SemaphoreType.DMA((1,)),
        ],
        compiler_params=pltpu.CompilerParams(
            collective_id=0, has_side_effects=True, vmem_limit_bytes=LIMIT
        ),
        name="gather_grams",
    )(x, aux)


def split_three(a):
    high = a.astype(jnp.bfloat16).astype(jnp.float32)
    rest = a - high
    middle = rest.astype(jnp.bfloat16).astype(jnp.float32)
    return high, middle, rest - middle


def thin_product(left, right):
    a, b, c = split_three(left)
    d, e, f = split_three(right)
    return lax.dot_general(
        jnp.concatenate([c, a, b, a, b, a], axis=0).astype(jnp.bfloat16),
        jnp.concatenate([d, f, e, e, d, d], axis=0).astype(jnp.bfloat16),
        (((0,), (0,)), ((), ())),
        preferred_element_type=jnp.float32,
    )


def sweep_panel(m_ref, batch, start, pivots):
    size, lanes = m_ref.shape[1:]
    sub = lax.broadcasted_iota(jnp.int32, (8, lanes), 0)
    lane = lax.broadcasted_iota(jnp.int32, (8, lanes), 1) - start
    inside = (lane >= 0) & (lane < pivots)
    unit = jnp.where(lane == sub, 1.0, 0.0)
    panels = [m_ref[b, pl.ds(start, 8), :] for b in range(batch)]
    if isinstance(start, int):
        turned, first = panels, start
    else:
        turned, first = [pltpu.roll(p, lanes - start, 1) for p in panels], 0
    columns = [
        [jnp.broadcast_to(p[:, first + j : first + j + 1], (8, lanes)) for j in range(pivots)]
        for p in turned
    ]
    solved = [jnp.where(inside, unit, p) for p in panels]
    for p in range(0, pivots, 2):
        q = p + 1
        at_p, at_q = sub == p, sub == q
        for b in range(batch):
            one, two = columns[b][p], columns[b][q]
            pp, pq = one[p : p + 1], two[p : p + 1]
            qp, qq = one[q : q + 1], two[q : q + 1]
            inverse = 1.0 / (pp * qq - pq * qp)

            def eliminate(t):
                tp, tq = t[p : p + 1], t[q : q + 1]
                up = (qq * tp - pq * tq) * inverse
                uq = (pp * tq - qp * tp) * inverse
                return jnp.where(at_p, up, jnp.where(at_q, uq, t - one * up - two * uq))

            solved[b] = eliminate(solved[b])
            for j in range(q + 1, pivots):
                columns[b][j] = eliminate(columns[b][j])
    row = lax.broadcasted_iota(jnp.int32, (size, lanes), 0) - start
    col = lax.broadcasted_iota(jnp.int32, (size, lanes), 1) - start
    cross = ((row >= 0) & (row < pivots)) | ((col >= 0) & (col < pivots))
    for b in range(batch):
        left = jnp.where(inside, -unit, panels[b])
        right = jnp.where(inside, -solved[b], solved[b])
        if pivots < 8:
            left = jnp.where(sub < pivots, left, 0.0)
            right = jnp.where(sub < pivots, right, 0.0)
        m_ref[b] = jnp.where(cross, 0.0, m_ref[b]) - thin_product(left, right)


def solve_kernel(
    systems, own, total, gram, cross, pairs, all_aux, sq, coef_ref, mean_ref, mats, rhs, lines, diag
):
    width = gram.shape[0]
    traits = coef_ref.shape[0] // own
    first = lax.axis_index("samp") * own
    fold_of = [jnp.minimum(first + i, systems - 1) // SHRINK for i in range(own)]
    folds = owned_folds(own, systems)
    aux_row = lax.broadcasted_iota(jnp.int32, (AUX, width), 0)
    fold_rows = (aux_row >= traits) & (aux_row < traits + FOLDS)
    fold_lines = lambda a: jnp.sum(jnp.where(fold_rows, a, 0.0), axis=0, keepdims=True)
    mean = fold_lines(all_aux[...]) / total
    scale = lax.rsqrt(sq[...] / total - mean * mean + EPS)
    mean_ref[...] = jnp.broadcast_to(mean, mean_ref.shape)
    pair_row = lax.broadcasted_iota(jnp.int32, (AUX, AUX), 0)
    pair_col = lax.broadcasted_iota(jnp.int32, (AUX, AUX), 1)
    pair_fold = (pair_col >= traits) & (pair_col < traits + FOLDS)
    eye = lax.broadcasted_iota(jnp.int32, (width, width), 0) == lax.broadcasted_iota(
        jnp.int32, (width, width), 1
    )
    column_of = lambda line: jnp.sum(jnp.where(eye, line, 0.0), axis=1, keepdims=True)
    mean_col, scale_col = column_of(mean), column_of(scale)
    for j in range(2):
        sums = fold_lines(cross[j])
        pair = pairs[j]
        kept = jnp.sum(jnp.where(pair_fold & (pair_row == pair_col), pair, 0.0))
        trait_sums = jnp.sum(jnp.where(pair_fold, pair, 0.0), axis=1, keepdims=True)[:traits]
        half = slice(j * width, (j + 1) * width)
        mats[j] = scale_col * scale * (
            gram[:, half] - mean_col * sums - column_of(sums) * mean + kept * (mean_col * mean)
        )
        lines[j] = scale * (cross[j, :traits] - trait_sums * mean)
    for i in range(own - 1, -1, -1):
        shrink = jnp.minimum(first + i, systems - 1) - fold_of[i] * SHRINK
        penalty = jnp.float32(RATIOS[0] * width)
        for l in range(1, SHRINK):
            penalty = jnp.where(shrink == l, jnp.float32(RATIOS[l] * width), penalty)
        late = jnp.where(fold_of[i] != folds[0], 1, 0)
        mats[i + 2] = mats[late] + jnp.where(eye, penalty, 0.0)
        rhs[i] = lines[late]
    steps = width // PANEL
    for j in range(steps):
        here = slice(j * PANEL, (j + 1) * PANEL)
        rest = slice((j + 1) * PANEL, width)
        at = diag.at[j]
        for i in range(own):
            at[i] = mats[i + 2, here, here]

        def one(step, _):
            sweep_panel(at, own, pl.multiple_of(step * 8, 8), 8)
            return 0

        lax.fori_loop(0, PANEL // 8, one, 0)
        for i in range(own):
            right = -high_dot(rhs[i, :, here], at[i], ((1,), (0,)))
            rhs[i, :, here] = right
            if j + 1 < steps:
                tail = mats[i + 2, here, rest]
                solved = high_dot(at[i], tail, ((1,), (0,)))
                mats[i + 2, rest, rest] += high_dot(tail, solved, ((0,), (0,)))
                rhs[i, :, rest] -= high_dot(right, tail, ((1,), (0,)))
    for j in range(steps - 2, -1, -1):
        here = slice(j * PANEL, (j + 1) * PANEL)
        rest = slice((j + 1) * PANEL, width)
        for i in range(own):
            back = high_dot(rhs[i, :, rest], mats[i + 2, here, rest], ((1,), (1,)))
            rhs[i, :, here] += high_dot(back, diag[j, i], ((1,), (0,)))
    for i in range(own):
        coef_ref[i * traits : (i + 1) * traits] = (rhs[i] * scale).astype(jnp.bfloat16)


def solve_level0(sums, traits, count, rows):
    width = sums[0].shape[0]
    own = owned_systems(count)
    f32 = jnp.float32
    return plain(
        functools.partial(solve_kernel, FOLDS * SHRINK, own, count * rows),
        (
            jax.ShapeDtypeStruct((own * traits, width), jnp.bfloat16),
            jax.ShapeDtypeStruct((8, width), f32),
        ),
        "solve_level0",
        *sums,
        scratch=[
            pltpu.VMEM((own + 2, width, width), f32),
            pltpu.VMEM((own, traits, width), f32),
            pltpu.VMEM((2, traits, width), f32),
            pltpu.VMEM((width // PANEL, own, PANEL, PANEL), f32),
        ],
    )


def predict(coef, mean, x, folds, o_ref):
    parts, _, group, _ = o_ref.shape
    traits = parts * group
    per_fold = SHRINK * traits
    coef = coef[: FOLDS * per_fold]
    raw = lax.dot_general(
        coef, x, (((1,), (1,)), ((), ())), preferred_element_type=jnp.float32
    )
    shift = jnp.sum(coef.astype(jnp.float32) * mean, axis=1, keepdims=True)
    raw = raw - shift
    out = jnp.zeros((per_fold, raw.shape[1]), jnp.float32)
    for k in range(FOLDS):
        out = jnp.where(folds == k, raw[k * per_fold : (k + 1) * per_fold], out)
    for g in range(parts):
        for l in range(SHRINK):
            o_ref[g, l] = out[l * traits + g * group : l * traits + (g + 1) * group]


def level_kernel(
    depth, blk, coef_ref, mean_ref, x_ref, traits_ref, folds_ref,
    p_ref, f_ref, sum_ref,
    coefs, sent, part, arrived,
    send_line, send_pair, recv, send_blk, recv_blk, send_sum, recv_sum,
):
    count = 2 * depth
    me = lax.axis_index("samp")
    here = lax.axis_index("blk")
    z, x = me // 2, lax.rem(me, 2)
    partner = z * 2 + 1 - x
    barrier = pltpu.get_barrier_semaphore()
    for axis, size, at in (("samp", count, me), ("blk", blk, here)):
        for step in range(1, size):
            pl.semaphore_signal(
                barrier,
                inc=1,
                device_id={axis: lax.rem(at + step, size)},
                device_id_type=MESH,
            )
    coefs[me] = coef_ref[...]
    pl.semaphore_wait(barrier, count + blk - 2)

    def coef_copy(slot, sem, target):
        return pltpu.make_async_remote_copy(
            src_ref=coefs.at[slot],
            dst_ref=coefs.at[slot],
            send_sem=sem,
            recv_sem=recv.at[slot],
            device_id={"samp": target},
            device_id_type=MESH,
        )

    mate = lambda step: lax.rem(z + step, depth) * 2 + x
    for step in range(1, depth):
        coef_copy(me, send_line.at[step], mate(step)).start()
    coef_copy(me, send_pair.at[0], partner).start()
    for step in range(1, depth):
        coef_copy(mate(step), send_pair.at[0], partner).wait_recv()
        coef_copy(mate(step), send_pair.at[step], partner).start()
    for step in range(depth):
        slot = lax.rem(z + step, depth) * 2 + 1 - x
        coef_copy(slot, send_pair.at[0], partner).wait_recv()
    predict(
        coefs[...].reshape(-1, coefs.shape[2]),
        mean_ref[:1],
        x_ref[...],
        folds_ref[...],
        sent,
    )

    def pred_copy(step, slot):
        other = lax.rem(here + step, blk)
        return pltpu.make_async_remote_copy(
            src_ref=sent.at[other],
            dst_ref=p_ref.at[slot],
            send_sem=send_blk.at[step],
            recv_sem=recv_blk.at[slot],
            device_id={"blk": other},
            device_id_type=MESH,
        )

    for step in range(1, blk):
        pred_copy(step, here).start()
    p_ref[here] = sent[here]
    for step in range(1, depth):
        coef_copy(me, send_line.at[step], partner).wait_send()
    for step in range(depth):
        coef_copy(me, send_pair.at[step], partner).wait_send()
    for step in range(1, blk):
        pred_copy(step, lax.rem(here + step, blk)).wait()
    moments(p_ref, traits_ref, folds_ref, f_ref, part.at[0])
    stages = part.shape[0]
    copies = []
    for stage in range(stages):
        bit = 2**stage
        other = me + bit - 2 * bit * lax.rem(me // bit, 2)
        copy = pltpu.make_async_remote_copy(
            src_ref=part.at[stage],
            dst_ref=arrived.at[stage],
            send_sem=send_sum.at[stage],
            recv_sem=recv_sum.at[stage],
            device_id={"samp": other},
            device_id_type=MESH,
        )
        copy.start()
        copies.append(copy)
        copy.wait_recv()
        summed = part[stage] + arrived[stage]
        if stage + 1 < stages:
            part[stage + 1] = summed
        else:
            sum_ref[...] = summed
    for copy in copies:
        copy.wait_send()


def moments(p_ref, traits_ref, folds_ref, f_ref, e_ref):
    blocks, shrinks, group, rows = p_ref.shape
    preds = blocks * shrinks
    f_ref[...] = jnp.zeros_like(f_ref)
    for t in range(group):
        base = t * ROWS1
        for b in range(blocks):
            for l in range(shrinks):
                at = base + b * shrinks + l
                f_ref[at : at + 1] = p_ref[b, l, t : t + 1]
        f_ref[base + preds : base + preds + 1] = traits_ref[t : t + 1]
        f_ref[base + preds + 1 : base + preds + 2] = jnp.ones((1, rows), jnp.float32)
    f = f_ref[...]
    size = group * ROWS1
    folds = folds_ref[...]
    lane = lax.broadcasted_iota(jnp.int32, (ROWS1, size), 1)
    for k in range(FOLDS):
        full = high_dot(jnp.where(folds == k, f, 0.0), f, ((1,), (1,)))
        packed = jnp.zeros((ROWS1, size), jnp.float32)
        for t in range(group):
            inside = (lane >= t * ROWS1) & (lane < (t + 1) * ROWS1)
            packed = jnp.where(inside, full[t * ROWS1 : (t + 1) * ROWS1], packed)
        e_ref[k * ROWS1 : (k + 1) * ROWS1] = packed


def blend_kernel(total, e_ref, f_ref, p_ref, folds_ref, level_ref, blend_ref, mats):
    blocks, shrinks, group, rows = p_ref.shape
    preds = blocks * shrinks
    summed = e_ref[...]
    shape = (ROWS1, ROWS1)
    row = lax.broadcasted_iota(jnp.int32, shape, 0)
    col = lax.broadcasted_iota(jnp.int32, shape, 1)
    col_in = lax.broadcasted_iota(jnp.int32, (ROWS1, 1), 0) < preds
    row_in = lax.broadcasted_iota(jnp.int32, (1, ROWS1), 1) < preds
    one_lane = lax.broadcasted_iota(jnp.int32, (1, ROWS1), 1) == preds + 1
    ridge = jnp.where((row == col) & (row < preds), total / 4.0, 0.0)
    own = [
        [
            summed[k * ROWS1 : (k + 1) * ROWS1, t * ROWS1 : (t + 1) * ROWS1]
            for k in range(FOLDS)
        ]
        for t in range(group)
    ]
    means, scales = [], []
    for t in range(group):
        full = own[t][0]
        for k in range(1, FOLDS):
            full = full + own[t][k]
        mean_row = jnp.where(row_in, full[preds + 1 : preds + 2] / total, 0.0)
        mean_col = jnp.where(col_in, full[:, preds + 1 : preds + 2] / total, 0.0)
        square = jnp.where(row == col, full, 0.0) / total
        sq_row = jnp.sum(square, axis=0, keepdims=True)
        sq_col = jnp.sum(square, axis=1, keepdims=True)
        scale_row = jnp.where(row_in, lax.rsqrt(sq_row - mean_row * mean_row + EPS), 1.0)
        scale_col = jnp.where(col_in, lax.rsqrt(sq_col - mean_col * mean_col + EPS), 1.0)
        means.append((mean_row, mean_col))
        scales.append((scale_row, scale_col))
        for k in range(FOLDS):
            train = full - own[t][k]
            sums_row = train[preds + 1 : preds + 2]
            sums_col = train[:, preds + 1 : preds + 2]
            kept = train[preds + 1 : preds + 2, preds + 1 : preds + 2]
            centered = (
                train - mean_col * sums_row - sums_col * mean_row + kept * (mean_col * mean_row)
            )
            mats[t * FOLDS + k] = scale_col * scale_row * centered + ridge
    for b in range(blocks):
        for l in range(shrinks):
            at = b * shrinks + l
            means_at = jnp.concatenate([means[t][1][at : at + 1] for t in range(group)], axis=0)
            scales_at = jnp.concatenate([scales[t][1][at : at + 1] for t in range(group)], axis=0)
            level_ref[b, l] = (p_ref[b, l] - means_at) * scales_at

    for start in range(0, preds, 8):
        sweep_panel(mats, group * FOLDS, start, min(8, preds - start))
    folds = folds_ref[...]
    for t in range(group):
        mean_row, scale_row = means[t][0], scales[t][0]
        lines = []
        first = jnp.zeros((1, 1), jnp.float32)
        second = jnp.zeros((1, 1), jnp.float32)
        for k in range(FOLDS):
            line = jnp.where(row_in, mats[t * FOLDS + k, preds : preds + 1, :] * scale_row, 0.0)
            offset = jnp.sum(line * mean_row, axis=1, keepdims=True)
            line = jnp.where(one_lane, -offset, line)
            lines.append(line)
            product = jnp.sum(own[t][k] * line, axis=1, keepdims=True)
            line_col = jnp.sum(jnp.where(row == col, line, 0.0), axis=1, keepdims=True)
            first = first + product[preds + 1 : preds + 2]
            second = second + jnp.sum(product * line_col, axis=0, keepdims=True)
        lines.append(jnp.zeros((8 - FOLDS, ROWS1), jnp.float32))
        every = high_dot(
            jnp.concatenate(lines, axis=0),
            f_ref[t * ROWS1 : (t + 1) * ROWS1],
            ((1,), (0,)),
        )
        p = jnp.zeros((1, rows), jnp.float32)
        for k in range(FOLDS):
            p = jnp.where(folds == k, every[k : k + 1], p)
        mean = first / total
        spread_of = second / total - mean * mean
        blend_ref[t : t + 1] = (p - mean) * lax.rsqrt(spread_of + EPS)


def plain(kernel, out_shape, name, *args, scratch=()):
    return pl.pallas_call(
        kernel,
        out_shape=out_shape,
        in_specs=[VMEM] * len(args),
        out_specs=jax.tree.map(lambda _: VMEM, out_shape),
        scratch_shapes=list(scratch),
        compiler_params=pltpu.CompilerParams(vmem_limit_bytes=LIMIT),
        name=name,
    )(*args)


def fast(samp, blk, dosages, traits, folds):
    rows, width = dosages.shape
    count_traits = traits.shape[0]
    group = count_traits // blk
    f32 = jnp.float32
    fold_ids = jnp.arange(AUX - count_traits, dtype=jnp.int32)
    one_hot = (folds[None, :] == fold_ids[:, None]).astype(jnp.bfloat16)
    aux = jnp.concatenate([traits, one_hot], axis=0)
    folds_row = folds[None, :]
    own_traits = lax.dynamic_slice_in_dim(
        traits, lax.axis_index("blk") * group, group, 0
    ).astype(f32)
    sums = gather_grams(dosages, aux, samp, count_traits)
    coef, mean = solve_level0(sums, count_traits, samp, rows)
    shape = jax.ShapeDtypeStruct((blk, SHRINK, group, rows), f32)
    size = group * ROWS1
    own = owned_systems(samp) * count_traits
    depth = samp // 2
    stages = samp.bit_length() - 1
    dma = pltpu.SemaphoreType.DMA
    pred, stacked, moment_sums = pl.pallas_call(
        functools.partial(level_kernel, depth, blk),
        out_shape=(
            shape,
            jax.ShapeDtypeStruct((size, rows), f32),
            jax.ShapeDtypeStruct((FOLDS * ROWS1, size), f32),
        ),
        in_specs=[VMEM] * 5,
        out_specs=(VMEM,) * 3,
        scratch_shapes=[
            pltpu.VMEM((samp, own, width), jnp.bfloat16),
            pltpu.VMEM(shape.shape, f32),
            pltpu.VMEM((stages, FOLDS * ROWS1, size), f32),
            pltpu.VMEM((stages, FOLDS * ROWS1, size), f32),
            dma((depth,)),
            dma((depth,)),
            dma((samp,)),
            dma((blk,)),
            dma((blk,)),
            dma((stages,)),
            dma((stages,)),
        ],
        compiler_params=pltpu.CompilerParams(
            collective_id=1, has_side_effects=True, vmem_limit_bytes=LIMIT
        ),
        name="predict_level0",
    )(coef, mean, dosages, own_traits, folds_row)
    level0, blend = plain(
        functools.partial(blend_kernel, float(samp * rows)),
        (shape, jax.ShapeDtypeStruct((group, rows), f32)),
        "blend",
        moment_sums,
        stacked,
        pred,
        folds_row,
        scratch=[pltpu.VMEM((group * FOLDS, ROWS1, ROWS1), f32)],
    )
    return level0, blend


def solution(mesh):
    in_specs = (P("samp", "blk"), P(None, "samp"), P("samp"))
    out_specs = (P(None, None, "blk", "samp"), P("blk", "samp"))
    samp, blk = mesh.shape["samp"], mesh.shape["blk"]
    body = functools.partial(fast, samp, blk) if samp == 8 else shards
    return jax.shard_map(body, mesh=mesh, in_specs=in_specs, out_specs=out_specs, check_vma=False)
```

```python
import functools

import jax
import jax.numpy as jnp
from jax import lax
from jax.experimental import pallas as pl
from jax.experimental.pallas import tpu as pltpu
from jax.sharding import PartitionSpec as P

FOLDS = 5
SHRINK = 5


RATIOS = (99.0, 3.0, 1.0, 1.0 / 3.0, 1.0 / 99.0)
EPS = 1e-05
HIGH = lax.Precision.HIGHEST


def solve_batch(systems, right_sides):
    factors = jnp.linalg.cholesky(systems)

    def solve_single(factor, right_side):
        return jax.scipy.linalg.cho_solve((factor, True), right_side)

    return jax.vmap(solve_single)(factors, right_sides)


def shards(dosages, traits, folds):
    rows, width = dosages.shape
    traits_count = traits.shape[0]
    fold_ids = jnp.arange(FOLDS, dtype=jnp.int32)
    masks = (folds[None, :] == fold_ids[:, None]).astype(jnp.float32)
    mask_half = masks.astype(jnp.bfloat16)
    traits_wide = traits.astype(jnp.float32)
    grams = []
    crosses = []
    for fold in range(FOLDS):
        weighted = dosages * mask_half[fold][:, None]
        grams.append(jnp.einsum("ri,rj->ij", dosages, weighted, preferred_element_type=jnp.float32))
        crosses.append(
            jnp.dot(traits * mask_half[fold][None, :], dosages, preferred_element_type=jnp.float32)
        )
    gram = jnp.stack(grams)
    cross = jnp.stack(crosses)
    sums = jnp.dot(mask_half, dosages, preferred_element_type=jnp.float32)
    counts = jnp.sum(masks, axis=1)
    trait_sums = jnp.einsum("ks,ts->kt", masks, traits_wide, precision=HIGH)
    gram, sums, cross, counts, trait_sums = lax.psum(
        (gram, sums, cross, counts, trait_sums), "samp"
    )
    total = jnp.sum(counts)
    mean = jnp.sum(sums, axis=0) / total
    gram_total = jnp.sum(gram, axis=0)
    variance = jnp.diagonal(gram_total) / total - mean * mean
    scale = lax.rsqrt(variance + EPS)
    sums_total = jnp.sum(sums, axis=0)
    cross_total = jnp.sum(cross, axis=0)
    trait_total = jnp.sum(trait_sums, axis=0)
    ratios = jnp.array(RATIOS, dtype=jnp.float32)
    identity = jnp.eye(width, dtype=jnp.float32)

    def train_system(fold):
        train_gram = gram_total - lax.dynamic_index_in_dim(gram, fold, 0, keepdims=False)
        train_sums = sums_total - lax.dynamic_index_in_dim(sums, fold, 0, keepdims=False)
        train_count = total - lax.dynamic_index_in_dim(counts, fold, 0, keepdims=False)
        train_cross = cross_total - lax.dynamic_index_in_dim(cross, fold, 0, keepdims=False)
        train_traits = trait_total - lax.dynamic_index_in_dim(trait_sums, fold, 0, keepdims=False)
        centered = (
            train_gram
            - mean[:, None] * train_sums[None, :]
            - train_sums[:, None] * mean[None, :]
            + train_count * mean[:, None] * mean[None, :]
        )
        system = scale[:, None] * centered * scale[None, :]
        target = scale[:, None] * (train_cross.T - mean[:, None] * train_traits[None, :])
        return (system, target)

    systems_count = FOLDS * SHRINK
    per_device = -(-systems_count // lax.axis_size("samp"))
    first = lax.axis_index("samp") * per_device

    def solve_own(offset):
        which = jnp.minimum(first + offset, systems_count - 1)
        fold = which // SHRINK
        shrink = which - fold * SHRINK
        system, target = train_system(fold)
        penalty = jnp.sum(
            jnp.where(jnp.arange(SHRINK, dtype=jnp.int32) == shrink, ratios * width, 0.0)
        )
        beta = solve_batch((system + penalty * identity)[None], target[None])[0]
        return (scale[:, None] * beta).astype(jnp.bfloat16)

    owned = lax.map(solve_own, jnp.arange(per_device, dtype=jnp.int32))
    collected = lax.all_gather(owned, "samp", axis=0, tiled=True)
    coef = collected[:systems_count].reshape(FOLDS, SHRINK, width, traits_count)
    coef_flat = coef.transpose(2, 0, 1, 3).reshape(width, FOLDS * SHRINK * traits_count)
    shift = jnp.einsum("v,klvt->klt", mean, coef.astype(jnp.float32), precision=HIGH)
    raw = jnp.einsum("vc,rv->cr", coef_flat, dosages, preferred_element_type=jnp.float32)
    outcome = raw.reshape(FOLDS, SHRINK, traits_count, rows) - shift[..., None]
    level_pred = jnp.einsum("kltr,kr->ltr", outcome, masks, precision=HIGH)
    group = traits_count // lax.axis_size("blk")
    start = lax.axis_index("blk") * group
    own_traits = lax.dynamic_slice_in_dim(traits_wide, start, group, 0)
    own_sums = lax.dynamic_slice_in_dim(trait_sums, start, group, 1)
    arrived = lax.all_to_all(level_pred[None], "blk", split_axis=2, concat_axis=0, tiled=True)
    count_pred = arrived.shape[0] * arrived.shape[1]
    flat = arrived.reshape(count_pred, group, rows)
    raw_grams = jnp.einsum("ks,ats,bts->ktab", masks, flat, flat, precision=HIGH)
    raw_cross = jnp.einsum("ks,ats,ts->kta", masks, flat, own_traits, precision=HIGH)
    raw_sums = jnp.einsum("ks,ats->kta", masks, flat, precision=HIGH)
    raw_grams, raw_cross, raw_sums = lax.psum((raw_grams, raw_cross, raw_sums), "samp")
    pred_mean = jnp.sum(raw_sums, axis=0) / total
    pred_sq = jnp.diagonal(jnp.sum(raw_grams, axis=0), axis1=1, axis2=2)
    pred_scale = lax.rsqrt(pred_sq / total - pred_mean * pred_mean + EPS)
    standard = (flat - pred_mean.T[:, :, None]) * pred_scale.T[:, :, None]
    outer_scale = pred_scale[None, :, :, None] * pred_scale[None, :, None, :]
    fold_grams = outer_scale * (
        raw_grams
        - pred_mean[None, :, :, None] * raw_sums[:, :, None, :]
        - raw_sums[:, :, :, None] * pred_mean[None, :, None, :]
        + counts[:, None, None, None] * pred_mean[None, :, :, None] * pred_mean[None, :, None, :]
    )
    fold_cross = pred_scale[None] * (raw_cross - pred_mean[None] * own_sums[:, :, None])
    level0 = standard.reshape(arrived.shape)
    train_grams = jnp.sum(fold_grams, axis=0)[None] - fold_grams
    train_cross = jnp.sum(fold_cross, axis=0)[None] - fold_cross
    shrunk = train_grams + total / 4.0 * jnp.eye(count_pred, dtype=jnp.float32)
    weights = solve_batch(
        shrunk.reshape(-1, count_pred, count_pred), train_cross.reshape(-1, count_pred)
    )
    weights = weights.reshape(FOLDS, group, count_pred)
    every_fold = jnp.einsum("ats,kta->kts", standard, weights, precision=HIGH)
    blended = jnp.einsum("kts,ks->ts", every_fold, masks, precision=HIGH)
    blend_sum, blend_sq = lax.psum(
        (jnp.sum(blended, axis=-1), jnp.sum(blended * blended, axis=-1)), "samp"
    )
    blend_mean = blend_sum / total
    blend_var = blend_sq / total - blend_mean * blend_mean
    blend = (blended - blend_mean[:, None]) * lax.rsqrt(blend_var + EPS)[:, None]
    return (level0, blend)


MESH = pl.DeviceIdType.MESH
AUX = 32
ROWS1 = 24
PANEL = 128
LIMIT = 48 * 1024 * 1024
VMEM = pl.BlockSpec(memory_space=pltpu.VMEM)
HBM = pl.BlockSpec(memory_space=pltpu.HBM)


def high_dot(a, b, dims):
    return lax.dot_general(
        a, b, (dims, ((), ())), precision=HIGH, preferred_element_type=jnp.float32
    )


def greet(axis, count):
    barrier = pltpu.get_barrier_semaphore()
    me = lax.axis_index(axis)
    for step in range(1, count):
        pl.semaphore_signal(
            barrier, inc=1, device_id={axis: lax.rem(me + step, count)}, device_id_type=MESH
        )
    pl.semaphore_wait(barrier, count - 1)


def ranked(z, depth, rank):
    near = jnp.minimum(z, depth - 1 - z)
    both = jnp.where(lax.rem(rank, 2) == 1, z - (rank + 1) // 2, z + rank // 2)
    one = jnp.where(z < depth - 1 - z, z + rank - near, z - rank + near)
    return jnp.where(rank <= 2 * near, both, one)


def gram_kernel(
    depth, own_systems, x_ref, traits_ref, folds_ref,
    gram, cross, pairs, all_aux, sq,
    xs, auxs, send_up, send_down, send_pair, recv, asend, arecv, own, send_extra, recv_half,
):
    me = lax.axis_index("samp")
    z, x = me // 2, lax.rem(me, 2)
    partner = z * 2 + 1 - x
    count = 2 * depth
    is_end = (z == 0) | (z == depth - 1)
    is_middle = (z > 0) & (z < depth - 1)
    far = jnp.where(z < depth // 2, depth - 1, 0)
    near = depth - 1 - far
    half = xs.shape[1] // 2
    keep = pltpu.make_async_copy(x_ref, xs.at[me], own)
    keep.start()
    traits = traits_ref.shape[0]
    fold_id = lax.broadcasted_iota(jnp.int32, (AUX - traits, xs.shape[1]), 0)
    auxs[me, :traits] = traits_ref[...]
    auxs[me, traits:] = jnp.where(folds_ref[...] == fold_id, 1.0, 0.0).astype(jnp.bfloat16)
    greet("samp", count)

    def x_copy(slot, sem, target):
        return pltpu.make_async_remote_copy(
            src_ref=xs.at[slot],
            dst_ref=xs.at[slot],
            send_sem=sem,
            recv_sem=recv.at[slot],
            device_id={"samp": target},
            device_id_type=MESH,
        )

    def half_copy(slot, part, send_sem, recv_sem, target):
        piece = xs.at[slot, pl.ds(part * half, half)]
        return pltpu.make_async_remote_copy(
            src_ref=piece,
            dst_ref=piece,
            send_sem=send_sem,
            recv_sem=recv_sem,
            device_id={"samp": target},
            device_id_type=MESH,
        )

    def to_pair(rank, layer, slot, act):
        @pl.when((is_end & (layer != far)) | (is_middle & (layer != near)))
        def _():
            act(x_copy(slot, send_pair.at[rank], partner))

        @pl.when(is_end & (layer == far))
        def _():
            act(half_copy(slot, 1, send_pair.at[rank], recv.at[slot], partner))

    def extra(act):
        target = jnp.where((z == 0) | ((z != depth - 1) & (z >= depth // 2)), me + 2, me - 2)

        @pl.when(is_end)
        def _():
            act(x_copy(partner, send_extra.at[0], target))

        @pl.when(is_middle)
        def _():
            slot = far * 2 + 1 - x
            act(half_copy(slot, 0, send_extra.at[0], recv_half.at[0], target))

    def aux_copy(step, slot):
        other = lax.rem(me + step, count)
        return pltpu.make_async_remote_copy(
            src_ref=auxs.at[slot],
            dst_ref=auxs.at[slot],
            send_sem=asend.at[step],
            recv_sem=arecv.at[slot],
            device_id={"samp": other},
            device_id_type=MESH,
        )

    keep.wait()
    _, width = gram.shape
    width = width // 2
    rows = xs.shape[1]
    folds = owned_folds(own_systems, FOLDS * SHRINK)
    aux_row = lax.broadcasted_iota(jnp.int32, (AUX, width), 0)
    fold_rows = (aux_row >= traits) & (aux_row < traits + FOLDS)
    picks = jnp.concatenate(
        [
            jnp.where(fold_rows & (aux_row != traits + fold), 1.0, 0.0).astype(jnp.bfloat16)
            for fold in folds
        ],
        axis=1,
    )
    row_id = lax.broadcasted_iota(jnp.int32, (AUX, rows), 0)

    def forward(rank, layer, slot):
        @pl.when((layer <= z) & (z + 1 < depth))
        def _():
            x_copy(slot, send_up.at[rank], me + 2).start()

        @pl.when((layer >= z) & (z >= 1))
        def _():
            x_copy(slot, send_down.at[rank], me - 2).start()

        to_pair(rank, layer, slot, lambda copy: copy.start())

    forward(0, z, me)
    for step in range(1, count):
        aux_copy(step, me).start()
    for ref in (gram, cross, pairs, all_aux, sq):
        ref[...] = jnp.zeros_like(ref)

    def add_block(i, _):
        body = i < 2 * depth - 2
        swap = is_end & (i >= 2) & body
        i_first = i
        i = jnp.where(swap, i + 1 - 2 * lax.rem(i, 2), i)
        is_column = (i < 2) | (body & (lax.rem(i, 2) == 0))
        column_rank = jnp.where(i < 2, i, i // 2 + 1)
        pair_rank = jnp.where(body, (i - 3) // 2, i - depth)
        rank = jnp.where(is_column, column_rank, pair_rank)
        layer = ranked(z, depth, rank)
        slot = layer * 2 + jnp.where(is_column, x, 1 - x)

        @pl.when(i_first > 0)
        def _():
            cut = is_end & jnp.logical_not(is_column) & (layer == far)

            @pl.when(jnp.logical_not(cut))
            def _():
                x_copy(slot, send_pair.at[0], partner).wait_recv()

            @pl.when(cut)
            def _():
                half_copy(slot, 1, send_pair.at[0], recv.at[slot], partner).wait_recv()
                half_copy(slot, 0, send_pair.at[0], recv_half.at[0], partner).wait_recv()

            @pl.when(is_column)
            def _():
                forward(rank, layer, slot)

            @pl.when(jnp.logical_not(is_column) & (layer == jnp.where(is_end, z, far)))
            def _():
                extra(lambda copy: copy.start())

            aux_copy(1, slot).wait_recv()

        block = xs[slot]
        aux = auxs[slot]
        aux_wide = aux.astype(jnp.float32)
        keep = lax.dot_general(
            aux, picks, (((0,), (0,)), ((), ())), preferred_element_type=jnp.float32
        ).astype(jnp.bfloat16)
        weighted = jnp.concatenate([block, block], axis=1) * keep
        gram[...] += lax.dot_general(
            block, weighted, (((0,), (0,)), ((), ())), preferred_element_type=jnp.float32
        )
        all_aux[...] += jnp.dot(aux, block, preferred_element_type=jnp.float32)
        wide = block.astype(jnp.float32)
        sq[...] += jnp.sum(wide * wide, axis=0, keepdims=True)
        for j, fold in enumerate(folds):
            held = jnp.sum(jnp.where(row_id == traits + fold, aux_wide, 0.0), axis=0, keepdims=True)
            aux_train = (aux_wide * (1.0 - held)).astype(jnp.bfloat16)
            cross[j] += jnp.dot(aux_train, block, preferred_element_type=jnp.float32)
            pairs[j] += lax.dot_general(
                aux_train, aux, (((1,), (1,)), ((), ())), preferred_element_type=jnp.float32
            )
        return 0

    lax.fori_loop(0, count, add_block, 0)
    for step in range(1, count):
        aux_copy(step, me).wait_send()
    for rank in range(depth):
        layer = ranked(z, depth, jnp.int32(rank))
        slot = layer * 2 + x

        @pl.when((layer <= z) & (z + 1 < depth))
        def _():
            x_copy(slot, send_up.at[rank], partner).wait_send()

        @pl.when((layer >= z) & (z >= 1))
        def _():
            x_copy(slot, send_down.at[rank], partner).wait_send()

        to_pair(rank, layer, slot, lambda copy: copy.wait_send())
    extra(lambda copy: copy.wait_send())


def owned_systems(count):
    return -(-FOLDS * SHRINK // count)


def owned_folds(own, systems):
    first = lax.axis_index("samp") * own
    return [jnp.minimum(first + i, systems - 1) // SHRINK for i in (0, own - 1)]


def gather_grams(x, traits, folds, count):
    rows, width = x.shape
    f32 = jnp.float32
    depth = count // 2
    return pl.pallas_call(
        functools.partial(gram_kernel, depth, owned_systems(count)),
        out_shape=(
            jax.ShapeDtypeStruct((width, 2 * width), f32),
            jax.ShapeDtypeStruct((2, AUX, width), f32),
            jax.ShapeDtypeStruct((2, AUX, AUX), f32),
            jax.ShapeDtypeStruct((AUX, width), f32),
            jax.ShapeDtypeStruct((1, width), f32),
        ),
        in_specs=[HBM, VMEM, VMEM],
        out_specs=(VMEM,) * 5,
        scratch_shapes=[
            pltpu.VMEM((count, rows, width), x.dtype),
            pltpu.VMEM((count, AUX, rows), traits.dtype),
            pltpu.SemaphoreType.DMA((depth,)),
            pltpu.SemaphoreType.DMA((depth,)),
            pltpu.SemaphoreType.DMA((depth,)),
            pltpu.SemaphoreType.DMA((count,)),
            pltpu.SemaphoreType.DMA((count,)),
            pltpu.SemaphoreType.DMA((count,)),
            pltpu.SemaphoreType.DMA,
            pltpu.SemaphoreType.DMA((1,)),
            pltpu.SemaphoreType.DMA((1,)),
        ],
        compiler_params=pltpu.CompilerParams(
            collective_id=0, has_side_effects=True, vmem_limit_bytes=LIMIT
        ),
        name="gather_grams",
    )(x, traits, folds)


def split_three(a):
    high = a.astype(jnp.bfloat16).astype(jnp.float32)
    rest = a - high
    middle = rest.astype(jnp.bfloat16).astype(jnp.float32)
    return high, middle, rest - middle


def thin_product(left, right):
    a, b, c = split_three(left)
    d, e, f = split_three(right)
    return lax.dot_general(
        jnp.concatenate([c, a, b, a, b, a], axis=0).astype(jnp.bfloat16),
        jnp.concatenate([d, f, e, e, d, d], axis=0).astype(jnp.bfloat16),
        (((0,), (0,)), ((), ())),
        preferred_element_type=jnp.float32,
    )


def sweep_panel(m_ref, batch, start, pivots):
    size, lanes = m_ref.shape[1:]
    sub = lax.broadcasted_iota(jnp.int32, (8, lanes), 0)
    lane = lax.broadcasted_iota(jnp.int32, (8, lanes), 1) - start
    inside = (lane >= 0) & (lane < pivots)
    unit = jnp.where(lane == sub, 1.0, 0.0)
    panels = [m_ref[b, pl.ds(start, 8), :] for b in range(batch)]
    if isinstance(start, int):
        turned, first = panels, start
    else:
        turned, first = [pltpu.roll(p, lanes - start, 1) for p in panels], 0
    columns = [
        [jnp.broadcast_to(p[:, first + j : first + j + 1], (8, lanes)) for j in range(pivots)]
        for p in turned
    ]
    solved = [jnp.where(inside, unit, p) for p in panels]
    for p in range(0, pivots, 2):
        q = p + 1
        at_p, at_q = sub == p, sub == q
        for b in range(batch):
            one, two = columns[b][p], columns[b][q]
            pp, pq = one[p : p + 1], two[p : p + 1]
            qp, qq = one[q : q + 1], two[q : q + 1]
            inverse = 1.0 / (pp * qq - pq * qp)

            def eliminate(t):
                tp, tq = t[p : p + 1], t[q : q + 1]
                up = (qq * tp - pq * tq) * inverse
                uq = (pp * tq - qp * tp) * inverse
                return jnp.where(at_p, up, jnp.where(at_q, uq, t - one * up - two * uq))

            solved[b] = eliminate(solved[b])
            for j in range(q + 1, pivots):
                columns[b][j] = eliminate(columns[b][j])
    row = lax.broadcasted_iota(jnp.int32, (size, lanes), 0) - start
    col = lax.broadcasted_iota(jnp.int32, (size, lanes), 1) - start
    cross = ((row >= 0) & (row < pivots)) | ((col >= 0) & (col < pivots))
    for b in range(batch):
        left = jnp.where(inside, -unit, panels[b])
        right = jnp.where(inside, -solved[b], solved[b])
        if pivots < 8:
            left = jnp.where(sub < pivots, left, 0.0)
            right = jnp.where(sub < pivots, right, 0.0)
        m_ref[b] = jnp.where(cross, 0.0, m_ref[b]) - thin_product(left, right)


def solve_kernel(
    systems, own, total, gram, cross, pairs, all_aux, sq, coef_ref, mean_ref, mats, rhs, lines, diag
):
    width = gram.shape[0]
    traits = coef_ref.shape[0] // own
    first = lax.axis_index("samp") * own
    fold_of = [jnp.minimum(first + i, systems - 1) // SHRINK for i in range(own)]
    folds = owned_folds(own, systems)
    aux_row = lax.broadcasted_iota(jnp.int32, (AUX, width), 0)
    fold_rows = (aux_row >= traits) & (aux_row < traits + FOLDS)
    fold_lines = lambda a: jnp.sum(jnp.where(fold_rows, a, 0.0), axis=0, keepdims=True)
    mean = fold_lines(all_aux[...]) / total
    scale = lax.rsqrt(sq[...] / total - mean * mean + EPS)
    mean_ref[...] = jnp.broadcast_to(mean, mean_ref.shape)
    pair_row = lax.broadcasted_iota(jnp.int32, (AUX, AUX), 0)
    pair_col = lax.broadcasted_iota(jnp.int32, (AUX, AUX), 1)
    pair_fold = (pair_col >= traits) & (pair_col < traits + FOLDS)
    eye = lax.broadcasted_iota(jnp.int32, (width, width), 0) == lax.broadcasted_iota(
        jnp.int32, (width, width), 1
    )
    column_of = lambda line: jnp.sum(jnp.where(eye, line, 0.0), axis=1, keepdims=True)
    mean_col, scale_col = column_of(mean), column_of(scale)
    for j in range(2):
        sums = fold_lines(cross[j])
        pair = pairs[j]
        kept = jnp.sum(jnp.where(pair_fold & (pair_row == pair_col), pair, 0.0))
        trait_sums = jnp.sum(jnp.where(pair_fold, pair, 0.0), axis=1, keepdims=True)[:traits]
        half = slice(j * width, (j + 1) * width)
        mats[j] = scale_col * scale * (
            gram[:, half] - mean_col * sums - column_of(sums) * mean + kept * (mean_col * mean)
        )
        lines[j] = scale * (cross[j, :traits] - trait_sums * mean)
    for i in range(own - 1, -1, -1):
        shrink = jnp.minimum(first + i, systems - 1) - fold_of[i] * SHRINK
        penalty = jnp.float32(RATIOS[0] * width)
        for l in range(1, SHRINK):
            penalty = jnp.where(shrink == l, jnp.float32(RATIOS[l] * width), penalty)
        late = jnp.where(fold_of[i] != folds[0], 1, 0)
        mats[i + 2] = mats[late] + jnp.where(eye, penalty, 0.0)
        rhs[i] = lines[late]
    steps = width // PANEL
    for j in range(steps):
        here = slice(j * PANEL, (j + 1) * PANEL)
        rest = slice((j + 1) * PANEL, width)
        at = diag.at[j]
        for i in range(own):
            at[i] = mats[i + 2, here, here]

        def one(step, _):
            sweep_panel(at, own, pl.multiple_of(step * 8, 8), 8)
            return 0

        lax.fori_loop(0, PANEL // 8, one, 0)
        for i in range(own):
            right = -high_dot(rhs[i, :, here], at[i], ((1,), (0,)))
            rhs[i, :, here] = right
            if j + 1 < steps:
                tail = mats[i + 2, here, rest]
                solved = high_dot(at[i], tail, ((1,), (0,)))
                for at_row in range((j + 1) * PANEL, width, PANEL):
                    lead = at_row - (j + 1) * PANEL
                    mats[i + 2, at_row : at_row + PANEL, at_row:] += high_dot(
                        tail[:, lead : lead + PANEL], solved[:, lead:], ((0,), (0,))
                    )
                rhs[i, :, rest] -= high_dot(right, tail, ((1,), (0,)))
    for j in range(steps - 2, -1, -1):
        here = slice(j * PANEL, (j + 1) * PANEL)
        rest = slice((j + 1) * PANEL, width)
        for i in range(own):
            back = high_dot(rhs[i, :, rest], mats[i + 2, here, rest], ((1,), (1,)))
            rhs[i, :, here] += high_dot(back, diag[j, i], ((1,), (0,)))
    for i in range(own):
        coef_ref[i * traits : (i + 1) * traits] = (rhs[i] * scale).astype(jnp.bfloat16)


def solve_level0(sums, traits, count, rows):
    width = sums[0].shape[0]
    own = owned_systems(count)
    f32 = jnp.float32
    return plain(
        functools.partial(solve_kernel, FOLDS * SHRINK, own, count * rows),
        (
            jax.ShapeDtypeStruct((own * traits, width), jnp.bfloat16),
            jax.ShapeDtypeStruct((8, width), f32),
        ),
        "solve_level0",
        *sums,
        scratch=[
            pltpu.VMEM((own + 2, width, width), f32),
            pltpu.VMEM((own, traits, width), f32),
            pltpu.VMEM((2, traits, width), f32),
            pltpu.VMEM((width // PANEL, own, PANEL, PANEL), f32),
        ],
    )


def predict(coef, mean, x, folds, o_ref):
    parts, _, group, _ = o_ref.shape
    traits = parts * group
    per_fold = SHRINK * traits
    coef = coef[: FOLDS * per_fold]
    raw = lax.dot_general(
        coef, x, (((1,), (1,)), ((), ())), preferred_element_type=jnp.float32
    )
    shift = jnp.sum(coef.astype(jnp.float32) * mean, axis=1, keepdims=True)
    raw = raw - shift
    out = jnp.zeros((per_fold, raw.shape[1]), jnp.float32)
    for k in range(FOLDS):
        out = jnp.where(folds == k, raw[k * per_fold : (k + 1) * per_fold], out)
    for g in range(parts):
        for l in range(SHRINK):
            o_ref[g, l] = out[l * traits + g * group : l * traits + (g + 1) * group]


def level_kernel(
    depth, blk, coef_ref, mean_ref, x_ref, traits_ref, folds_ref,
    p_ref, f_ref, sum_ref,
    coefs, sent, part, arrived,
    send_line, send_pair, recv, send_blk, recv_blk, send_sum, recv_sum,
):
    count = 2 * depth
    me = lax.axis_index("samp")
    here = lax.axis_index("blk")
    z, x = me // 2, lax.rem(me, 2)
    partner = z * 2 + 1 - x
    barrier = pltpu.get_barrier_semaphore()
    for axis, size, at in (("samp", count, me), ("blk", blk, here)):
        for step in range(1, size):
            pl.semaphore_signal(
                barrier,
                inc=1,
                device_id={axis: lax.rem(at + step, size)},
                device_id_type=MESH,
            )
    coefs[me] = coef_ref[...]
    pl.semaphore_wait(barrier, count + blk - 2)

    def coef_copy(slot, sem, target):
        return pltpu.make_async_remote_copy(
            src_ref=coefs.at[slot],
            dst_ref=coefs.at[slot],
            send_sem=sem,
            recv_sem=recv.at[slot],
            device_id={"samp": target},
            device_id_type=MESH,
        )

    mate = lambda step: lax.rem(z + step, depth) * 2 + x
    for step in range(1, depth):
        coef_copy(me, send_line.at[step], mate(step)).start()
    coef_copy(me, send_pair.at[0], partner).start()
    for step in range(1, depth):
        coef_copy(mate(step), send_pair.at[0], partner).wait_recv()
        coef_copy(mate(step), send_pair.at[step], partner).start()
    for step in range(depth):
        slot = lax.rem(z + step, depth) * 2 + 1 - x
        coef_copy(slot, send_pair.at[0], partner).wait_recv()
    predict(
        coefs[...].reshape(-1, coefs.shape[2]),
        mean_ref[:1],
        x_ref[...],
        folds_ref[...],
        sent,
    )

    def pred_copy(step, slot):
        other = lax.rem(here + step, blk)
        return pltpu.make_async_remote_copy(
            src_ref=sent.at[other],
            dst_ref=p_ref.at[slot],
            send_sem=send_blk.at[step],
            recv_sem=recv_blk.at[slot],
            device_id={"blk": other},
            device_id_type=MESH,
        )

    for step in range(1, blk):
        pred_copy(step, here).start()
    p_ref[here] = sent[here]
    for step in range(1, depth):
        coef_copy(me, send_line.at[step], partner).wait_send()
    for step in range(depth):
        coef_copy(me, send_pair.at[step], partner).wait_send()
    for step in range(1, blk):
        pred_copy(step, lax.rem(here + step, blk)).wait()
    moments(here * p_ref.shape[2], p_ref, traits_ref, folds_ref, f_ref, part.at[0])
    stages = part.shape[0]
    copies = []
    for stage in range(stages):
        bit = 2**stage
        other = me + bit - 2 * bit * lax.rem(me // bit, 2)
        copy = pltpu.make_async_remote_copy(
            src_ref=part.at[stage],
            dst_ref=arrived.at[stage],
            send_sem=send_sum.at[stage],
            recv_sem=recv_sum.at[stage],
            device_id={"samp": other},
            device_id_type=MESH,
        )
        copy.start()
        copies.append(copy)
        copy.wait_recv()
        summed = part[stage] + arrived[stage]
        if stage + 1 < stages:
            part[stage + 1] = summed
        else:
            sum_ref[...] = summed
    for copy in copies:
        copy.wait_send()


def moments(first, p_ref, traits_ref, folds_ref, f_ref, e_ref):
    blocks, shrinks, group, rows = p_ref.shape
    preds = blocks * shrinks
    f_ref[...] = jnp.zeros_like(f_ref)
    traits = traits_ref[...].astype(jnp.float32)
    trait_id = lax.broadcasted_iota(jnp.int32, traits.shape, 0) - first
    for t in range(group):
        base = t * ROWS1
        for b in range(blocks):
            for l in range(shrinks):
                at = base + b * shrinks + l
                f_ref[at : at + 1] = p_ref[b, l, t : t + 1]
        f_ref[base + preds : base + preds + 1] = jnp.sum(
            jnp.where(trait_id == t, traits, 0.0), axis=0, keepdims=True
        )
        f_ref[base + preds + 1 : base + preds + 2] = jnp.ones((1, rows), jnp.float32)
    f = f_ref[...]
    size = group * ROWS1
    folds = folds_ref[...]
    lane = lax.broadcasted_iota(jnp.int32, (ROWS1, size), 1)
    for k in range(FOLDS):
        full = high_dot(jnp.where(folds == k, f, 0.0), f, ((1,), (1,)))
        packed = jnp.zeros((ROWS1, size), jnp.float32)
        for t in range(group):
            inside = (lane >= t * ROWS1) & (lane < (t + 1) * ROWS1)
            packed = jnp.where(inside, full[t * ROWS1 : (t + 1) * ROWS1], packed)
        e_ref[k * ROWS1 : (k + 1) * ROWS1] = packed


def blend_kernel(total, e_ref, f_ref, p_ref, folds_ref, level_ref, blend_ref, mats):
    blocks, shrinks, group, rows = p_ref.shape
    preds = blocks * shrinks
    summed = e_ref[...]
    shape = (ROWS1, ROWS1)
    row = lax.broadcasted_iota(jnp.int32, shape, 0)
    col = lax.broadcasted_iota(jnp.int32, shape, 1)
    col_in = lax.broadcasted_iota(jnp.int32, (ROWS1, 1), 0) < preds
    row_in = lax.broadcasted_iota(jnp.int32, (1, ROWS1), 1) < preds
    one_lane = lax.broadcasted_iota(jnp.int32, (1, ROWS1), 1) == preds + 1
    ridge = jnp.where((row == col) & (row < preds), total / 4.0, 0.0)
    own = [
        [
            summed[k * ROWS1 : (k + 1) * ROWS1, t * ROWS1 : (t + 1) * ROWS1]
            for k in range(FOLDS)
        ]
        for t in range(group)
    ]
    means, scales = [], []
    for t in range(group):
        full = own[t][0]
        for k in range(1, FOLDS):
            full = full + own[t][k]
        mean_row = jnp.where(row_in, full[preds + 1 : preds + 2] / total, 0.0)
        mean_col = jnp.where(col_in, full[:, preds + 1 : preds + 2] / total, 0.0)
        square = jnp.where(row == col, full, 0.0) / total
        sq_row = jnp.sum(square, axis=0, keepdims=True)
        sq_col = jnp.sum(square, axis=1, keepdims=True)
        scale_row = jnp.where(row_in, lax.rsqrt(sq_row - mean_row * mean_row + EPS), 1.0)
        scale_col = jnp.where(col_in, lax.rsqrt(sq_col - mean_col * mean_col + EPS), 1.0)
        means.append((mean_row, mean_col))
        scales.append((scale_row, scale_col))
        for k in range(FOLDS):
            train = full - own[t][k]
            sums_row = train[preds + 1 : preds + 2]
            sums_col = train[:, preds + 1 : preds + 2]
            kept = train[preds + 1 : preds + 2, preds + 1 : preds + 2]
            centered = (
                train - mean_col * sums_row - sums_col * mean_row + kept * (mean_col * mean_row)
            )
            mats[t * FOLDS + k] = scale_col * scale_row * centered + ridge
    for b in range(blocks):
        for l in range(shrinks):
            at = b * shrinks + l
            means_at = jnp.concatenate([means[t][1][at : at + 1] for t in range(group)], axis=0)
            scales_at = jnp.concatenate([scales[t][1][at : at + 1] for t in range(group)], axis=0)
            level_ref[b, l] = (p_ref[b, l] - means_at) * scales_at

    for start in range(0, preds, 8):
        sweep_panel(mats, group * FOLDS, start, min(8, preds - start))
    folds = folds_ref[...]
    for t in range(group):
        mean_row, scale_row = means[t][0], scales[t][0]
        lines = []
        first = jnp.zeros((1, 1), jnp.float32)
        second = jnp.zeros((1, 1), jnp.float32)
        for k in range(FOLDS):
            line = jnp.where(row_in, mats[t * FOLDS + k, preds : preds + 1, :] * scale_row, 0.0)
            offset = jnp.sum(line * mean_row, axis=1, keepdims=True)
            line = jnp.where(one_lane, -offset, line)
            lines.append(line)
            product = jnp.sum(own[t][k] * line, axis=1, keepdims=True)
            line_col = jnp.sum(jnp.where(row == col, line, 0.0), axis=1, keepdims=True)
            first = first + product[preds + 1 : preds + 2]
            second = second + jnp.sum(product * line_col, axis=0, keepdims=True)
        lines.append(jnp.zeros((8 - FOLDS, ROWS1), jnp.float32))
        every = high_dot(
            jnp.concatenate(lines, axis=0),
            f_ref[t * ROWS1 : (t + 1) * ROWS1],
            ((1,), (0,)),
        )
        p = jnp.zeros((1, rows), jnp.float32)
        for k in range(FOLDS):
            p = jnp.where(folds == k, every[k : k + 1], p)
        mean = first / total
        spread_of = second / total - mean * mean
        blend_ref[t : t + 1] = (p - mean) * lax.rsqrt(spread_of + EPS)


def plain(kernel, out_shape, name, *args, scratch=()):
    return pl.pallas_call(
        kernel,
        out_shape=out_shape,
        in_specs=[VMEM] * len(args),
        out_specs=jax.tree.map(lambda _: VMEM, out_shape),
        scratch_shapes=list(scratch),
        compiler_params=pltpu.CompilerParams(vmem_limit_bytes=LIMIT),
        name=name,
    )(*args)


def fast(samp, blk, dosages, traits, folds):
    rows, width = dosages.shape
    count_traits = traits.shape[0]
    group = count_traits // blk
    f32 = jnp.float32
    folds_row = folds[None, :]
    sums = gather_grams(dosages, traits, folds_row, samp)
    coef, mean = solve_level0(sums, count_traits, samp, rows)
    shape = jax.ShapeDtypeStruct((blk, SHRINK, group, rows), f32)
    size = group * ROWS1
    own = owned_systems(samp) * count_traits
    depth = samp // 2
    stages = samp.bit_length() - 1
    dma = pltpu.SemaphoreType.DMA
    pred, stacked, moment_sums = pl.pallas_call(
        functools.partial(level_kernel, depth, blk),
        out_shape=(
            shape,
            jax.ShapeDtypeStruct((size, rows), f32),
            jax.ShapeDtypeStruct((FOLDS * ROWS1, size), f32),
        ),
        in_specs=[VMEM] * 5,
        out_specs=(VMEM,) * 3,
        scratch_shapes=[
            pltpu.VMEM((samp, own, width), jnp.bfloat16),
            pltpu.VMEM(shape.shape, f32),
            pltpu.VMEM((stages, FOLDS * ROWS1, size), f32),
            pltpu.VMEM((stages, FOLDS * ROWS1, size), f32),
            dma((depth,)),
            dma((depth,)),
            dma((samp,)),
            dma((blk,)),
            dma((blk,)),
            dma((stages,)),
            dma((stages,)),
        ],
        compiler_params=pltpu.CompilerParams(
            collective_id=1, has_side_effects=True, vmem_limit_bytes=LIMIT
        ),
        name="predict_level0",
    )(coef, mean, dosages, traits, folds_row)
    level0, blend = plain(
        functools.partial(blend_kernel, float(samp * rows)),
        (shape, jax.ShapeDtypeStruct((group, rows), f32)),
        "blend",
        moment_sums,
        stacked,
        pred,
        folds_row,
        scratch=[pltpu.VMEM((group * FOLDS, ROWS1, ROWS1), f32)],
    )
    return level0, blend


def solution(mesh):
    in_specs = (P("samp", "blk"), P(None, "samp"), P("samp"))
    out_specs = (P(None, None, "blk", "samp"), P("blk", "samp"))
    samp, blk = mesh.shape["samp"], mesh.shape["blk"]
    body = functools.partial(fast, samp, blk) if samp == 8 else shards
    return jax.shard_map(body, mesh=mesh, in_specs=in_specs, out_specs=out_specs, check_vma=False)
```
